128 devices in a mesh: visit: 32 (over y, x, core), band: 4 (over z).
Axes of the slice: x: 4, y: 4, z: 4, core: 2. Of those that a mesh axis runs over, the one named last changes fastest.
Arguments:
- exposures: float32 [4, 64, 552, 552], P('band', 'visit'), may hold values from -8 to 8
- variance: float32 [4, 64, 16, 16], P('band', 'visit'), may hold values from 0.3 to 3
- mask_planes: int32 [4, 64, 16, 16], P('band', 'visit'), may hold values from 0 to 4095
- kernel_table: float32 [64, 27], replicated, may hold values from -3 to 3
- kernel_index: int32 [4, 64], P('band', 'visit'), may hold values from 0 to 63
- tile_owner: int32 [4, 1024, 1], P('band', 'visit'), may hold values from 0 to 31; in each aligned block of 32 rows (0 to 31, 32 to 63, ..., all dimensions but the last counted through in order) at most 2 rows name the same one
- tile_slot: int32 [4, 1024], P('band', 'visit'), may hold values from 0 to 7
Outputs:
- coadd_image: float32 [4, 256, 128, 128], P('band', 'visit')
- detection: float32 [256, 128, 128], P('visit')
The draws below stay inside these ranges and needn't reach their ends.
Inputs may be any that keep to these rules, and one draw needn't show every extreme that they name: `tile_owner`: in each aligned block of 32 items of one band (the items of one device), no owner is named more than 2 times.
All inputs are finite; a program needn't handle non-finite values.
Results may differ from the reference program's by a relative error of at most 0.0003.
Values sent between devices are 32-bit elements; how exact they have to be, the bound alone decides.
No kernel may reach another device: no remote copies, remote signals or barrier semaphores. Data moves between devices by JAX's collectives and lax.ppermute only.
A program may use at most 128 MiB of HBM per device.

```python
import math
import jax
import jax.numpy as jnp
import numpy as np
from jax import lax

BLOCK = 512
TILE = 128
CELL = 32
KSIZE = 41
NBASIS = 27
NPLANES = 12
NTAB = 64
BLK_DEV = 2
OWN_DEV = 8
CAP = 2
NBAND = 4
BLOCKS = 64
PADDED = 552
TILES_BLK = 16
ITEMS = 1024
OUT_TILES = 256
N_VISIT = 32


def place_ends(array, key, low, largest):
    longest = array.shape.index(max(array.shape))
    spots = []
    for shift in (0, 1):
        where = [jax.random.randint(jax.random.fold_in(key, axis), (), 0, length) for axis, length in enumerate(array.shape)]
        where[longest] = (where[longest] + shift) % array.shape[longest]
        spots.append(tuple(where))
    return array.at[spots[0]].set(low).at[spots[1]].set(largest)


def shard_levels(key, shape, shards, least, top_value):
    factor_of = 1.0
    for axis_at, shards_of in shards:
        heights = jax.random.uniform(jax.random.fold_in(jax.random.fold_in(key, 6), axis_at), (shards_of,), jnp.float32, least / len(shards), top_value / len(shards))
        factor_of = factor_of * jnp.repeat(jnp.exp(heights), shape[axis_at] // shards_of).reshape((-1,) + (1,) * (len(shape) - 1 - axis_at))
    return factor_of


def routed_block(rng, own, number, rows, number_of, top, most, skew):
    sequence = jax.random.permutation(rng, number_of)
    packed, common = portions_of(number_of, rows * top, most, skew, True), portions_of(number_of, rows * top, most, skew, False)
    places = jnp.arange(number_of)

    def named(tallies, rotation):
        used = int((tallies > 0).sum())
        fixed = max(1, used // 4)
        shifted = fixed + (places - fixed + rotation * (used - fixed)) % max(1, number_of - fixed)
        return jnp.zeros((number_of,), jnp.int32).at[sequence[jnp.where(places < fixed, places, shifted)]].set(jnp.asarray(tallies, jnp.int32))

    tallies = jnp.where(number % 4 == 0, named(packed, number // 4), named(common, number - number // 4 - 1))
    mixed = jax.random.permutation(jax.random.fold_in(own, 3), number_of)
    giver, sink = mixed[0:number_of // 2 * 2:2], mixed[1:number_of // 2 * 2:2]
    margin = jnp.minimum(tallies[giver] - 1, most - tallies[sink]) // 2
    margin = jnp.where((giver == sequence[0]) | (sink == sequence[0]) | (tallies[sink] == 0), 0, jnp.maximum(margin, 0))
    shifted = jax.random.randint(jax.random.fold_in(own, 4), (number_of // 2,), 0, 1 << 20) % (margin + 1)
    tallies = tallies.at[giver].add(-shifted).at[sink].add(shifted)
    items = jnp.searchsorted(jnp.cumsum(tallies), jnp.arange(rows * top), side="right").astype(jnp.int32)
    table = items.reshape(top, rows).T
    table = table[jax.random.permutation(jax.random.fold_in(own, 1), rows)]
    rotation = jax.random.randint(jax.random.fold_in(own, 2), (rows, 1), 0, top)
    return jnp.take_along_axis(table, (jnp.arange(top)[None, :] + rotation) % top, axis=1)


def portions_of(number_of, total, limit, lean, full):
    portions = [(1 << 20) // math.isqrt(rank ** lean) + 1 for rank in range(1, number_of + 1)]
    largest = limit if full else min(limit, max(-(-total // number_of), total * portions[0] // sum(portions)))
    least = 1 if total - largest >= number_of - 1 else 0
    given, surplus = [largest] + [least] * (number_of - 1), total - largest - least * (number_of - 1)
    while surplus > 0:
        free = [i for i in range(1, number_of) if given[i] < largest] or [i for i in range(1, number_of) if given[i] < limit]
        mass, remaining = sum([portions[i] for i in free]), surplus
        for i in free:
            more = min(limit - given[i], max(1, remaining * portions[i] // mass), surplus)
            given[i] = given[i] + more
            surplus = surplus - more
    return np.array(given)


def noise(rng, dims, scale, reach, cuts=(), held_as=jnp.bfloat16):
    drawn = scale * jax.random.normal(rng, dims, jnp.float32)
    if cuts:
        drawn = drawn * shard_levels(rng, dims, cuts, -0.22, 0.18)
    return jnp.clip(drawn, -reach, reach).astype(held_as)


def setup_inputs(seed: int = 0) -> dict:
    splits = jax.random.split(jax.random.key(seed), 8)
    exposures = noise(splits[0], (NBAND, BLOCKS, PADDED, PADDED), 1.0, 8.0, ((0, 4), (1, 32)), jnp.float32)
    variance = jnp.clip(jnp.exp(math.log(3.0) - 2.3025851 * jax.random.uniform(splits[1], (NBAND, BLOCKS, BLOCK // CELL, BLOCK // CELL), jnp.float32) ** shard_levels(splits[1], (NBAND, BLOCKS, BLOCK // CELL, BLOCK // CELL), ((0, 4), (1, 32)), -0.2, 0.2)), 0.3, 3.0)
    mask_planes = place_ends(jax.random.randint(splits[2], (NBAND, BLOCKS, BLOCK // CELL, BLOCK // CELL), 0, 2 ** NPLANES), jax.random.fold_in(splits[2], 1), 0, (2 ** NPLANES) - 1).astype(jnp.int32)
    kernel_table = noise(splits[3], (NTAB, NBASIS), 0.5, 3.0, (), jnp.float32)
    kernel_index = place_ends(jax.random.randint(splits[4], (NBAND, BLOCKS), 0, NTAB), jax.random.fold_in(splits[4], 1), 0, NTAB - 1).astype(jnp.int32)
    tile_owner_keys = jax.random.split(jax.random.fold_in(splits[5], 1), NBAND * ITEMS // (TILES_BLK * BLK_DEV))
    tile_owner_turns = jax.random.permutation(jax.random.fold_in(splits[5], 3), NBAND * ITEMS // (TILES_BLK * BLK_DEV))
    tile_owner = jax.vmap(lambda own, number: routed_block(jax.random.fold_in(splits[5], 2), own, number, TILES_BLK * BLK_DEV, N_VISIT, 1, CAP, 2))(tile_owner_keys, tile_owner_turns).reshape((NBAND, ITEMS, 1))
    tile_slot = place_ends(jax.random.randint(splits[6], (NBAND, ITEMS), 0, OWN_DEV), jax.random.fold_in(splits[6], 1), 0, OWN_DEV - 1).astype(jnp.int32)
    return dict(exposures=exposures, variance=variance, mask_planes=mask_planes, kernel_table=kernel_table, kernel_index=kernel_index, tile_owner=tile_owner, tile_slot=tile_slot)


width_fractions = (0.075, 0.15, 0.3)
family_degrees = (4, 2, 2)
prior_weight = 0.05
reject_planes = 3

def filter_bank(taps):
    half_width = (taps - 1) // 2
    offsets = jnp.arange(taps, dtype=jnp.float32) - half_width
    profiles = []
    for family in range(3):
        gauss_width = width_fractions[family] * half_width
        for degree in range(family_degrees[family] + 1):
            scaled = offsets / gauss_width
            profile = scaled ** degree * jnp.exp(-0.5 * scaled * scaled)
            profiles.append(profile / jnp.sqrt(jnp.sum(profile * profile)))
    return jnp.stack(profiles)

def basis_pattern():
    starts = (0, 5, 8)
    planes = []
    for family in range(3):
        for first in range(family_degrees[family] + 1):
            for second in range(family_degrees[family] + 1 - first):
                plane = np.zeros((11, 11), np.float32)
                plane[starts[family] + first, starts[family] + second] = 1.0
                planes.append(plane)
    return np.stack(planes)

def toeplitz(bank, outputs, inputs):
    filters_count, taps = bank.shape
    padded = jnp.concatenate([bank, jnp.zeros((filters_count, inputs + 1 - taps), jnp.float32)], axis=1)
    tiled = jnp.tile(padded, (1, outputs))[:, :outputs * inputs]
    return tiled.reshape(filters_count, outputs, inputs)

def weigh_block(pixels, cell_var, cell_bits, mixing, across, down):
    strips = BLOCK // TILE
    highest = lax.Precision.HIGHEST

    def one_strip(strip_index):
        start = (strip_index * TILE).astype(jnp.int32)
        strip = lax.dynamic_slice_in_dim(pixels, start, TILE + KSIZE - 1, 0)
        spread = jnp.einsum('yj,gxj->ygx', strip, across, precision=highest)
        combined = jnp.einsum('gh,yhx->gyx', mixing, spread, precision=highest)
        return jnp.einsum('gay,gyx->ax', down, combined, precision=highest)
    matched = lax.map(one_strip, jnp.arange(strips, dtype=jnp.int32))
    usable = (jnp.bitwise_and(cell_bits, reject_planes) != reject_planes).astype(jnp.float32)
    weight = usable / cell_var
    cells = BLOCK // CELL
    per_tile = TILE // CELL
    pixel_weight = jnp.broadcast_to(weight[:, None, :, None], (cells, CELL, cells, CELL)).reshape(strips, TILE, BLOCK)
    product = matched * pixel_weight
    tile_values = product.reshape(strips, TILE, strips, TILE).transpose(0, 2, 1, 3).reshape(strips * strips, TILE * TILE)
    tile_cells = weight.reshape(strips, per_tile, strips, per_tile).transpose(0, 2, 1, 3).reshape(strips * strips, per_tile * per_tile)
    return (tile_values, tile_cells)

def finish(total, weight_sum):
    tiles_count = total.shape[0]
    per_tile = TILE // CELL
    spread_weight = jnp.broadcast_to(weight_sum.reshape(tiles_count, per_tile, 1, per_tile, 1), (tiles_count, per_tile, CELL, per_tile, CELL)).reshape(tiles_count, TILE, TILE) + prior_weight
    image = total.reshape(tiles_count, TILE, TILE) / spread_weight
    return (image, image * image * spread_weight)

def reference(exposures, variance, mask_planes, kernel_table, kernel_index, tile_owner, tile_slot):
    bank = filter_bank(KSIZE)
    across = toeplitz(bank, BLOCK, BLOCK + KSIZE - 1)
    down = toeplitz(bank, TILE, TILE + KSIZE - 1)
    pattern = jnp.asarray(basis_pattern()).astype(jnp.float32)
    chosen = kernel_table[kernel_index.reshape(-1)]
    mixings = jnp.einsum('bk,kgh->bgh', chosen, pattern, precision=lax.Precision.HIGHEST)
    cells = BLOCK // CELL

    def per_block(inputs):
        pixels, cell_var, cell_bits, mixing = inputs
        return weigh_block(pixels, cell_var, cell_bits, mixing, across, down)
    tile_values, tile_cells = lax.map(per_block, (exposures.reshape(-1, PADDED, PADDED), variance.reshape(-1, cells, cells), mask_planes.reshape(-1, cells, cells), mixings))
    tile_values = tile_values.reshape(NBAND, ITEMS, TILE * TILE)
    tile_cells = tile_cells.reshape(NBAND, ITEMS, -1)
    target = (tile_owner[:, :, 0] * OWN_DEV + tile_slot).astype(jnp.int32)
    images = []
    detection = jnp.zeros((OUT_TILES, TILE, TILE), jnp.float32)
    for band_index in range(NBAND):
        total = jax.ops.segment_sum(tile_values[band_index], target[band_index], num_segments=OUT_TILES)
        weight_sum = jax.ops.segment_sum(tile_cells[band_index], target[band_index], num_segments=OUT_TILES)
        image, chi_terms = finish(total, weight_sum)
        images.append(image)
        detection = detection + chi_terms
    return (jnp.stack(images), detection)
```

```python
import functools

import jax
import jax.numpy as jnp
import numpy as np
from jax import lax
from jax.experimental import pallas as pl
from jax.experimental.pallas import tpu as pltpu
from jax.sharding import PartitionSpec as P

BLOCK = 512
TILE = 128
CELL = 32
KSIZE = 41
OWN_DEV = 8
PADDED = BLOCK + KSIZE - 1
WIDE = 640
NFILT = 11
VISITS = 32
SIDE = BLOCK // TILE
CELLS = BLOCK // CELL
PER_TILE = TILE // CELL
TILES_BLK = SIDE * SIDE
CHIPS = VISITS // 2
PIECE = TILE // CHIPS
INFO = 8
SPAN = TILE + KSIZE - 1
HALF = SPAN // 2
TALL = 560

width_fractions = (0.075, 0.15, 0.3)
family_degrees = (4, 2, 2)
prior_weight = 0.05
reject_planes = 3

f32 = jnp.float32
bf16 = jnp.bfloat16


def as_halves(matrix):
    high = matrix.astype(np.float32).astype(bf16)
    low = (matrix - high.astype(np.float64)).astype(np.float32).astype(bf16)
    return high, low


def transforms():
    number = np.arange(HALF)
    angle = 2 * np.pi * (number + 0.5) / SPAN
    taps = np.arange(SPAN)
    cosine, sine = np.cos(angle[:, None] * taps), np.sin(angle[:, None] * taps)
    spot = 8 * (number // 4) + number % 4

    by_row = np.zeros((SPAN, SPAN))
    by_row[spot], by_row[spot + 4] = cosine, sine
    by_lane = np.zeros((2 * TILE, SPAN))
    by_lane[:HALF], by_lane[TILE:TILE + HALF] = cosine, sine

    across = np.zeros((2 * TILE, 2 * TILE))
    across[:SPAN] = by_lane.T
    down = np.zeros((SPAN + 8, SPAN))
    down[:SPAN] = by_row
    back_down = by_row.T[:TILE] * (2 / SPAN)
    back_across = by_lane[:, :TILE] * (2 / SPAN)

    def three(matrix):
        high, low = as_halves(matrix)
        rest = np.zeros((matrix.shape[0], 512 - 3 * SPAN), bf16)
        return np.concatenate([high, high, low, rest], axis=1)

    same = np.zeros((SPAN, TILE), np.float32)
    cross = np.zeros((SPAN, TILE), np.float32)
    same[spot, :KSIZE] = same[spot + 4, :KSIZE] = cosine[:, :KSIZE]
    cross[spot, :KSIZE], cross[spot + 4, :KSIZE] = sine[:, :KSIZE], -sine[:, :KSIZE]
    along = np.zeros((TILE, 2 * TILE), np.float32)
    along[:KSIZE, :HALF], along[:KSIZE, TILE:TILE + HALF] = cosine[:, :KSIZE].T, -sine[:, :KSIZE].T
    return (
        np.stack(as_halves(across)),
        three(down),
        three(back_down),
        np.concatenate(as_halves(back_across), axis=1),
        np.stack([same, cross]),
        along,
    )


def filter_terms():
    starts = (0, 5, 8)
    terms = []
    for family in range(3):
        for first in range(family_degrees[family] + 1):
            for second in range(family_degrees[family] + 1 - first):
                terms.append((starts[family] + first, starts[family] + second))
    return terms


def profiles_at(offset):
    half_width = (KSIZE - 1) // 2
    inside = (offset >= 0) & (offset < KSIZE)
    taps = offset.astype(f32) - half_width
    values = []
    for family in range(3):
        scaled = taps / (width_fractions[family] * half_width)
        value = jnp.where(inside, jnp.exp(-0.5 * scaled * scaled), 0.0)
        for degree in range(family_degrees[family] + 1):
            values.append(value)
            value = value * scaled
    return values


def split(value):
    high = value.astype(bf16)
    return high, (value - high.astype(f32)).astype(bf16)


def cell_weights(variance, bits):
    usable = (jnp.bitwise_and(bits, reject_planes) != reject_planes).astype(f32)
    return usable / variance


def item_info(var_ref, bits_ref, owner_ref, slot_ref):
    exact = lax.Precision.HIGHEST
    lane = lax.broadcasted_iota(jnp.int32, (1, TILE), 1)
    row = lax.broadcasted_iota(jnp.int32, (CELLS, TILE), 0)
    item = lane % TILES_BLK
    cell_row = (item // SIDE) * PER_TILE + lane // (2 * TILES_BLK)
    columns = None
    for block in range(2):
        picked = ((row == cell_row) & ((lane // TILES_BLK) % 2 == block)).astype(f32)
        term = lax.dot_general(
            cell_weights(var_ref[block], bits_ref[block]), picked,
            (((0,), (0,)), ((), ())), precision=exact, preferred_element_type=f32,
        )
        columns = term if columns is None else columns + term
    rows = []
    for n in range(PER_TILE):
        chosen = row == (item % SIDE) * PER_TILE + n
        rows.append(jnp.sum(jnp.where(chosen, columns, 0.0), axis=0, keepdims=True))
    target = (owner_ref[...] * OWN_DEV + slot_ref[...]).astype(f32)
    rows.append(jnp.concatenate([target, jnp.zeros((1, TILE - 2 * TILES_BLK), f32)], axis=1))
    rows.append(jnp.zeros((INFO - PER_TILE - 1, TILE), f32))
    return jnp.concatenate(rows, axis=0)


def exact_dot(left, right, sides=((1,), (0,))):
    return lax.dot_general(
        left, right, (sides, ((), ())), precision=lax.Precision.HIGHEST, preferred_element_type=f32
    )


def stacked_halves(value):
    high = value.astype(bf16).astype(f32)
    rest = jnp.zeros((512 - 3 * SPAN, value.shape[1]), f32)
    return jnp.concatenate([high, value - high, high, rest], axis=0).astype(bf16)


def filter_bank():
    taps = lax.broadcasted_iota(jnp.int32, (1, TILE), 1)
    rows = [value / jnp.sqrt(jnp.sum(value * value, axis=1, keepdims=True)) for value in profiles_at(taps)]
    return jnp.concatenate(rows + [jnp.zeros((16 - NFILT, TILE), f32)], axis=0)


def kernel_spectrum(filters, which, table_ref, down_taps_ref, along_ref):
    first = lax.broadcasted_iota(jnp.int32, (16, 16), 0)
    second = lax.broadcasted_iota(jnp.int32, (16, 16), 1)
    mixing = jnp.zeros((16, 16), f32)
    for number, (p, q) in enumerate(filter_terms()):
        mixing = jnp.where((first == p) & (second == q), table_ref[number, which], mixing)
    across = exact_dot(mixing, exact_dot(filters, along_ref[...]))
    return [
        exact_dot(exact_dot(down_taps_ref[part], filters, ((1,), (1,))), across)
        for part in range(2)
    ]


def match_kernel(
    index_hbm, table_hbm, image_hbm, var_hbm, bits_hbm, owner_hbm, slot_hbm,
    across_hbm, down_hbm, back_down_hbm, back_across_hbm, down_taps_hbm, along_hbm, out_hbm,
    index_ref, table_ref, image_ref, var_ref, bits_ref, owner_ref, slot_ref,
    across_ref, down_ref, back_down_ref, back_across_ref, down_taps_ref, along_ref, sems, out_sems,
    tail_ref, high_ref, low_ref, wave_ref, stack_ref, turn_ref, result_ref, rows_ref, factor_ref,
    weight_ref, out_ref,
    *, block,
):
    copies = [
        pltpu.make_async_copy(source, goal, sems.at[number])
        for number, (source, goal) in enumerate((
            (index_hbm, index_ref),
            (table_hbm, table_ref),
            (down_taps_hbm, down_taps_ref),
            (along_hbm, along_ref),
            (image_hbm.at[0, block], image_ref),
            (across_hbm, across_ref),
            (var_hbm.at[0], var_ref),
            (bits_hbm.at[0], bits_ref),
            (owner_hbm, owner_ref),
            (slot_hbm, slot_ref),
            (down_hbm, down_ref),
            (back_down_hbm, back_down_ref),
            (back_across_hbm, back_across_ref),
        ))
    ]
    for copy in copies:
        copy.start()
    tail_ref[...] = jnp.zeros_like(tail_ref)
    filters = filter_bank()
    for copy in copies:
        copy.wait()

    tail_ref[:PADDED, :PADDED - BLOCK] = image_ref[:, BLOCK:]
    whole = TALL - 16
    for columns, source in ((slice(0, BLOCK), image_ref), (slice(BLOCK, WIDE), tail_ref)):
        width = columns.stop - columns.start
        high_ref[:whole, columns], low_ref[:whole, columns] = split(source[:whole, :width])
        last = jnp.concatenate([source[whole:PADDED, :width], jnp.zeros((8, width), f32)], axis=0)
        high_ref[whole:, columns], low_ref[whole:, columns] = split(last)

    forward = jnp.concatenate([across_ref[0], across_ref[0], across_ref[1]], axis=0)
    backward = jnp.concatenate([back_across_ref[...], back_across_ref[...]], axis=0)
    pair = 2 * TILE
    for column in range(SIDE):
        lanes = slice(column * TILE, column * TILE + pair)
        high, low = high_ref[:, lanes], low_ref[:, lanes]
        wave_ref[:, column * pair:(column + 1) * pair] = jnp.dot(
            jnp.concatenate([high, low, high], axis=1), forward, preferred_element_type=f32
        )

    same, cross = kernel_spectrum(filters, index_ref[0, block], table_ref, down_taps_ref, along_ref)
    factor_ref[0] = same.reshape(SPAN // 8, 8, pair)
    factor_ref[1] = cross.reshape(SPAN // 8, 8, pair)

    spread = (
        lax.broadcasted_iota(jnp.int32, (CELLS, BLOCK), 1) // CELL
        == lax.broadcasted_iota(jnp.int32, (CELLS, BLOCK), 0)
    ).astype(f32)
    weight_ref[...] = exact_dot(cell_weights(var_ref[block], bits_ref[block]), spread)
    sends = []
    if block == 0:
        info = item_info(var_ref, bits_ref, owner_ref, slot_ref)
        out_ref[:, TILES_BLK] = jnp.broadcast_to(info[None], (CHIPS, INFO, TILE))
        sends.append(
            pltpu.make_async_copy(out_ref.at[:, TILES_BLK], out_hbm.at[:, TILES_BLK], out_sems.at[TILES_BLK])
        )
        sends[-1].start()

    for line in range(SIDE):
        for column in range(SIDE):
            lanes = slice(column * pair, (column + 1) * pair)
            stack_ref[line, :, lanes] = stacked_halves(
                wave_ref[line * TILE:line * TILE + SPAN, lanes]
            )
        turn_ref[line] = jnp.dot(down_ref[...], stack_ref[line], preferred_element_type=f32)

    for line in range(SIDE):
        for column in range(SIDE):
            lanes = slice(column * pair, (column + 1) * pair)
            wave = turn_ref[line, :SPAN, lanes].reshape(SPAN // 8, 8, pair)
            turned = pltpu.roll(wave, 4, 1)
            wave_c, wave_s = wave[..., :TILE], wave[..., TILE:]
            turned_c, turned_s = turned[..., :TILE], turned[..., TILE:]
            same_c, same_s = factor_ref[0, :, :, :TILE], factor_ref[0, :, :, TILE:]
            cross_c, cross_s = factor_ref[1, :, :, :TILE], factor_ref[1, :, :, TILE:]
            result_c = wave_c * same_c + turned_c * cross_c - wave_s * same_s - turned_s * cross_s
            result_s = wave_s * same_c + turned_s * cross_c + wave_c * same_s + turned_c * cross_s
            result = jnp.concatenate(
                [result_c.reshape(SPAN, TILE), result_s.reshape(SPAN, TILE)], axis=1
            )
            result_ref[line, :, lanes] = stacked_halves(result)
        rows = jnp.dot(back_down_ref[...], result_ref[line], preferred_element_type=f32)
        for column in range(SIDE):
            high, low = split(rows[:, column * pair:(column + 1) * pair])
            rows_ref[column, line * TILE:(line + 1) * TILE, :pair] = high
            rows_ref[column, line * TILE:(line + 1) * TILE, pair:] = low

    for column in range(SIDE):
        matched = jnp.dot(rows_ref[column], backward, preferred_element_type=f32)
        matched = matched[:, :TILE] + matched[:, TILE:]
        weight = weight_ref[:, column * TILE:(column + 1) * TILE]
        weighted = matched.reshape(CELLS, CELL, TILE) * weight[:, None, :]
        weighted = weighted.reshape(SIDE, CHIPS, PIECE, TILE)
        for line in range(SIDE):
            item = line * SIDE + column
            out_ref[:, item] = weighted[line]
            sends.append(
                pltpu.make_async_copy(out_ref.at[:, item], out_hbm.at[:, item], out_sems.at[item])
            )
            sends[-1].start()
    for send in sends:
        send.wait()


def match_block(block, exposures, variance, bits, table, index, owner, slot):
    blocks = exposures.shape[1]
    items = blocks * TILES_BLK
    groups = TILES_BLK + (1 if block == 0 else 0)
    matrices = transforms()
    pieces = pl.pallas_call(
        functools.partial(match_kernel, block=block),
        out_shape=jax.ShapeDtypeStruct((CHIPS, groups, PIECE, TILE), f32),
        in_specs=[pl.BlockSpec(memory_space=pltpu.HBM)] * (7 + len(matrices)),
        out_specs=pl.BlockSpec(memory_space=pltpu.HBM),
        scratch_shapes=[
            pltpu.SMEM((1, blocks), jnp.int32),
            pltpu.SMEM(table.shape, f32),
            pltpu.VMEM((PADDED, PADDED), f32),
            pltpu.VMEM((blocks, CELLS, CELLS), f32),
            pltpu.VMEM((blocks, CELLS, CELLS), jnp.int32),
            pltpu.VMEM((1, items), jnp.int32),
            pltpu.VMEM((1, items), jnp.int32),
            *[pltpu.VMEM(matrix.shape, matrix.dtype) for matrix in matrices],
            pltpu.SemaphoreType.DMA((7 + len(matrices),)),
            pltpu.SemaphoreType.DMA((TILES_BLK + 1,)),
            pltpu.VMEM((TALL, TILE), f32),
            pltpu.VMEM((TALL, WIDE), bf16),
            pltpu.VMEM((TALL, WIDE), bf16),
            pltpu.VMEM((TALL, 2 * BLOCK), f32),
            pltpu.VMEM((SIDE, 512, 2 * BLOCK), bf16),
            pltpu.VMEM((SIDE, SPAN + 8, 2 * BLOCK), f32),
            pltpu.VMEM((SIDE, 512, 2 * BLOCK), bf16),
            pltpu.VMEM((SIDE, BLOCK, 4 * TILE), bf16),
            pltpu.VMEM((2, SPAN // 8, 8, 2 * TILE), f32),
            pltpu.VMEM((CELLS, BLOCK), f32),
            pltpu.VMEM((CHIPS, groups, PIECE, TILE), f32),
        ],
        compiler_params=pltpu.CompilerParams(vmem_limit_bytes=60 << 20),
        cost_estimate=pl.CostEstimate(
            flops=2 * 256 * 256 * 20000, bytes_accessed=3 << 20, transcendentals=0
        ),
        name="match_block",
    )(index, table, exposures, variance, bits, owner, slot, *matrices)
    return pieces.reshape(CHIPS, groups * PIECE, TILE)


def partial_kernel(place_ref, first_ref, second_ref, mine_ref, other_ref):
    core = place_ref[0] % 2
    per_group = TILE // TILES_BLK
    lane = lax.broadcasted_iota(jnp.int32, (INFO, TILE), 1)
    info = [first_ref[source, TILES_BLK * PIECE:, :] for source in range(CHIPS)]
    tables = []
    for block in range(2):
        rows = []
        for m in range(PER_TILE):
            groups = []
            for group in range(CHIPS // per_group):
                total = None
                for member in range(per_group):
                    goal = member * TILES_BLK
                    shift = (goal - (m * 2 + block) * TILES_BLK) % TILE
                    value = info[group * per_group + member]
                    value = pltpu.roll(value, shift, 1) if shift else value
                    here = (lane >= goal) & (lane < goal + TILES_BLK)
                    total = value if total is None else jnp.where(here, value, total)
                groups.append(total)
            rows.append(jnp.concatenate(groups, axis=1))
        tables.append(rows)

    targets = VISITS * OWN_DEV
    owned = targets // 2
    items = CHIPS * TILES_BLK
    row = lax.broadcasted_iota(jnp.int32, (targets, items), 0)
    side = (row // owned + core) % 2
    inner = row % owned
    wanted = ((inner // OWN_DEV) * 2 + side) * OWN_DEV + inner % OWN_DEV
    routes = []
    sums = None
    over_items = (((1,), (1,)), ((), ()))
    for block in range(2):
        target = tables[block][0][PER_TILE:PER_TILE + 1, :].astype(jnp.int32)
        route = jnp.where(wanted == target, 1.0, 0.0).astype(bf16)
        routes.append(route)
        weights = jnp.concatenate(
            tables[block] + [jnp.zeros((TILE - INFO * PER_TILE, items), f32)], axis=0
        )
        for half in split(weights):
            term = lax.dot_general(route, half, over_items, preferred_element_type=f32)
            sums = term if sums is None else sums + term
    mine_ref[owned * PIECE:, :] = sums[:owned]
    other_ref[owned * PIECE:, :] = sums[owned:]
    for line in range(PIECE):
        total = None
        for route, part_ref in zip(routes, (first_ref, second_ref)):
            part = part_ref[:, pl.ds(line, TILES_BLK, PIECE), :].reshape(items, TILE)
            high, low = split(part)
            term = jnp.dot(
                route, jnp.concatenate([high, low], axis=1), preferred_element_type=f32
            )
            total = term if total is None else total + term
        total = total[:, :TILE] + total[:, TILE:]
        mine_ref[pl.ds(line, owned, PIECE), :] = total[:owned]
        other_ref[pl.ds(line, owned, PIECE), :] = total[owned:]


def spread_cells(sums, cell_row):
    pattern = (
        lax.broadcasted_iota(jnp.int32, (TILE, TILE), 1) // CELL + cell_row * INFO
        == lax.broadcasted_iota(jnp.int32, (TILE, TILE), 0)
    ).astype(f32)
    return jnp.dot(sums, pattern, precision=lax.Precision.HIGHEST, preferred_element_type=f32)


def merge_kernel(place_ref, mine_ref, other_ref, out_ref):
    owned = VISITS * OWN_DEV // 2
    cell_row = (place_ref[0] // 2) // (CELL // PIECE)
    sums = mine_ref[owned * PIECE:, :] + other_ref[owned * PIECE:, :]
    scale = 1.0 / (spread_cells(sums, cell_row) + prior_weight)
    total = mine_ref[:owned * PIECE, :] + other_ref[:owned * PIECE, :]
    total = total.reshape(owned, PIECE, TILE) * scale[:, None, :]
    out_ref[...] = total.reshape(owned * PIECE, TILE)


def owner_kernel(place_ref, mine_ref, other_ref, part_ref, image_ref, chi_ref):
    owned = VISITS * OWN_DEV // 2
    rows = pl.ds(pl.multiple_of(owned * PIECE + (place_ref[0] // 2) * OWN_DEV, OWN_DEV), OWN_DEV)
    sums = mine_ref[rows, :] + other_ref[rows, :]
    spread = [spread_cells(sums, cell_row) + prior_weight for cell_row in range(PER_TILE)]
    for slot in range(OWN_DEV):
        image = part_ref[:, slot * PIECE:(slot + 1) * PIECE, :].reshape(TILE, TILE)
        image_ref[slot] = image
        weight = jnp.concatenate(
            [jnp.broadcast_to(spread[m][slot:slot + 1], (CELL, TILE)) for m in range(PER_TILE)],
            axis=0,
        )
        chi_ref[slot] = image * image * weight


def local(exposures, variance, mask_planes, kernel_table, kernel_index, tile_owner, tile_slot):
    place = lax.axis_index("visit").astype(jnp.int32).reshape(1)
    smem = pl.BlockSpec(memory_space=pltpu.SMEM)
    vmem = pl.BlockSpec(memory_space=pltpu.VMEM)
    params = pltpu.CompilerParams(vmem_limit_bytes=32 << 20)
    same_core = [list(range(core, VISITS, 2)) for core in range(2)]
    owned = VISITS * OWN_DEV // 2

    def exchange(pieces):
        return lax.all_to_all(pieces, "visit", 0, 0, axis_index_groups=same_core, tiled=True)

    table = kernel_table.T
    owner = tile_owner.reshape(tile_slot.shape)
    parts = []
    for block in range(exposures.shape[1]):
        pieces = match_block(
            block, exposures, variance, mask_planes, table, kernel_index, owner, tile_slot
        )
        parts.append(exchange(pieces))

    mine, other = pl.pallas_call(
        partial_kernel,
        out_shape=[jax.ShapeDtypeStruct((owned * (PIECE + 1), TILE), f32)] * 2,
        in_specs=[smem, vmem, vmem],
        out_specs=[vmem, vmem],
        compiler_params=params,
        name="partial_sums",
    )(place, *parts)
    other = lax.ppermute(other, "visit", [(device, device ^ 1) for device in range(VISITS)])
    pieces = pl.pallas_call(
        merge_kernel,
        out_shape=jax.ShapeDtypeStruct((owned * PIECE, TILE), f32),
        in_specs=[smem, vmem, vmem],
        out_specs=vmem,
        compiler_params=params,
        name="merge_cores",
    )(place, mine, other)
    pieces = exchange(pieces.reshape(CHIPS, OWN_DEV * PIECE, TILE))
    image, chi = pl.pallas_call(
        owner_kernel,
        out_shape=[jax.ShapeDtypeStruct((OWN_DEV, TILE, TILE), f32)] * 2,
        in_specs=[smem, vmem, vmem, vmem],
        out_specs=[vmem, vmem],
        compiler_params=params,
        name="own",
    )(place, mine, other, pieces)

    pairings = ([(0, 1), (1, 0), (2, 3), (3, 2)], [(0, 3), (3, 0), (1, 2), (2, 1)])
    halves = [chi[:OWN_DEV // 2], chi[OWN_DEV // 2:]]
    for turn in range(2):
        halves = [
            half + lax.ppermute(half, "band", pairings[(turn + number) % 2])
            for number, half in enumerate(halves)
        ]
    return image[None], jnp.concatenate(halves, axis=0)


def solution(mesh):
    placed = (
        P("band", "visit", None, None),
        P("band", "visit", None, None),
        P("band", "visit", None, None),
        P(),
        P("band", "visit"),
        P("band", "visit", None),
        P("band", "visit"),
    )
    return jax.shard_map(
        local,
        mesh=mesh,
        in_specs=placed,
        out_specs=(P("band", "visit", None, None), P("visit", None, None)),
        check_vma=False,
    )
```

```python
import functools

import jax
import jax.numpy as jnp
import numpy as np
from jax import lax
from jax.experimental import pallas as pl
from jax.experimental.pallas import tpu as pltpu
from jax.sharding import PartitionSpec as P

BLOCK = 512
TILE = 128
CELL = 32
KSIZE = 41
OWN_DEV = 8
PADDED = BLOCK + KSIZE - 1
WIDE = 640
NFILT = 11
VISITS = 32
SIDE = BLOCK // TILE
CELLS = BLOCK // CELL
PER_TILE = TILE // CELL
TILES_BLK = SIDE * SIDE
CHIPS = VISITS // 2
PIECE = TILE // CHIPS
INFO = 8
SPAN = TILE + KSIZE - 1
HALF = SPAN // 2
TALL = 560

width_fractions = (0.075, 0.15, 0.3)
family_degrees = (4, 2, 2)
prior_weight = 0.05
reject_planes = 3

f32 = jnp.float32
bf16 = jnp.bfloat16


def as_halves(matrix):
    high = matrix.astype(np.float32).astype(bf16)
    low = (matrix - high.astype(np.float64)).astype(np.float32).astype(bf16)
    return high, low


def transforms():
    number = np.arange(HALF)
    angle = 2 * np.pi * (number + 0.5) / SPAN
    taps = np.arange(SPAN)
    cosine, sine = np.cos(angle[:, None] * taps), np.sin(angle[:, None] * taps)
    spot = 8 * (number // 4) + number % 4

    by_row = np.zeros((SPAN, SPAN))
    by_row[spot], by_row[spot + 4] = cosine, sine
    by_lane = np.zeros((2 * TILE, SPAN))
    by_lane[:HALF], by_lane[TILE:TILE + HALF] = cosine, sine

    across = np.zeros((2 * TILE, 2 * TILE))
    across[:SPAN] = by_lane.T
    down = np.zeros((SPAN + 8, SPAN))
    down[:SPAN] = by_row
    back_down = by_row.T[:TILE] * (2 / SPAN)
    back_across = by_lane[:, :TILE] * (2 / SPAN)

    def three(matrix):
        high, low = as_halves(matrix)
        rest = np.zeros((matrix.shape[0], 512 - 3 * SPAN), bf16)
        return np.concatenate([high, high, low, rest], axis=1)

    same = np.zeros((SPAN, TILE), np.float32)
    cross = np.zeros((SPAN, TILE), np.float32)
    same[spot, :KSIZE] = same[spot + 4, :KSIZE] = cosine[:, :KSIZE]
    cross[spot, :KSIZE], cross[spot + 4, :KSIZE] = sine[:, :KSIZE], -sine[:, :KSIZE]
    along = np.zeros((TILE, 2 * TILE), np.float32)
    along[:KSIZE, :HALF], along[:KSIZE, TILE:TILE + HALF] = cosine[:, :KSIZE].T, -sine[:, :KSIZE].T
    return (
        np.stack(as_halves(across)),
        three(down),
        three(back_down),
        np.concatenate(as_halves(back_across), axis=1),
        np.stack([same, cross]),
        along,
    )


def filter_terms():
    starts = (0, 5, 8)
    terms = []
    for family in range(3):
        for first in range(family_degrees[family] + 1):
            for second in range(family_degrees[family] + 1 - first):
                terms.append((starts[family] + first, starts[family] + second))
    return terms


def profiles_at(offset):
    half_width = (KSIZE - 1) // 2
    inside = (offset >= 0) & (offset < KSIZE)
    taps = offset.astype(f32) - half_width
    values = []
    for family in range(3):
        scaled = taps / (width_fractions[family] * half_width)
        value = jnp.where(inside, jnp.exp(-0.5 * scaled * scaled), 0.0)
        for degree in range(family_degrees[family] + 1):
            values.append(value)
            value = value * scaled
    return values


def split(value):
    high = value.astype(bf16)
    return high, (value - high.astype(f32)).astype(bf16)


def cell_weights(variance, bits):
    usable = (jnp.bitwise_and(bits, reject_planes) != reject_planes).astype(f32)
    return usable / variance


def item_info(var_ref, bits_ref, owner_ref, slot_ref):
    exact = lax.Precision.HIGHEST
    lane = lax.broadcasted_iota(jnp.int32, (1, TILE), 1)
    row = lax.broadcasted_iota(jnp.int32, (CELLS, TILE), 0)
    item = lane % TILES_BLK
    cell_row = (item // SIDE) * PER_TILE + lane // (2 * TILES_BLK)
    columns = None
    for block in range(2):
        picked = ((row == cell_row) & ((lane // TILES_BLK) % 2 == block)).astype(f32)
        term = lax.dot_general(
            cell_weights(var_ref[block], bits_ref[block]), picked,
            (((0,), (0,)), ((), ())), precision=exact, preferred_element_type=f32,
        )
        columns = term if columns is None else columns + term
    rows = []
    for n in range(PER_TILE):
        chosen = row == (item % SIDE) * PER_TILE + n
        rows.append(jnp.sum(jnp.where(chosen, columns, 0.0), axis=0, keepdims=True))
    target = (owner_ref[...] * OWN_DEV + slot_ref[...]).astype(f32)
    rows.append(jnp.concatenate([target, jnp.zeros((1, TILE - 2 * TILES_BLK), f32)], axis=1))
    rows.append(jnp.zeros((INFO - PER_TILE - 1, TILE), f32))
    return jnp.concatenate(rows, axis=0)


def exact_dot(left, right, sides=((1,), (0,))):
    return lax.dot_general(
        left, right, (sides, ((), ())), precision=lax.Precision.HIGHEST, preferred_element_type=f32
    )


def stacked_halves(value):
    high = value.astype(bf16).astype(f32)
    return jnp.concatenate([high, value - high], axis=0).astype(bf16)


def against_halves(matrix, halves_ref):
    rows = jnp.concatenate([halves_ref[...], halves_ref[:SPAN + 8, :]], axis=0)
    return jnp.dot(matrix, rows, preferred_element_type=f32)


def filter_bank():
    taps = lax.broadcasted_iota(jnp.int32, (1, TILE), 1)
    rows = [value / jnp.sqrt(jnp.sum(value * value, axis=1, keepdims=True)) for value in profiles_at(taps)]
    return jnp.concatenate(rows + [jnp.zeros((16 - NFILT, TILE), f32)], axis=0)


def kernel_spectrum(filters, which, table_ref, down_taps_ref, along_ref):
    first = lax.broadcasted_iota(jnp.int32, (16, 16), 0)
    second = lax.broadcasted_iota(jnp.int32, (16, 16), 1)
    mixing = jnp.zeros((16, 16), f32)
    for number, (p, q) in enumerate(filter_terms()):
        mixing = jnp.where((first == p) & (second == q), table_ref[number, which], mixing)
    across = exact_dot(mixing, exact_dot(filters, along_ref[...]))
    return [
        exact_dot(exact_dot(down_taps_ref[part], filters, ((1,), (1,))), across)
        for part in range(2)
    ]


def match_kernel(
    index_hbm, table_hbm, image_hbm, var_hbm, bits_hbm, owner_hbm, slot_hbm,
    across_hbm, down_hbm, back_down_hbm, back_across_hbm, down_taps_hbm, along_hbm, out_hbm,
    index_ref, table_ref, image_ref, var_ref, bits_ref, owner_ref, slot_ref,
    across_ref, down_ref, back_down_ref, back_across_ref, down_taps_ref, along_ref, sems, out_sems,
    tail_ref, high_ref, low_ref, wave_ref, stack_ref, turn_ref, result_ref, rows_ref, factor_ref,
    weight_ref, out_ref,
):
    blocks = range(2)
    copies = [
        pltpu.make_async_copy(source, goal, sems.at[number])
        for number, (source, goal) in enumerate((
            (index_hbm, index_ref),
            (table_hbm, table_ref),
            (down_taps_hbm, down_taps_ref),
            (along_hbm, along_ref),
            (image_hbm.at[0, 0], image_ref.at[0]),
            (across_hbm, across_ref),
            (var_hbm.at[0], var_ref),
            (bits_hbm.at[0], bits_ref),
            (owner_hbm, owner_ref),
            (slot_hbm, slot_ref),
            (image_hbm.at[0, 1], image_ref.at[1]),
            (down_hbm, down_ref),
            (back_down_hbm, back_down_ref),
            (back_across_hbm, back_across_ref),
        ))
    ]
    for copy in copies:
        copy.start()
    tail_ref[...] = jnp.zeros_like(tail_ref)
    filters = filter_bank()
    spread = (
        lax.broadcasted_iota(jnp.int32, (CELLS, BLOCK), 1) // CELL
        == lax.broadcasted_iota(jnp.int32, (CELLS, BLOCK), 0)
    ).astype(f32)
    for copy in copies:
        copy.wait()

    pair = 2 * TILE
    forward = jnp.concatenate([across_ref[0], across_ref[0], across_ref[1]], axis=0)
    backward = jnp.concatenate([back_across_ref[...], back_across_ref[...]], axis=0)
    sends = []

    def send(item):
        sends.append(pltpu.make_async_copy(out_ref.at[:, item], out_hbm.at[:, item], out_sems.at[item]))
        sends[-1].start()

    def halve(block):
        tail_ref[block, :PADDED, :PADDED - BLOCK] = image_ref[block, :, BLOCK:]
        whole = TALL - 16
        for first, width, source in ((0, BLOCK, image_ref), (BLOCK, TILE, tail_ref)):
            lanes = slice(first, first + width)
            high_ref[block, :whole, lanes], low_ref[block, :whole, lanes] = split(
                source[block, :whole, :width]
            )
            last = jnp.concatenate(
                [source[block, whole:PADDED, :width], jnp.zeros((8, width), f32)], axis=0
            )
            high_ref[block, whole:, lanes], low_ref[block, whole:, lanes] = split(last)

    def transform_across(block, column):
        lanes = slice(column * TILE, column * TILE + pair)
        high, low = high_ref[block, :, lanes], low_ref[block, :, lanes]
        wave_ref[block, :, column * pair:(column + 1) * pair] = jnp.dot(
            jnp.concatenate([high, low, high], axis=1), forward, preferred_element_type=f32
        )

    def prepare(block):
        same, cross = kernel_spectrum(
            filters, index_ref[0, block], table_ref, down_taps_ref, along_ref
        )
        factor_ref[block, 0] = same.reshape(SPAN // 8, 8, pair)
        factor_ref[block, 1] = cross.reshape(SPAN // 8, 8, pair)
        weight_ref[block] = exact_dot(cell_weights(var_ref[block], bits_ref[block]), spread)

    def transform_down(block, line):
        for column in range(SIDE):
            lanes = slice(column * pair, (column + 1) * pair)
            stack_ref[block, line, :, lanes] = stacked_halves(
                wave_ref[block, line * TILE:line * TILE + SPAN, lanes]
            )
        turn_ref[block, line] = against_halves(down_ref[...], stack_ref.at[block, line])

    def multiply(block, line):
        for column in range(SIDE):
            lanes = slice(column * pair, (column + 1) * pair)
            wave = turn_ref[block, line, :SPAN, lanes].reshape(SPAN // 8, 8, pair)
            turned = pltpu.roll(wave, 4, 1)
            wave_c, wave_s = wave[..., :TILE], wave[..., TILE:]
            turned_c, turned_s = turned[..., :TILE], turned[..., TILE:]
            same_c, same_s = factor_ref[block, 0, :, :, :TILE], factor_ref[block, 0, :, :, TILE:]
            cross_c, cross_s = factor_ref[block, 1, :, :, :TILE], factor_ref[block, 1, :, :, TILE:]
            result_c = wave_c * same_c + turned_c * cross_c - wave_s * same_s - turned_s * cross_s
            result_s = wave_s * same_c + turned_s * cross_c + wave_c * same_s + turned_c * cross_s
            result = jnp.concatenate(
                [result_c.reshape(SPAN, TILE), result_s.reshape(SPAN, TILE)], axis=1
            )
            result_ref[block, line, :, lanes] = stacked_halves(result)

    def back_down(block, line):
        rows = against_halves(back_down_ref[...], result_ref.at[block, line])
        for column in range(SIDE):
            high, low = split(rows[:, column * pair:(column + 1) * pair])
            rows_ref[block, column, line * TILE:(line + 1) * TILE, :pair] = high
            rows_ref[block, column, line * TILE:(line + 1) * TILE, pair:] = low

    def back_across(block, column):
        matched = jnp.dot(rows_ref[block, column], backward, preferred_element_type=f32)
        matched = matched[:, :TILE] + matched[:, TILE:]
        weight = weight_ref[block, :, column * TILE:(column + 1) * TILE]
        weighted = matched.reshape(CELLS, CELL, TILE) * weight[:, None, :]
        weighted = weighted.reshape(SIDE, CHIPS, PIECE, TILE)
        for line in range(SIDE):
            item = block * TILES_BLK + line * SIDE + column
            out_ref[:, item] = weighted[line]
            send(item)

    halve(0)
    for column in range(SIDE):
        transform_across(0, column)
    halve(1)
    for block in blocks:
        prepare(block)
    info = item_info(var_ref, bits_ref, owner_ref, slot_ref)
    out_ref[:, 2 * TILES_BLK] = jnp.broadcast_to(info[None], (CHIPS, INFO, TILE))
    send(2 * TILES_BLK)
    for line in range(SIDE):
        transform_across(1, line)
        transform_down(0, line)
    for line in range(SIDE):
        transform_down(1, line)
        multiply(0, line)
    for line in range(SIDE):
        back_down(0, line)
        multiply(1, line)
    for line in range(SIDE):
        back_across(0, line)
        back_down(1, line)
    for line in range(SIDE):
        back_across(1, line)
    for copy in sends:
        copy.wait()


def match_blocks(exposures, variance, bits, table, index, owner, slot):
    blocks = exposures.shape[1]
    items = blocks * TILES_BLK
    groups = items + 1
    matrices = transforms()
    pieces = pl.pallas_call(
        match_kernel,
        out_shape=jax.ShapeDtypeStruct((CHIPS, groups, PIECE, TILE), f32),
        in_specs=[pl.BlockSpec(memory_space=pltpu.HBM)] * (7 + len(matrices)),
        out_specs=pl.BlockSpec(memory_space=pltpu.HBM),
        scratch_shapes=[
            pltpu.SMEM((1, blocks), jnp.int32),
            pltpu.SMEM(table.shape, f32),
            pltpu.VMEM((blocks, PADDED, PADDED), f32),
            pltpu.VMEM((blocks, CELLS, CELLS), f32),
            pltpu.VMEM((blocks, CELLS, CELLS), jnp.int32),
            pltpu.VMEM((1, items), jnp.int32),
            pltpu.VMEM((1, items), jnp.int32),
            *[pltpu.VMEM(matrix.shape, matrix.dtype) for matrix in matrices],
            pltpu.SemaphoreType.DMA((8 + len(matrices),)),
            pltpu.SemaphoreType.DMA((groups,)),
            pltpu.VMEM((blocks, TALL, TILE), f32),
            pltpu.VMEM((blocks, TALL, WIDE), bf16),
            pltpu.VMEM((blocks, TALL, WIDE), bf16),
            pltpu.VMEM((blocks, TALL, 2 * BLOCK), f32),
            pltpu.VMEM((blocks, SIDE, 2 * SPAN, 2 * BLOCK), bf16),
            pltpu.VMEM((blocks, SIDE, SPAN + 8, 2 * BLOCK), f32),
            pltpu.VMEM((blocks, SIDE, 2 * SPAN, 2 * BLOCK), bf16),
            pltpu.VMEM((blocks, SIDE, BLOCK, 4 * TILE), bf16),
            pltpu.VMEM((blocks, 2, SPAN // 8, 8, 2 * TILE), f32),
            pltpu.VMEM((blocks, CELLS, BLOCK), f32),
            pltpu.VMEM((CHIPS, groups, PIECE, TILE), f32),
        ],
        compiler_params=pltpu.CompilerParams(vmem_limit_bytes=60 << 20),
        cost_estimate=pl.CostEstimate(
            flops=2 * 256 * 256 * 40000, bytes_accessed=6 << 20, transcendentals=0
        ),
        name="match_blocks",
    )(index, table, exposures, variance, bits, owner, slot, *matrices)
    return pieces.reshape(CHIPS, groups * PIECE, TILE)


def partial_kernel(place_ref, part_ref, mine_ref, other_ref):
    core = place_ref[0] % 2
    per_group = TILE // TILES_BLK
    lane = lax.broadcasted_iota(jnp.int32, (INFO, TILE), 1)
    info = [part_ref[source, 2 * TILES_BLK * PIECE:, :] for source in range(CHIPS)]
    tables = []
    for block in range(2):
        rows = []
        for m in range(PER_TILE):
            groups = []
            for group in range(CHIPS // per_group):
                total = None
                for member in range(per_group):
                    goal = member * TILES_BLK
                    shift = (goal - (m * 2 + block) * TILES_BLK) % TILE
                    value = info[group * per_group + member]
                    value = pltpu.roll(value, shift, 1) if shift else value
                    here = (lane >= goal) & (lane < goal + TILES_BLK)
                    total = value if total is None else jnp.where(here, value, total)
                groups.append(total)
            rows.append(jnp.concatenate(groups, axis=1))
        tables.append(rows)

    targets = VISITS * OWN_DEV
    owned = targets // 2
    items = CHIPS * TILES_BLK
    row = lax.broadcasted_iota(jnp.int32, (targets, items), 0)
    side = (row // owned + core) % 2
    inner = row % owned
    wanted = ((inner // OWN_DEV) * 2 + side) * OWN_DEV + inner % OWN_DEV
    routes = []
    sums = None
    over_items = (((1,), (1,)), ((), ()))
    for block in range(2):
        target = tables[block][0][PER_TILE:PER_TILE + 1, :].astype(jnp.int32)
        route = jnp.where(wanted == target, 1.0, 0.0).astype(bf16)
        routes.append(route)
        weights = jnp.concatenate(
            tables[block] + [jnp.zeros((TILE - INFO * PER_TILE, items), f32)], axis=0
        )
        for half in split(weights):
            term = lax.dot_general(route, half, over_items, preferred_element_type=f32)
            sums = term if sums is None else sums + term
    mine_ref[owned * PIECE:, :] = sums[:owned]
    other_ref[owned * PIECE:, :] = sums[owned:]
    for line in range(PIECE):
        total = None
        for block, route in enumerate(routes):
            rows = pl.ds(block * TILES_BLK * PIECE + line, TILES_BLK, PIECE)
            part = part_ref[:, rows, :].reshape(items, TILE)
            high, low = split(part)
            term = jnp.dot(
                route, jnp.concatenate([high, low], axis=1), preferred_element_type=f32
            )
            total = term if total is None else total + term
        total = total[:, :TILE] + total[:, TILE:]
        mine_ref[pl.ds(line, owned, PIECE), :] = total[:owned]
        other_ref[pl.ds(line, owned, PIECE), :] = total[owned:]


def spread_cells(sums, cell_row):
    pattern = (
        lax.broadcasted_iota(jnp.int32, (TILE, TILE), 1) // CELL + cell_row * INFO
        == lax.broadcasted_iota(jnp.int32, (TILE, TILE), 0)
    ).astype(f32)
    return jnp.dot(sums, pattern, precision=lax.Precision.HIGHEST, preferred_element_type=f32)


def merge_kernel(place_ref, mine_ref, other_ref, out_ref):
    owned = VISITS * OWN_DEV // 2
    cell_row = (place_ref[0] // 2) // (CELL // PIECE)
    sums = mine_ref[owned * PIECE:, :] + other_ref[owned * PIECE:, :]
    scale = 1.0 / (spread_cells(sums, cell_row) + prior_weight)
    total = mine_ref[:owned * PIECE, :] + other_ref[:owned * PIECE, :]
    total = total.reshape(owned, PIECE, TILE) * scale[:, None, :]
    out_ref[...] = total.reshape(owned * PIECE, TILE)


def owner_kernel(place_ref, mine_ref, other_ref, part_ref, image_ref, chi_ref):
    owned = VISITS * OWN_DEV // 2
    rows = pl.ds(pl.multiple_of(owned * PIECE + (place_ref[0] // 2) * OWN_DEV, OWN_DEV), OWN_DEV)
    sums = mine_ref[rows, :] + other_ref[rows, :]
    spread = [spread_cells(sums, cell_row) + prior_weight for cell_row in range(PER_TILE)]
    for slot in range(OWN_DEV):
        image = part_ref[:, slot * PIECE:(slot + 1) * PIECE, :].reshape(TILE, TILE)
        image_ref[slot] = image
        weight = jnp.concatenate(
            [jnp.broadcast_to(spread[m][slot:slot + 1], (CELL, TILE)) for m in range(PER_TILE)],
            axis=0,
        )
        chi_ref[slot] = image * image * weight


def local(exposures, variance, mask_planes, kernel_table, kernel_index, tile_owner, tile_slot):
    place = lax.axis_index("visit").astype(jnp.int32).reshape(1)
    smem = pl.BlockSpec(memory_space=pltpu.SMEM)
    vmem = pl.BlockSpec(memory_space=pltpu.VMEM)
    params = pltpu.CompilerParams(vmem_limit_bytes=32 << 20)
    same_core = [list(range(core, VISITS, 2)) for core in range(2)]
    owned = VISITS * OWN_DEV // 2

    def exchange(pieces):
        return lax.all_to_all(pieces, "visit", 0, 0, axis_index_groups=same_core, tiled=True)

    table = kernel_table.T
    owner = tile_owner.reshape(tile_slot.shape)
    parts = exchange(
        match_blocks(exposures, variance, mask_planes, table, kernel_index, owner, tile_slot)
    )
    mine, other = pl.pallas_call(
        partial_kernel,
        out_shape=[jax.ShapeDtypeStruct((owned * (PIECE + 1), TILE), f32)] * 2,
        in_specs=[smem, vmem],
        out_specs=[vmem, vmem],
        compiler_params=params,
        name="partial_sums",
    )(place, parts)
    other = lax.ppermute(other, "visit", [(device, device ^ 1) for device in range(VISITS)])
    pieces = pl.pallas_call(
        merge_kernel,
        out_shape=jax.ShapeDtypeStruct((owned * PIECE, TILE), f32),
        in_specs=[smem, vmem, vmem],
        out_specs=vmem,
        compiler_params=params,
        name="merge_cores",
    )(place, mine, other)
    pieces = exchange(pieces.reshape(CHIPS, OWN_DEV * PIECE, TILE))
    image, chi = pl.pallas_call(
        owner_kernel,
        out_shape=[jax.ShapeDtypeStruct((OWN_DEV, TILE, TILE), f32)] * 2,
        in_specs=[smem, vmem, vmem, vmem],
        out_specs=[vmem, vmem],
        compiler_params=params,
        name="own",
    )(place, mine, other, pieces)

    for turn in range(2):
        partners = [
            (visit * 4 + band, visit * 4 + (band ^ (1 if (visit + turn) % 2 else 3)))
            for visit in range(VISITS)
            for band in range(4)
        ]
        chi = chi + lax.ppermute(chi, ("visit", "band"), partners)
    return image[None], chi


def solution(mesh):
    placed = (
        P("band", "visit", None, None),
        P("band", "visit", None, None),
        P("band", "visit", None, None),
        P(),
        P("band", "visit"),
        P("band", "visit", None),
        P("band", "visit"),
    )
    return jax.shard_map(
        local,
        mesh=mesh,
        in_specs=placed,
        out_specs=(P("band", "visit", None, None), P("visit", None, None)),
        check_vma=False,
    )
```

```python
import functools

import jax
import jax.numpy as jnp
import numpy as np
from jax import lax
from jax.experimental import pallas as pl
from jax.experimental.pallas import tpu as pltpu
from jax.sharding import PartitionSpec as P

BLOCK = 512
TILE = 128
CELL = 32
KSIZE = 41
OWN_DEV = 8
PADDED = BLOCK + KSIZE - 1
WIDE = 640
NFILT = 11
VISITS = 32
SIDE = BLOCK // TILE
CELLS = BLOCK // CELL
PER_TILE = TILE // CELL
TILES_BLK = SIDE * SIDE
CHIPS = VISITS // 2
PIECE = TILE // CHIPS
INFO = 8
SPAN = TILE + KSIZE - 1
HALF = SPAN // 2
TALL = 560

width_fractions = (0.075, 0.15, 0.3)
family_degrees = (4, 2, 2)
prior_weight = 0.05
reject_planes = 3

f32 = jnp.float32
bf16 = jnp.bfloat16


def as_halves(matrix):
    high = matrix.astype(np.float32).astype(bf16)
    low = (matrix - high.astype(np.float64)).astype(np.float32).astype(bf16)
    return high, low


def transforms():
    number = np.arange(HALF)
    angle = 2 * np.pi * (number + 0.5) / SPAN
    taps = np.arange(SPAN)
    cosine, sine = np.cos(angle[:, None] * taps), np.sin(angle[:, None] * taps)
    spot = 8 * (number // 4) + number % 4

    by_row = np.zeros((SPAN, SPAN))
    by_row[spot], by_row[spot + 4] = cosine, sine
    by_lane = np.zeros((2 * TILE, SPAN))
    by_lane[:HALF], by_lane[TILE:TILE + HALF] = cosine, sine

    across = np.zeros((2 * TILE, 2 * TILE))
    across[:SPAN] = by_lane.T
    down = np.zeros((SPAN + 8, SPAN))
    down[:SPAN] = by_row
    back_down = by_row.T[:TILE] * (2 / SPAN)
    back_across = by_lane[:, :TILE] * (2 / SPAN)

    def three(matrix):
        high, low = as_halves(matrix)
        rest = np.zeros((matrix.shape[0], 512 - 3 * SPAN), bf16)
        return np.concatenate([high, high, low, rest], axis=1)

    same = np.zeros((SPAN, TILE), np.float32)
    cross = np.zeros((SPAN, TILE), np.float32)
    same[spot, :KSIZE] = same[spot + 4, :KSIZE] = cosine[:, :KSIZE]
    cross[spot, :KSIZE], cross[spot + 4, :KSIZE] = sine[:, :KSIZE], -sine[:, :KSIZE]
    along = np.zeros((TILE, 2 * TILE), np.float32)
    along[:KSIZE, :HALF], along[:KSIZE, TILE:TILE + HALF] = cosine[:, :KSIZE].T, -sine[:, :KSIZE].T
    return (
        np.stack(as_halves(across)),
        three(down),
        three(back_down),
        np.concatenate(as_halves(back_across), axis=1),
        np.stack([same, cross]),
        along,
    )


def filter_terms():
    starts = (0, 5, 8)
    terms = []
    for family in range(3):
        for first in range(family_degrees[family] + 1):
            for second in range(family_degrees[family] + 1 - first):
                terms.append((starts[family] + first, starts[family] + second))
    return terms


def profiles_at(offset):
    half_width = (KSIZE - 1) // 2
    inside = (offset >= 0) & (offset < KSIZE)
    taps = offset.astype(f32) - half_width
    values = []
    for family in range(3):
        scaled = taps / (width_fractions[family] * half_width)
        value = jnp.where(inside, jnp.exp(-0.5 * scaled * scaled), 0.0)
        for degree in range(family_degrees[family] + 1):
            values.append(value)
            value = value * scaled
    return values


def split(value):
    high = value.astype(bf16)
    return high, (value - high.astype(f32)).astype(bf16)


def cell_weights(variance, bits):
    usable = (jnp.bitwise_and(bits, reject_planes) != reject_planes).astype(f32)
    return usable / variance


def item_info(var_ref, bits_ref, owner_ref, slot_ref):
    exact = lax.Precision.HIGHEST
    lane = lax.broadcasted_iota(jnp.int32, (1, TILE), 1)
    row = lax.broadcasted_iota(jnp.int32, (CELLS, TILE), 0)
    item = lane % TILES_BLK
    cell_row = (item // SIDE) * PER_TILE + lane // (2 * TILES_BLK)
    columns = None
    for block in range(2):
        picked = ((row == cell_row) & ((lane // TILES_BLK) % 2 == block)).astype(f32)
        term = lax.dot_general(
            cell_weights(var_ref[block], bits_ref[block]), picked,
            (((0,), (0,)), ((), ())), precision=exact, preferred_element_type=f32,
        )
        columns = term if columns is None else columns + term
    rows = []
    for n in range(PER_TILE):
        chosen = row == (item % SIDE) * PER_TILE + n
        rows.append(jnp.sum(jnp.where(chosen, columns, 0.0), axis=0, keepdims=True))
    target = (owner_ref[...] * OWN_DEV + slot_ref[...]).astype(f32)
    rows.append(jnp.concatenate([target, jnp.zeros((1, TILE - 2 * TILES_BLK), f32)], axis=1))
    rows.append(jnp.zeros((INFO - PER_TILE - 1, TILE), f32))
    return jnp.concatenate(rows, axis=0)


def phase_masks(core):
    return (1, 3) if core == 0 else (3, 1)


def way_to(place, piece):
    core, offset = place % 2, jnp.bitwise_xor(place // 2, piece)
    first, second = 0, 0
    for coordinate in (offset // 4, offset % 4):
        high = coordinate // 2
        both = jnp.bitwise_xor(high, coordinate % 2)
        first = 2 * first + jnp.where(core == 0, both, high)
        second = 2 * second + jnp.where(core == 0, high, both)
    return 4 * first + second


def chip_at(place, first, second):
    core = place % 2
    one, two = jnp.where(core == 0, 1, 3), jnp.where(core == 0, 3, 1)
    offset = 0
    for bit in (2, 1):
        step = jnp.bitwise_xor(
            one if first & bit else 0, two if second & bit else 0
        )
        offset = 4 * offset + step
    return jnp.bitwise_xor(place // 2, offset)


def phase_partners(phase, way):
    partners = []
    for device in range(VISITS):
        mask = phase_masks(device % 2)[phase]
        partners.append((device, device ^ (2 * (4 * mask * (way // 2) + mask * (way % 2)))))
    return partners


def exact_dot(left, right, sides=((1,), (0,))):
    return lax.dot_general(
        left, right, (sides, ((), ())), precision=lax.Precision.HIGHEST, preferred_element_type=f32
    )


def stacked_halves(value):
    high = value.astype(bf16).astype(f32)
    return jnp.concatenate([high, value - high], axis=0).astype(bf16)


def against_halves(matrix, halves_ref):
    rows = jnp.concatenate([halves_ref[...], halves_ref[:SPAN + 8, :]], axis=0)
    return jnp.dot(matrix, rows, preferred_element_type=f32)


def filter_bank():
    taps = lax.broadcasted_iota(jnp.int32, (1, TILE), 1)
    rows = [value / jnp.sqrt(jnp.sum(value * value, axis=1, keepdims=True)) for value in profiles_at(taps)]
    return jnp.concatenate(rows + [jnp.zeros((16 - NFILT, TILE), f32)], axis=0)


def kernel_spectrum(filters, which, table_ref, down_taps_ref, along_ref):
    first = lax.broadcasted_iota(jnp.int32, (16, 16), 0)
    second = lax.broadcasted_iota(jnp.int32, (16, 16), 1)
    mixing = jnp.zeros((16, 16), f32)
    for number, (p, q) in enumerate(filter_terms()):
        mixing = jnp.where((first == p) & (second == q), table_ref[number, which], mixing)
    across = exact_dot(mixing, exact_dot(filters, along_ref[...]))
    return [
        exact_dot(exact_dot(down_taps_ref[part], filters, ((1,), (1,))), across)
        for part in range(2)
    ]


def match_kernel(
    place_ref, index_hbm, table_hbm, image_hbm, var_hbm, bits_hbm, owner_hbm, slot_hbm,
    across_hbm, down_hbm, back_down_hbm, back_across_hbm, down_taps_hbm, along_hbm, out_0, out_1, out_2, out_3,
    index_ref, table_ref, image_ref, var_ref, bits_ref, owner_ref, slot_ref,
    across_ref, down_ref, back_down_ref, back_across_ref, down_taps_ref, along_ref, sems, out_sems,
    tail_ref, high_ref, low_ref, wave_ref, stack_ref, turn_ref, result_ref, rows_ref, factor_ref,
    weight_ref, out_ref,
):
    blocks = range(2)
    copies = [
        pltpu.make_async_copy(source, goal, sems.at[number])
        for number, (source, goal) in enumerate((
            (index_hbm, index_ref),
            (table_hbm, table_ref),
            (down_taps_hbm, down_taps_ref),
            (along_hbm, along_ref),
            (image_hbm.at[0, 0], image_ref.at[0]),
            (across_hbm, across_ref),
            (var_hbm.at[0], var_ref),
            (bits_hbm.at[0], bits_ref),
            (owner_hbm, owner_ref),
            (slot_hbm, slot_ref),
            (image_hbm.at[0, 1], image_ref.at[1]),
            (down_hbm, down_ref),
            (back_down_hbm, back_down_ref),
            (back_across_hbm, back_across_ref),
        ))
    ]
    for copy in copies:
        copy.start()
    tail_ref[...] = jnp.zeros_like(tail_ref)
    filters = filter_bank()
    spread = (
        lax.broadcasted_iota(jnp.int32, (CELLS, BLOCK), 1) // CELL
        == lax.broadcasted_iota(jnp.int32, (CELLS, BLOCK), 0)
    ).astype(f32)
    for copy in copies:
        copy.wait()

    pair = 2 * TILE
    forward = jnp.concatenate([across_ref[0], across_ref[0], across_ref[1]], axis=0)
    backward = jnp.concatenate([back_across_ref[...], back_across_ref[...]], axis=0)
    sends = []
    spots = [way_to(place_ref[0], piece) for piece in range(CHIPS)]

    def send(part, first, last):
        for way, out_hbm in enumerate((out_0, out_1, out_2, out_3)):
            ways = slice(way * 4, way * 4 + 4)
            sends.append(
                pltpu.make_async_copy(
                    out_ref.at[ways, first:last], out_hbm.at[:, first:last], out_sems.at[part, way]
                )
            )
            sends[-1].start()

    def halve(block):
        tail_ref[block, :PADDED, :PADDED - BLOCK] = image_ref[block, :, BLOCK:]
        whole = TALL - 16
        for first, width, source in ((0, BLOCK, image_ref), (BLOCK, TILE, tail_ref)):
            lanes = slice(first, first + width)
            high_ref[block, :whole, lanes], low_ref[block, :whole, lanes] = split(
                source[block, :whole, :width]
            )
            last = jnp.concatenate(
                [source[block, whole:PADDED, :width], jnp.zeros((8, width), f32)], axis=0
            )
            high_ref[block, whole:, lanes], low_ref[block, whole:, lanes] = split(last)

    def transform_across(block, column):
        lanes = slice(column * TILE, column * TILE + pair)
        high, low = high_ref[block, :, lanes], low_ref[block, :, lanes]
        wave_ref[block, :, column * pair:(column + 1) * pair] = jnp.dot(
            jnp.concatenate([high, low, high], axis=1), forward, preferred_element_type=f32
        )

    def prepare(block):
        same, cross = kernel_spectrum(
            filters, index_ref[0, block], table_ref, down_taps_ref, along_ref
        )
        factor_ref[block, 0] = same.reshape(SPAN // 8, 8, pair)
        factor_ref[block, 1] = cross.reshape(SPAN // 8, 8, pair)
        weight_ref[block] = exact_dot(cell_weights(var_ref[block], bits_ref[block]), spread)

    def transform_down(block, line):
        for column in range(SIDE):
            lanes = slice(column * pair, (column + 1) * pair)
            stack_ref[block, line, :, lanes] = stacked_halves(
                wave_ref[block, line * TILE:line * TILE + SPAN, lanes]
            )
        turn_ref[block, line] = against_halves(down_ref[...], stack_ref.at[block, line])

    def multiply(block, line):
        for column in range(SIDE):
            lanes = slice(column * pair, (column + 1) * pair)
            wave = turn_ref[block, line, :SPAN, lanes].reshape(SPAN // 8, 8, pair)
            turned = pltpu.roll(wave, 4, 1)
            wave_c, wave_s = wave[..., :TILE], wave[..., TILE:]
            turned_c, turned_s = turned[..., :TILE], turned[..., TILE:]
            same_c, same_s = factor_ref[block, 0, :, :, :TILE], factor_ref[block, 0, :, :, TILE:]
            cross_c, cross_s = factor_ref[block, 1, :, :, :TILE], factor_ref[block, 1, :, :, TILE:]
            result_c = wave_c * same_c + turned_c * cross_c - wave_s * same_s - turned_s * cross_s
            result_s = wave_s * same_c + turned_s * cross_c + wave_c * same_s + turned_c * cross_s
            result = jnp.concatenate(
                [result_c.reshape(SPAN, TILE), result_s.reshape(SPAN, TILE)], axis=1
            )
            result_ref[block, line, :, lanes] = stacked_halves(result)

    def back_down(block, line):
        rows = against_halves(back_down_ref[...], result_ref.at[block, line])
        for column in range(SIDE):
            high, low = split(rows[:, column * pair:(column + 1) * pair])
            rows_ref[block, column, line * TILE:(line + 1) * TILE, :pair] = high
            rows_ref[block, column, line * TILE:(line + 1) * TILE, pair:] = low

    def back_across(block, column):
        matched = jnp.dot(rows_ref[block, column], backward, preferred_element_type=f32)
        matched = matched[:, :TILE] + matched[:, TILE:]
        weight = weight_ref[block, :, column * TILE:(column + 1) * TILE]
        weighted = matched.reshape(CELLS, CELL, TILE) * weight[:, None, :]
        weighted = weighted.reshape(SIDE, CHIPS, PIECE, TILE)
        for line in range(SIDE):
            item = block * TILES_BLK + line * SIDE + column
            for piece in range(CHIPS):
                out_ref[spots[piece], item] = weighted[line, piece]

    halve(0)
    for column in range(SIDE):
        transform_across(0, column)
    halve(1)
    for block in blocks:
        prepare(block)
    info = item_info(var_ref, bits_ref, owner_ref, slot_ref)
    out_ref[:, 2 * TILES_BLK] = jnp.broadcast_to(info[None], (CHIPS, INFO, TILE))
    for line in range(SIDE):
        transform_across(1, line)
        transform_down(0, line)
    for line in range(SIDE):
        transform_down(1, line)
        multiply(0, line)
    for line in range(SIDE):
        back_down(0, line)
        multiply(1, line)
    for line in range(SIDE):
        back_across(0, line)
        back_down(1, line)
    send(0, 0, TILES_BLK)
    for line in range(SIDE):
        back_across(1, line)
    send(1, TILES_BLK, 2 * TILES_BLK + 1)
    for copy in sends:
        copy.wait()


def match_blocks(place, exposures, variance, bits, table, index, owner, slot):
    blocks = exposures.shape[1]
    items = blocks * TILES_BLK
    groups = items + 1
    matrices = transforms()
    return pl.pallas_call(
        match_kernel,
        out_shape=[jax.ShapeDtypeStruct((4, groups, PIECE, TILE), f32)] * 4,
        in_specs=[pl.BlockSpec(memory_space=pltpu.SMEM)]
        + [pl.BlockSpec(memory_space=pltpu.HBM)] * (7 + len(matrices)),
        out_specs=[pl.BlockSpec(memory_space=pltpu.HBM)] * 4,
        scratch_shapes=[
            pltpu.SMEM((1, blocks), jnp.int32),
            pltpu.SMEM(table.shape, f32),
            pltpu.VMEM((blocks, PADDED, PADDED), f32),
            pltpu.VMEM((blocks, CELLS, CELLS), f32),
            pltpu.VMEM((blocks, CELLS, CELLS), jnp.int32),
            pltpu.VMEM((1, items), jnp.int32),
            pltpu.VMEM((1, items), jnp.int32),
            *[pltpu.VMEM(matrix.shape, matrix.dtype) for matrix in matrices],
            pltpu.SemaphoreType.DMA((8 + len(matrices),)),
            pltpu.SemaphoreType.DMA((2, 4)),
            pltpu.VMEM((blocks, TALL, TILE), f32),
            pltpu.VMEM((blocks, TALL, WIDE), bf16),
            pltpu.VMEM((blocks, TALL, WIDE), bf16),
            pltpu.VMEM((blocks, TALL, 2 * BLOCK), f32),
            pltpu.VMEM((blocks, SIDE, 2 * SPAN, 2 * BLOCK), bf16),
            pltpu.VMEM((blocks, SIDE, SPAN + 8, 2 * BLOCK), f32),
            pltpu.VMEM((blocks, SIDE, 2 * SPAN, 2 * BLOCK), bf16),
            pltpu.VMEM((blocks, SIDE, BLOCK, 4 * TILE), bf16),
            pltpu.VMEM((blocks, 2, SPAN // 8, 8, 2 * TILE), f32),
            pltpu.VMEM((blocks, CELLS, BLOCK), f32),
            pltpu.VMEM((CHIPS, groups, PIECE, TILE), f32),
        ],
        compiler_params=pltpu.CompilerParams(vmem_limit_bytes=60 << 20),
        cost_estimate=pl.CostEstimate(
            flops=2 * 256 * 256 * 40000, bytes_accessed=6 << 20, transcendentals=0
        ),
        name="match_blocks",
    )(place, index, table, exposures, variance, bits, owner, slot, *matrices)


WAYS = (0, 3, 1, 2)


def keep_kernel(part_hbm, out_ref, sem):
    copy = pltpu.make_async_copy(part_hbm, out_ref, sem)
    copy.start()
    copy.wait()


def turn_kernel(*refs):
    for first, part_ref in zip(WAYS, refs[:4]):
        for second, out_ref in enumerate(refs[4:]):
            out_ref[first] = part_ref[second]


def partial_kernel(place_ref, *refs):
    part_refs, (mine_ref, other_ref) = refs[:4], refs[4:]
    core = place_ref[0] % 2
    per_group = TILE // TILES_BLK
    lane = lax.broadcasted_iota(jnp.int32, (INFO, TILE), 1)
    info = [part_refs[source // 4][source % 4, 2 * TILES_BLK * PIECE:] for source in range(CHIPS)]
    tables = []
    for block in range(2):
        rows = []
        for m in range(PER_TILE):
            groups = []
            for group in range(CHIPS // per_group):
                total = None
                for member in range(per_group):
                    goal = member * TILES_BLK
                    shift = (goal - (m * 2 + block) * TILES_BLK) % TILE
                    value = info[group * per_group + member]
                    value = pltpu.roll(value, shift, 1) if shift else value
                    here = (lane >= goal) & (lane < goal + TILES_BLK)
                    total = value if total is None else jnp.where(here, value, total)
                groups.append(total)
            rows.append(jnp.concatenate(groups, axis=1))
        tables.append(rows)

    targets = VISITS * OWN_DEV
    owned = targets // 2
    items = CHIPS * TILES_BLK
    row = lax.broadcasted_iota(jnp.int32, (targets, items), 0)
    side = (row // owned + core) % 2
    inner = row % owned
    wanted = ((inner // OWN_DEV) * 2 + side) * OWN_DEV + inner % OWN_DEV
    routes = []
    sums = None
    over_items = (((1,), (1,)), ((), ()))
    for block in range(2):
        target = tables[block][0][PER_TILE:PER_TILE + 1, :].astype(jnp.int32)
        route = jnp.where(wanted == target, 1.0, 0.0).astype(bf16)
        routes.append(route)
        weights = jnp.concatenate(
            tables[block] + [jnp.zeros((TILE - INFO * PER_TILE, items), f32)], axis=0
        )
        for half in split(weights):
            term = lax.dot_general(route, half, over_items, preferred_element_type=f32)
            sums = term if sums is None else sums + term
    mine_ref[owned * PIECE:, :] = sums[:owned]
    other_ref[owned * PIECE:, :] = sums[owned:]
    for line in range(PIECE):
        total = None
        for block, route in enumerate(routes):
            rows = pl.ds(block * TILES_BLK * PIECE + line, TILES_BLK, PIECE)
            part = jnp.concatenate(
                [part_ref[:, rows, :].reshape(items // 4, TILE) for part_ref in part_refs], axis=0
            )
            high, low = split(part)
            term = jnp.dot(
                route, jnp.concatenate([high, low], axis=1), preferred_element_type=f32
            )
            total = term if total is None else total + term
        total = total[:, :TILE] + total[:, TILE:]
        mine_ref[pl.ds(line, owned, PIECE), :] = total[:owned]
        other_ref[pl.ds(line, owned, PIECE), :] = total[owned:]


def spread_cells(sums, cell_row):
    pattern = (
        lax.broadcasted_iota(jnp.int32, (TILE, TILE), 1) // CELL + cell_row * INFO
        == lax.broadcasted_iota(jnp.int32, (TILE, TILE), 0)
    ).astype(f32)
    return jnp.dot(sums, pattern, precision=lax.Precision.HIGHEST, preferred_element_type=f32)


def merge_kernel(place_ref, mine_ref, other_ref, *refs):
    out_refs, scale_ref = refs[:4], refs[4]
    owned = VISITS * OWN_DEV // 2
    cell_row = (place_ref[0] // 2) // (CELL // PIECE)
    sums = mine_ref[owned * PIECE:, :] + other_ref[owned * PIECE:, :]
    scale_ref[...] = 1.0 / (spread_cells(sums, cell_row) + prior_weight)
    height = OWN_DEV * PIECE
    for first in range(4):
        for second in range(4):
            goal = chip_at(place_ref[0], first, second)
            rows = pl.ds(pl.multiple_of(goal * height, height), height)
            scale = scale_ref[pl.ds(pl.multiple_of(goal * OWN_DEV, OWN_DEV), OWN_DEV), :]
            total = (mine_ref[rows, :] + other_ref[rows, :]).reshape(OWN_DEV, PIECE, TILE)
            out_refs[first][second] = total * scale[:, None, :]


def owner_kernel(place_ref, mine_ref, other_ref, *refs):
    part_refs, (image_ref, chi_ref) = refs[:4], refs[4:]
    owned = VISITS * OWN_DEV // 2
    chip = place_ref[0] // 2
    rows = pl.ds(pl.multiple_of(owned * PIECE + chip * OWN_DEV, OWN_DEV), OWN_DEV)
    sums = mine_ref[rows, :] + other_ref[rows, :]
    spread = [spread_cells(sums, cell_row) + prior_weight for cell_row in range(PER_TILE)]
    for second, part_ref in zip(WAYS, part_refs):
        for first in range(4):
            source = chip_at(place_ref[0], first, second)
            image_ref[:, pl.ds(pl.multiple_of(source * PIECE, PIECE), PIECE), :] = part_ref[first]
    for slot in range(OWN_DEV):
        image = image_ref[slot]
        weight = jnp.concatenate(
            [jnp.broadcast_to(spread[m][slot:slot + 1], (CELL, TILE)) for m in range(PER_TILE)],
            axis=0,
        )
        chi_ref[slot] = image * image * weight


def local(exposures, variance, mask_planes, kernel_table, kernel_index, tile_owner, tile_slot):
    place = lax.axis_index("visit").astype(jnp.int32).reshape(1)
    smem = pl.BlockSpec(memory_space=pltpu.SMEM)
    vmem = pl.BlockSpec(memory_space=pltpu.VMEM)
    params = pltpu.CompilerParams(vmem_limit_bytes=32 << 20)
    owned = VISITS * OWN_DEV // 2

    def exchange(parts):
        for phase in range(2):
            parts = [
                lax.ppermute(parts[way], "visit", phase_partners(phase, way)) if way else parts[0]
                for way in WAYS
            ]
            if phase == 0:
                parts = pl.pallas_call(
                    turn_kernel,
                    out_shape=[jax.ShapeDtypeStruct(parts[0].shape, f32)] * 4,
                    in_specs=[vmem] * 4,
                    out_specs=[vmem] * 4,
                    compiler_params=params,
                    name="turn",
                )(*parts)
        return parts

    table = kernel_table.T
    owner = tile_owner.reshape(tile_slot.shape)
    parts = match_blocks(
        place, exposures, variance, mask_planes, table, kernel_index, owner, tile_slot
    )
    own = pl.pallas_call(
        keep_kernel,
        out_shape=jax.ShapeDtypeStruct(parts[0].shape, f32),
        in_specs=[pl.BlockSpec(memory_space=pltpu.HBM)],
        out_specs=vmem,
        scratch_shapes=[pltpu.SemaphoreType.DMA],
        compiler_params=params,
        name="keep",
    )(parts[0])
    parts = [part.reshape(4, -1, TILE) for part in exchange([own, *parts[1:]])]

    mine, other = pl.pallas_call(
        partial_kernel,
        out_shape=[jax.ShapeDtypeStruct((owned * (PIECE + 1), TILE), f32)] * 2,
        in_specs=[smem] + [vmem] * 4,
        out_specs=[vmem, vmem],
        compiler_params=params,
        name="partial_sums",
    )(place, *parts)
    other = lax.ppermute(other, "visit", [(device, device ^ 1) for device in range(VISITS)])
    pieces = pl.pallas_call(
        merge_kernel,
        out_shape=[jax.ShapeDtypeStruct((4, OWN_DEV, PIECE, TILE), f32)] * 4,
        in_specs=[smem, vmem, vmem],
        out_specs=[vmem] * 4,
        scratch_shapes=[pltpu.VMEM((owned, TILE), f32)],
        compiler_params=params,
        name="merge_cores",
    )(place, mine, other)
    pieces = exchange(pieces)
    image, chi = pl.pallas_call(
        owner_kernel,
        out_shape=[jax.ShapeDtypeStruct((OWN_DEV, TILE, TILE), f32)] * 2,
        in_specs=[smem, vmem, vmem] + [vmem] * 4,
        out_specs=[vmem, vmem],
        compiler_params=params,
        name="own",
    )(place, mine, other, *pieces)

    pairings = ([(0, 1), (1, 0), (2, 3), (3, 2)], [(0, 3), (3, 0), (1, 2), (2, 1)])
    halves = [chi[:OWN_DEV // 2], chi[OWN_DEV // 2:]]
    for turn in range(2):
        halves = [
            half + lax.ppermute(half, "band", pairings[(turn + number) % 2])
            for number, half in enumerate(halves)
        ]
    return image[None], jnp.concatenate(halves, axis=0)


def solution(mesh):
    placed = (
        P("band", "visit", None, None),
        P("band", "visit", None, None),
        P("band", "visit", None, None),
        P(),
        P("band", "visit"),
        P("band", "visit", None),
        P("band", "visit"),
    )
    return jax.shard_map(
        local,
        mesh=mesh,
        in_specs=placed,
        out_specs=(P("band", "visit", None, None), P("visit", None, None)),
        check_vma=False,
    )
```

```python
import functools

import jax
import jax.numpy as jnp
import numpy as np
from jax import lax
from jax.experimental import pallas as pl
from jax.experimental.pallas import tpu as pltpu
from jax.sharding import PartitionSpec as P

BLOCK = 512
TILE = 128
CELL = 32
KSIZE = 41
OWN_DEV = 8
PADDED = BLOCK + KSIZE - 1
WIDE = 640
NFILT = 11
VISITS = 32
SIDE = BLOCK // TILE
CELLS = BLOCK // CELL
PER_TILE = TILE // CELL
TILES_BLK = SIDE * SIDE
CHIPS = VISITS // 2
PIECE = TILE // CHIPS
INFO = 8
SPAN = TILE + KSIZE - 1
HALF = SPAN // 2
TALL = 560

width_fractions = (0.075, 0.15, 0.3)
family_degrees = (4, 2, 2)
prior_weight = 0.05
reject_planes = 3

f32 = jnp.float32
bf16 = jnp.bfloat16


def as_halves(matrix):
    high = matrix.astype(np.float32).astype(bf16)
    low = (matrix - high.astype(np.float64)).astype(np.float32).astype(bf16)
    return high, low


def transforms():
    number = np.arange(HALF)
    angle = 2 * np.pi * (number + 0.5) / SPAN
    taps = np.arange(SPAN)
    cosine, sine = np.cos(angle[:, None] * taps), np.sin(angle[:, None] * taps)
    spot = 8 * (number // 4) + number % 4

    by_row = np.zeros((SPAN, SPAN))
    by_row[spot], by_row[spot + 4] = cosine, sine
    by_lane = np.zeros((2 * TILE, SPAN))
    by_lane[:HALF], by_lane[TILE:TILE + HALF] = cosine, sine

    across = np.zeros((2 * TILE, 2 * TILE))
    across[:SPAN] = by_lane.T
    down = np.zeros((SPAN + 8, SPAN))
    down[:SPAN] = by_row
    back_down = by_row.T[:TILE] * (2 / SPAN)
    back_across = by_lane[:, :TILE] * (2 / SPAN)

    def three(matrix):
        high, low = as_halves(matrix)
        rest = np.zeros((matrix.shape[0], 512 - 3 * SPAN), bf16)
        return np.concatenate([high, high, low, rest], axis=1)

    same = np.zeros((SPAN, TILE), np.float32)
    cross = np.zeros((SPAN, TILE), np.float32)
    same[spot, :KSIZE] = same[spot + 4, :KSIZE] = cosine[:, :KSIZE]
    cross[spot, :KSIZE], cross[spot + 4, :KSIZE] = sine[:, :KSIZE], -sine[:, :KSIZE]
    along = np.zeros((TILE, 2 * TILE), np.float32)
    along[:KSIZE, :HALF], along[:KSIZE, TILE:TILE + HALF] = cosine[:, :KSIZE].T, -sine[:, :KSIZE].T
    return (
        np.stack(as_halves(across)),
        three(down),
        three(back_down),
        np.concatenate(as_halves(back_across), axis=1),
        np.stack([same, cross]),
        along,
    )


def filter_terms():
    starts = (0, 5, 8)
    terms = []
    for family in range(3):
        for first in range(family_degrees[family] + 1):
            for second in range(family_degrees[family] + 1 - first):
                terms.append((starts[family] + first, starts[family] + second))
    return terms


def profiles_at(offset):
    half_width = (KSIZE - 1) // 2
    inside = (offset >= 0) & (offset < KSIZE)
    taps = offset.astype(f32) - half_width
    values = []
    for family in range(3):
        scaled = taps / (width_fractions[family] * half_width)
        value = jnp.where(inside, jnp.exp(-0.5 * scaled * scaled), 0.0)
        for degree in range(family_degrees[family] + 1):
            values.append(value)
            value = value * scaled
    return values


def split(value):
    high = value.astype(bf16)
    return high, (value - high.astype(f32)).astype(bf16)


def cell_weights(variance, bits):
    usable = (jnp.bitwise_and(bits, reject_planes) != reject_planes).astype(f32)
    return usable / variance


def item_info(var_ref, bits_ref, owner_ref, slot_ref):
    exact = lax.Precision.HIGHEST
    lane = lax.broadcasted_iota(jnp.int32, (1, TILE), 1)
    row = lax.broadcasted_iota(jnp.int32, (CELLS, TILE), 0)
    item = lane % TILES_BLK
    cell_row = (item // SIDE) * PER_TILE + lane // (2 * TILES_BLK)
    columns = None
    for block in range(2):
        picked = ((row == cell_row) & ((lane // TILES_BLK) % 2 == block)).astype(f32)
        term = lax.dot_general(
            cell_weights(var_ref[block], bits_ref[block]), picked,
            (((0,), (0,)), ((), ())), precision=exact, preferred_element_type=f32,
        )
        columns = term if columns is None else columns + term
    rows = []
    for n in range(PER_TILE):
        chosen = row == (item % SIDE) * PER_TILE + n
        rows.append(jnp.sum(jnp.where(chosen, columns, 0.0), axis=0, keepdims=True))
    target = (owner_ref[...] * OWN_DEV + slot_ref[...]).astype(f32)
    rows.append(jnp.concatenate([target, jnp.zeros((1, TILE - 2 * TILES_BLK), f32)], axis=1))
    rows.append(jnp.zeros((INFO - PER_TILE - 1, TILE), f32))
    return jnp.concatenate(rows, axis=0)


def phase_masks(core):
    return (1, 3) if core == 0 else (3, 1)


def way_to(place, piece):
    core, offset = place % 2, jnp.bitwise_xor(place // 2, piece)
    first, second = 0, 0
    for coordinate in (offset // 4, offset % 4):
        high = coordinate // 2
        both = jnp.bitwise_xor(high, coordinate % 2)
        first = 2 * first + jnp.where(core == 0, both, high)
        second = 2 * second + jnp.where(core == 0, high, both)
    return 4 * first + second


def phase_partners(phase, way):
    partners = []
    for device in range(VISITS):
        mask = phase_masks(device % 2)[phase]
        partners.append((device, device ^ (2 * (4 * mask * (way // 2) + mask * (way % 2)))))
    return partners


def exact_dot(left, right, sides=((1,), (0,))):
    return lax.dot_general(
        left, right, (sides, ((), ())), precision=lax.Precision.HIGHEST, preferred_element_type=f32
    )


def stacked_halves(value):
    high = value.astype(bf16).astype(f32)
    return jnp.concatenate([high, value - high], axis=0).astype(bf16)


def against_halves(matrix, halves_ref):
    rows = jnp.concatenate([halves_ref[...], halves_ref[:SPAN + 8, :]], axis=0)
    return jnp.dot(matrix, rows, preferred_element_type=f32)


def filter_bank():
    taps = lax.broadcasted_iota(jnp.int32, (1, TILE), 1)
    rows = [value / jnp.sqrt(jnp.sum(value * value, axis=1, keepdims=True)) for value in profiles_at(taps)]
    return jnp.concatenate(rows + [jnp.zeros((16 - NFILT, TILE), f32)], axis=0)


def kernel_spectrum(filters, which, table_ref, down_taps_ref, along_ref):
    first = lax.broadcasted_iota(jnp.int32, (16, 16), 0)
    second = lax.broadcasted_iota(jnp.int32, (16, 16), 1)
    mixing = jnp.zeros((16, 16), f32)
    for number, (p, q) in enumerate(filter_terms()):
        mixing = jnp.where((first == p) & (second == q), table_ref[number, which], mixing)
    across = exact_dot(mixing, exact_dot(filters, along_ref[...]))
    return [
        exact_dot(exact_dot(down_taps_ref[part], filters, ((1,), (1,))), across)
        for part in range(2)
    ]


def match_kernel(
    place_ref, index_hbm, table_hbm, image_hbm, var_hbm, bits_hbm, owner_hbm, slot_hbm,
    across_hbm, down_hbm, back_down_hbm, back_across_hbm, down_taps_hbm, along_hbm,
    out_0, out_1, out_2, out_3,
    index_ref, table_ref, image_ref, var_ref, bits_ref, owner_ref, slot_ref,
    across_ref, down_ref, back_down_ref, back_across_ref, down_taps_ref, along_ref, sems, out_sems,
    tail_ref, high_ref, low_ref, wave_ref, stack_ref, turn_ref, result_ref, rows_ref, factor_ref,
    weight_ref, out_ref,
    *, block,
):
    copies = [
        pltpu.make_async_copy(source, goal, sems.at[number])
        for number, (source, goal) in enumerate((
            (index_hbm, index_ref),
            (table_hbm, table_ref),
            (down_taps_hbm, down_taps_ref),
            (along_hbm, along_ref),
            (image_hbm.at[0, block], image_ref),
            (across_hbm, across_ref),
            (var_hbm.at[0], var_ref),
            (bits_hbm.at[0], bits_ref),
            (owner_hbm, owner_ref),
            (slot_hbm, slot_ref),
            (down_hbm, down_ref),
            (back_down_hbm, back_down_ref),
            (back_across_hbm, back_across_ref),
        ))
    ]
    for copy in copies:
        copy.start()
    tail_ref[...] = jnp.zeros_like(tail_ref)
    filters = filter_bank()
    spread = (
        lax.broadcasted_iota(jnp.int32, (CELLS, BLOCK), 1) // CELL
        == lax.broadcasted_iota(jnp.int32, (CELLS, BLOCK), 0)
    ).astype(f32)
    for copy in copies:
        copy.wait()

    pair = 2 * TILE
    forward = jnp.concatenate([across_ref[0], across_ref[0], across_ref[1]], axis=0)
    backward = jnp.concatenate([back_across_ref[...], back_across_ref[...]], axis=0)
    spots = [way_to(place_ref[0], piece) for piece in range(CHIPS)]

    def halve():
        tail_ref[:PADDED, :PADDED - BLOCK] = image_ref[:, BLOCK:]
        whole = TALL - 16
        for first, width, source in ((0, BLOCK, image_ref), (BLOCK, TILE, tail_ref)):
            lanes = slice(first, first + width)
            high_ref[:whole, lanes], low_ref[:whole, lanes] = split(source[:whole, :width])
            last = jnp.concatenate(
                [source[whole:PADDED, :width], jnp.zeros((8, width), f32)], axis=0
            )
            high_ref[whole:, lanes], low_ref[whole:, lanes] = split(last)

    def transform_across(column):
        lanes = slice(column * TILE, column * TILE + pair)
        high, low = high_ref[:, lanes], low_ref[:, lanes]
        wave_ref[column] = jnp.dot(
            jnp.concatenate([high, low, high], axis=1), forward, preferred_element_type=f32
        )

    def prepare():
        same, cross = kernel_spectrum(
            filters, index_ref[0, block], table_ref, down_taps_ref, along_ref
        )
        factor_ref[0] = same.reshape(SPAN // 8, 8, pair)
        factor_ref[1] = cross.reshape(SPAN // 8, 8, pair)
        weight_ref[...] = exact_dot(cell_weights(var_ref[block], bits_ref[block]), spread)
        if block == 0:
            info = item_info(var_ref, bits_ref, owner_ref, slot_ref)
            out_ref[:, TILES_BLK] = jnp.broadcast_to(info[None], (CHIPS, INFO, TILE))

    def stack(tile):
        column, line = divmod(tile, SIDE)
        stack_ref[tile] = stacked_halves(wave_ref[column, line * TILE:line * TILE + SPAN, :])

    def transform_down(tile):
        turn_ref[tile] = against_halves(down_ref[...], stack_ref.at[tile])

    def multiply(tile):
        wave = turn_ref[tile, :SPAN].reshape(SPAN // 8, 8, pair)
        turned = pltpu.roll(wave, 4, 1)
        wave_c, wave_s = wave[..., :TILE], wave[..., TILE:]
        turned_c, turned_s = turned[..., :TILE], turned[..., TILE:]
        same_c, same_s = factor_ref[0, :, :, :TILE], factor_ref[0, :, :, TILE:]
        cross_c, cross_s = factor_ref[1, :, :, :TILE], factor_ref[1, :, :, TILE:]
        result_c = wave_c * same_c + turned_c * cross_c - wave_s * same_s - turned_s * cross_s
        result_s = wave_s * same_c + turned_s * cross_c + wave_c * same_s + turned_c * cross_s
        result = jnp.concatenate(
            [result_c.reshape(SPAN, TILE), result_s.reshape(SPAN, TILE)], axis=1
        )
        result_ref[tile] = stacked_halves(result)

    def back_down(tile):
        column, line = divmod(tile, SIDE)
        high, low = split(against_halves(back_down_ref[...], result_ref.at[tile]))
        rows_ref[column, line * TILE:(line + 1) * TILE, :pair] = high
        rows_ref[column, line * TILE:(line + 1) * TILE, pair:] = low

    def back_across(column):
        matched = jnp.dot(rows_ref[column], backward, preferred_element_type=f32)
        matched = matched[:, :TILE] + matched[:, TILE:]
        weight = weight_ref[:, column * TILE:(column + 1) * TILE]
        weighted = matched.reshape(CELLS, CELL, TILE) * weight[:, None, :]
        weighted = weighted.reshape(SIDE, CHIPS, PIECE, TILE)
        for line in range(SIDE):
            item = line * SIDE + column
            for piece in range(CHIPS):
                out_ref[spots[piece], item] = weighted[line, piece]

    halve()
    transform_across(0)
    prepare()
    for step in range(TILES_BLK + 5):
        if step % SIDE == 0 and step // SIDE + 1 < SIDE:
            transform_across(step // SIDE + 1)
        for delay, stage in enumerate((stack, transform_down, multiply, back_down)):
            if 0 <= step - delay < TILES_BLK:
                stage(step - delay)
        column, rest = divmod(step - 4, SIDE)
        if rest == SIDE - 1 and 0 <= column < SIDE:
            back_across(column)
    sends = [
        pltpu.make_async_copy(out_ref.at[way * 4:way * 4 + 4], out_hbm, out_sems.at[way])
        for way, out_hbm in enumerate((out_0, out_1, out_2, out_3))
    ]
    for way in (3, 1, 2, 0):
        sends[way].start()
    for send in sends:
        send.wait()


def match_block(block, place, exposures, variance, bits, table, index, owner, slot):
    blocks = exposures.shape[1]
    items = blocks * TILES_BLK
    groups = TILES_BLK + (1 if block == 0 else 0)
    matrices = transforms()
    return pl.pallas_call(
        functools.partial(match_kernel, block=block),
        out_shape=[jax.ShapeDtypeStruct((4, groups, PIECE, TILE), f32)] * 4,
        in_specs=[pl.BlockSpec(memory_space=pltpu.SMEM)]
        + [pl.BlockSpec(memory_space=pltpu.HBM)] * (7 + len(matrices)),
        out_specs=[pl.BlockSpec(memory_space=pltpu.HBM)] * 4,
        scratch_shapes=[
            pltpu.SMEM((1, blocks), jnp.int32),
            pltpu.SMEM(table.shape, f32),
            pltpu.VMEM((PADDED, PADDED), f32),
            pltpu.VMEM((blocks, CELLS, CELLS), f32),
            pltpu.VMEM((blocks, CELLS, CELLS), jnp.int32),
            pltpu.VMEM((1, items), jnp.int32),
            pltpu.VMEM((1, items), jnp.int32),
            *[pltpu.VMEM(matrix.shape, matrix.dtype) for matrix in matrices],
            pltpu.SemaphoreType.DMA((7 + len(matrices),)),
            pltpu.SemaphoreType.DMA((4,)),
            pltpu.VMEM((TALL, TILE), f32),
            pltpu.VMEM((TALL, WIDE), bf16),
            pltpu.VMEM((TALL, WIDE), bf16),
            pltpu.VMEM((SIDE, TALL, 2 * TILE), f32),
            pltpu.VMEM((TILES_BLK, 2 * SPAN, 2 * TILE), bf16),
            pltpu.VMEM((TILES_BLK, SPAN + 8, 2 * TILE), f32),
            pltpu.VMEM((TILES_BLK, 2 * SPAN, 2 * TILE), bf16),
            pltpu.VMEM((SIDE, BLOCK, 4 * TILE), bf16),
            pltpu.VMEM((2, SPAN // 8, 8, 2 * TILE), f32),
            pltpu.VMEM((CELLS, BLOCK), f32),
            pltpu.VMEM((CHIPS, groups, PIECE, TILE), f32),
        ],
        compiler_params=pltpu.CompilerParams(vmem_limit_bytes=59 << 20),
        cost_estimate=pl.CostEstimate(
            flops=2 * 256 * 256 * 40000, bytes_accessed=3 << 20, transcendentals=0
        ),
        name="match_block",
    )(place, index, table, exposures, variance, bits, owner, slot, *matrices)


WAYS = (0, 3, 1, 2)


def keep_kernel(part_hbm, out_ref, sem):
    copy = pltpu.make_async_copy(part_hbm, out_ref, sem)
    copy.start()
    copy.wait()


def turn_kernel(*refs):
    for first, part_ref in zip(WAYS, refs[:4]):
        for second, out_ref in enumerate(refs[4:]):
            out_ref[first] = part_ref[second]


def partial_kernel(place_ref, *refs):
    first_refs, second_refs, (mine_ref, other_ref) = refs[:4], refs[4:8], refs[8:]
    core = place_ref[0] % 2
    per_group = TILE // TILES_BLK
    lane = lax.broadcasted_iota(jnp.int32, (INFO, TILE), 1)
    info = [first_refs[source // 4][source % 4, TILES_BLK * PIECE:] for source in range(CHIPS)]
    tables = []
    for block in range(2):
        rows = []
        for m in range(PER_TILE):
            groups = []
            for group in range(CHIPS // per_group):
                total = None
                for member in range(per_group):
                    goal = member * TILES_BLK
                    shift = (goal - (m * 2 + block) * TILES_BLK) % TILE
                    value = info[group * per_group + member]
                    value = pltpu.roll(value, shift, 1) if shift else value
                    here = (lane >= goal) & (lane < goal + TILES_BLK)
                    total = value if total is None else jnp.where(here, value, total)
                groups.append(total)
            rows.append(jnp.concatenate(groups, axis=1))
        tables.append(rows)

    targets = VISITS * OWN_DEV
    owned = targets // 2
    items = CHIPS * TILES_BLK
    row = lax.broadcasted_iota(jnp.int32, (targets, items), 0)
    side = (row // owned + core) % 2
    inner = row % owned
    wanted = ((inner // OWN_DEV) * 2 + side) * OWN_DEV + inner % OWN_DEV
    routes = []
    sums = None
    over_items = (((1,), (1,)), ((), ()))
    for block in range(2):
        target = tables[block][0][PER_TILE:PER_TILE + 1, :].astype(jnp.int32)
        route = jnp.where(wanted == target, 1.0, 0.0).astype(bf16)
        routes.append(route)
        weights = jnp.concatenate(
            tables[block] + [jnp.zeros((TILE - INFO * PER_TILE, items), f32)], axis=0
        )
        for half in split(weights):
            term = lax.dot_general(route, half, over_items, preferred_element_type=f32)
            sums = term if sums is None else sums + term
    mine_ref[owned * PIECE:, :] = sums[:owned]
    other_ref[owned * PIECE:, :] = sums[owned:]
    for line in range(PIECE):
        total = None
        rows = pl.ds(line, TILES_BLK, PIECE)
        for route, part_refs in zip(routes, (first_refs, second_refs)):
            part = jnp.concatenate(
                [part_ref[:, rows, :].reshape(items // 4, TILE) for part_ref in part_refs], axis=0
            )
            high, low = split(part)
            term = jnp.dot(
                route, jnp.concatenate([high, low], axis=1), preferred_element_type=f32
            )
            total = term if total is None else total + term
        total = total[:, :TILE] + total[:, TILE:]
        mine_ref[pl.ds(line, owned, PIECE), :] = total[:owned]
        other_ref[pl.ds(line, owned, PIECE), :] = total[owned:]


def spread_cells(sums, cell_row):
    pattern = (
        lax.broadcasted_iota(jnp.int32, (TILE, TILE), 1) // CELL + cell_row * INFO
        == lax.broadcasted_iota(jnp.int32, (TILE, TILE), 0)
    ).astype(f32)
    return jnp.dot(sums, pattern, precision=lax.Precision.HIGHEST, preferred_element_type=f32)


def merge_kernel(place_ref, mine_ref, other_ref, out_ref):
    owned = VISITS * OWN_DEV // 2
    cell_row = (place_ref[0] // 2) // (CELL // PIECE)
    sums = mine_ref[owned * PIECE:, :] + other_ref[owned * PIECE:, :]
    scale = 1.0 / (spread_cells(sums, cell_row) + prior_weight)
    total = mine_ref[:owned * PIECE, :] + other_ref[:owned * PIECE, :]
    total = total.reshape(owned, PIECE, TILE) * scale[:, None, :]
    out_ref[...] = total.reshape(owned * PIECE, TILE)


def owner_kernel(place_ref, mine_ref, other_ref, part_ref, image_ref, chi_ref):
    owned = VISITS * OWN_DEV // 2
    rows = pl.ds(pl.multiple_of(owned * PIECE + (place_ref[0] // 2) * OWN_DEV, OWN_DEV), OWN_DEV)
    sums = mine_ref[rows, :] + other_ref[rows, :]
    spread = [spread_cells(sums, cell_row) + prior_weight for cell_row in range(PER_TILE)]
    for slot in range(OWN_DEV):
        image = part_ref[:, slot * PIECE:(slot + 1) * PIECE, :].reshape(TILE, TILE)
        image_ref[slot] = image
        weight = jnp.concatenate(
            [jnp.broadcast_to(spread[m][slot:slot + 1], (CELL, TILE)) for m in range(PER_TILE)],
            axis=0,
        )
        chi_ref[slot] = image * image * weight


def local(exposures, variance, mask_planes, kernel_table, kernel_index, tile_owner, tile_slot):
    place = lax.axis_index("visit").astype(jnp.int32).reshape(1)
    smem = pl.BlockSpec(memory_space=pltpu.SMEM)
    vmem = pl.BlockSpec(memory_space=pltpu.VMEM)
    params = pltpu.CompilerParams(vmem_limit_bytes=32 << 20)
    owned = VISITS * OWN_DEV // 2

    def exchange(parts):
        for phase in range(2):
            parts = [
                lax.ppermute(parts[way], "visit", phase_partners(phase, way)) if way else parts[0]
                for way in WAYS
            ]
            if phase == 0:
                parts = pl.pallas_call(
                    turn_kernel,
                    out_shape=[jax.ShapeDtypeStruct(parts[0].shape, f32)] * 4,
                    in_specs=[vmem] * 4,
                    out_specs=[vmem] * 4,
                    compiler_params=params,
                    name="turn",
                )(*parts)
        return parts

    table = kernel_table.T
    owner = tile_owner.reshape(tile_slot.shape)
    parts = []
    for block in range(exposures.shape[1]):
        pieces = match_block(
            block, place, exposures, variance, mask_planes, table, kernel_index, owner, tile_slot
        )
        own = pl.pallas_call(
            keep_kernel,
            out_shape=jax.ShapeDtypeStruct(pieces[0].shape, f32),
            in_specs=[pl.BlockSpec(memory_space=pltpu.HBM)],
            out_specs=vmem,
            scratch_shapes=[pltpu.SemaphoreType.DMA],
            compiler_params=params,
            name="keep",
        )(pieces[0])
        parts.extend(exchange([own, *pieces[1:]]))
    parts = [part.reshape(4, -1, TILE) for part in parts]

    mine, other = pl.pallas_call(
        partial_kernel,
        out_shape=[jax.ShapeDtypeStruct((owned * (PIECE + 1), TILE), f32)] * 2,
        in_specs=[smem] + [vmem] * 8,
        out_specs=[vmem, vmem],
        compiler_params=params,
        name="partial_sums",
    )(place, *parts)
    other = lax.ppermute(other, "visit", [(device, device ^ 1) for device in range(VISITS)])
    pieces = pl.pallas_call(
        merge_kernel,
        out_shape=jax.ShapeDtypeStruct((owned * PIECE, TILE), f32),
        in_specs=[smem, vmem, vmem],
        out_specs=vmem,
        compiler_params=params,
        name="merge_cores",
    )(place, mine, other)
    pieces = lax.all_to_all(
        pieces.reshape(CHIPS, OWN_DEV * PIECE, TILE),
        "visit",
        0,
        0,
        axis_index_groups=[list(range(core, VISITS, 2)) for core in range(2)],
        tiled=True,
    )
    image, chi = pl.pallas_call(
        owner_kernel,
        out_shape=[jax.ShapeDtypeStruct((OWN_DEV, TILE, TILE), f32)] * 2,
        in_specs=[smem, vmem, vmem, vmem],
        out_specs=[vmem, vmem],
        compiler_params=params,
        name="own",
    )(place, mine, other, pieces)

    pairings = ([(0, 1), (1, 0), (2, 3), (3, 2)], [(0, 3), (3, 0), (1, 2), (2, 1)])
    halves = [chi[:OWN_DEV // 2], chi[OWN_DEV // 2:]]
    for turn in range(2):
        halves = [
            half + lax.ppermute(half, "band", pairings[(turn + number) % 2])
            for number, half in enumerate(halves)
        ]
    return image[None], jnp.concatenate(halves, axis=0)


def solution(mesh):
    placed = (
        P("band", "visit", None, None),
        P("band", "visit", None, None),
        P("band", "visit", None, None),
        P(),
        P("band", "visit"),
        P("band", "visit", None),
        P("band", "visit"),
    )
    return jax.shard_map(
        local,
        mesh=mesh,
        in_specs=placed,
        out_specs=(P("band", "visit", None, None), P("visit", None, None)),
        check_vma=False,
    )
```

```python
import functools

import jax
import jax.numpy as jnp
import numpy as np
from jax import lax
from jax.experimental import pallas as pl
from jax.experimental.pallas import tpu as pltpu
from jax.sharding import PartitionSpec as P

BLOCK = 512
TILE = 128
CELL = 32
KSIZE = 41
OWN_DEV = 8
PADDED = BLOCK + KSIZE - 1
WIDE = 640
NFILT = 11
VISITS = 32
SIDE = BLOCK // TILE
CELLS = BLOCK // CELL
PER_TILE = TILE // CELL
TILES_BLK = SIDE * SIDE
CHIPS = VISITS // 2
PIECE = TILE // CHIPS
INFO = 8
SPAN = TILE + KSIZE - 1
HALF = SPAN // 2
TALL = 560
TAPS = 48

width_fractions = (0.075, 0.15, 0.3)
family_degrees = (4, 2, 2)
prior_weight = 0.05
reject_planes = 3

f32 = jnp.float32
bf16 = jnp.bfloat16


def as_halves(matrix):
    high = matrix.astype(np.float32).astype(bf16)
    low = (matrix - high.astype(np.float64)).astype(np.float32).astype(bf16)
    return high, low


def transforms():
    number = np.arange(HALF)
    angle = 2 * np.pi * (number + 0.5) / SPAN
    taps = np.arange(SPAN)
    cosine, sine = np.cos(angle[:, None] * taps), np.sin(angle[:, None] * taps)
    spot = 8 * (number // 4) + number % 4

    by_row = np.zeros((SPAN, SPAN))
    by_row[spot], by_row[spot + 4] = cosine, sine
    by_lane = np.zeros((2 * TILE, SPAN))
    by_lane[:HALF], by_lane[TILE:TILE + HALF] = cosine, sine

    across = np.zeros((2 * TILE, 2 * TILE))
    across[:SPAN] = by_lane.T
    down = np.zeros((SPAN + 8, SPAN))
    down[:SPAN] = by_row
    back_down = by_row.T[:TILE] * (2 / SPAN)
    back_across = by_lane[:, :TILE] * (2 / SPAN)

    def three(matrix, width=512):
        high, low = as_halves(matrix)
        rest = np.zeros((matrix.shape[0], width - 3 * matrix.shape[1]), bf16)
        return np.concatenate([high, high, low, rest], axis=1)

    same = np.zeros((SPAN + 8, TAPS))
    cross = np.zeros((SPAN + 8, TAPS))
    same[spot, :KSIZE] = same[spot + 4, :KSIZE] = cosine[:, :KSIZE]
    cross[spot, :KSIZE], cross[spot + 4, :KSIZE] = sine[:, :KSIZE], -sine[:, :KSIZE]
    along = np.zeros((TILE, 2 * TILE), np.float32)
    along[:KSIZE, :HALF], along[:KSIZE, TILE:TILE + HALF] = cosine[:, :KSIZE].T, -sine[:, :KSIZE].T
    return (
        np.concatenate(as_halves(across), axis=0),
        three(down),
        three(back_down),
        np.concatenate(as_halves(back_across), axis=1),
        np.concatenate([three(same, 256), three(cross, 256)], axis=0),
        along,
    )


def filter_terms():
    starts = (0, 5, 8)
    terms = []
    for family in range(3):
        for first in range(family_degrees[family] + 1):
            for second in range(family_degrees[family] + 1 - first):
                terms.append((starts[family] + first, starts[family] + second))
    return terms


def profiles_at(offset):
    half_width = (KSIZE - 1) // 2
    inside = (offset >= 0) & (offset < KSIZE)
    taps = offset.astype(f32) - half_width
    values = []
    for family in range(3):
        scaled = taps / (width_fractions[family] * half_width)
        value = jnp.where(inside, jnp.exp(-0.5 * scaled * scaled), 0.0)
        for degree in range(family_degrees[family] + 1):
            values.append(value)
            value = value * scaled
    return values


def split(value):
    high = value.astype(bf16)
    return high, (value - high.astype(f32)).astype(bf16)


def cell_weights(variance, bits):
    usable = (jnp.bitwise_and(bits, reject_planes) != reject_planes).astype(f32)
    return usable / variance


def item_info(var_ref, bits_ref, owner_ref, slot_ref):
    exact = lax.Precision.HIGHEST
    lane = lax.broadcasted_iota(jnp.int32, (1, TILE), 1)
    row = lax.broadcasted_iota(jnp.int32, (CELLS, TILE), 0)
    item = lane % TILES_BLK
    cell_row = (item // SIDE) * PER_TILE + lane // (2 * TILES_BLK)
    columns = None
    for block in range(2):
        picked = ((row == cell_row) & ((lane // TILES_BLK) % 2 == block)).astype(f32)
        term = lax.dot_general(
            cell_weights(var_ref[block], bits_ref[block]), picked,
            (((0,), (0,)), ((), ())), precision=exact, preferred_element_type=f32,
        )
        columns = term if columns is None else columns + term
    rows = []
    for n in range(PER_TILE):
        chosen = row == (item % SIDE) * PER_TILE + n
        rows.append(jnp.sum(jnp.where(chosen, columns, 0.0), axis=0, keepdims=True))
    target = (owner_ref[...] * OWN_DEV + slot_ref[...]).astype(f32)
    rows.append(jnp.concatenate([target, jnp.zeros((1, TILE - 2 * TILES_BLK), f32)], axis=1))
    rows.append(jnp.zeros((INFO - PER_TILE - 1, TILE), f32))
    return jnp.concatenate(rows, axis=0)


def phase_masks(core):
    return (1, 3) if core == 0 else (3, 1)


def way_to(place, piece):
    core, offset = place % 2, jnp.bitwise_xor(place // 2, piece)
    first, second = 0, 0
    for coordinate in (offset // 4, offset % 4):
        high = coordinate // 2
        both = jnp.bitwise_xor(high, coordinate % 2)
        first = 2 * first + jnp.where(core == 0, both, high)
        second = 2 * second + jnp.where(core == 0, high, both)
    return 4 * first + second


def phase_partners(phase, way):
    partners = []
    for device in range(VISITS):
        mask = phase_masks(device % 2)[phase]
        partners.append((device, device ^ (2 * (4 * mask * (way // 2) + mask * (way % 2)))))
    return partners


def exact_dot(left, right, sides=((1,), (0,))):
    return lax.dot_general(
        left, right, (sides, ((), ())), precision=lax.Precision.HIGHEST, preferred_element_type=f32
    )


def stacked_halves(value):
    high = value.astype(bf16).astype(f32)
    return jnp.concatenate([high, value - high], axis=0).astype(bf16)


def against_halves(matrix, halves_ref):
    rows = jnp.concatenate([halves_ref[...], halves_ref[:SPAN + 8, :]], axis=0)
    return jnp.dot(matrix, rows, preferred_element_type=f32)


def filter_bank():
    taps = lax.broadcasted_iota(jnp.int32, (1, TILE), 1)
    values = profiles_at(taps)
    norms = [jnp.sqrt(jnp.sum(value * value, axis=1, keepdims=True)) for value in values]
    rows = [value / norm for value, norm in zip(values, norms)]
    wide = jnp.concatenate(rows + [jnp.zeros((16 - NFILT, TILE), f32)], axis=0)
    lane = lax.broadcasted_iota(jnp.int32, (TAPS, TILE), 1)
    tall = jnp.zeros((TAPS, TILE), f32)
    for number, (value, norm) in enumerate(
        zip(profiles_at(lax.broadcasted_iota(jnp.int32, (TAPS, TILE), 0)), norms)
    ):
        tall = jnp.where(lane == number, value / norm, tall)
    return wide, tall


def kernel_spectrum(filters, which, table_ref, down_taps_ref, along_ref):
    first = lax.broadcasted_iota(jnp.int32, (16, 16), 0)
    second = lax.broadcasted_iota(jnp.int32, (16, 16), 1)
    mixing = jnp.zeros((16, 16), f32)
    for number, (p, q) in enumerate(filter_terms()):
        mixing = jnp.where((first == p) & (second == q), table_ref[number, which], mixing)
    wide, tall = filters
    across = exact_dot(mixing, exact_dot(wide, along_ref[...]))
    across = jnp.concatenate([across, jnp.zeros((TILE - 16, 2 * TILE), f32)], axis=0)
    mixed = exact_dot(tall, across)
    high = mixed.astype(bf16).astype(f32)
    rest = jnp.zeros((256 - 3 * TAPS, 2 * TILE), f32)
    mixed = jnp.concatenate([high, mixed - high, high, rest], axis=0).astype(bf16)
    both = jnp.dot(down_taps_ref[...], mixed, preferred_element_type=f32)
    return both[:SPAN], both[SPAN + 8:2 * SPAN + 8]


def match_kernel(
    place_ref, index_hbm, table_hbm, image_hbm, var_hbm, bits_hbm, owner_hbm, slot_hbm,
    across_hbm, down_hbm, back_down_hbm, back_across_hbm, down_taps_hbm, along_hbm,
    *rest, block,
):
    count = 4 if block == 0 else 1
    outs = rest[:count]
    (
        index_ref, table_ref, image_ref, var_ref, bits_ref, owner_ref, slot_ref,
        across_ref, down_ref, back_down_ref, back_across_ref, down_taps_ref, along_ref, sems,
        out_sems, tail_ref, high_ref, low_ref, wave_ref, stack_ref, turn_ref, result_ref, rows_ref,
        factor_ref, weight_ref, out_ref,
    ) = rest[count:]
    copies = [
        pltpu.make_async_copy(source, goal, sems.at[number])
        for number, (source, goal) in enumerate((
            (index_hbm, index_ref),
            (table_hbm, table_ref),
            (down_taps_hbm, down_taps_ref),
            (along_hbm, along_ref),
            (image_hbm.at[0, block], image_ref),
            (across_hbm, across_ref),
            (var_hbm.at[0], var_ref),
            (bits_hbm.at[0], bits_ref),
            (owner_hbm, owner_ref),
            (slot_hbm, slot_ref),
            (down_hbm, down_ref),
            (back_down_hbm, back_down_ref),
            (back_across_hbm, back_across_ref),
        ))
    ]
    for copy in copies:
        copy.start()
    tail_ref[...] = jnp.zeros_like(tail_ref)
    filters = filter_bank()
    spread = (
        lax.broadcasted_iota(jnp.int32, (CELLS, BLOCK), 1) // CELL
        == lax.broadcasted_iota(jnp.int32, (CELLS, BLOCK), 0)
    ).astype(f32)
    for copy in copies:
        copy.wait()

    pair = 2 * TILE
    forward = jnp.concatenate([across_ref[:pair], across_ref[...]], axis=0)
    backward = jnp.concatenate([back_across_ref[...], back_across_ref[...]], axis=0)
    spots = range(CHIPS)
    if block == 0:
        spots = [way_to(place_ref[0], piece) for piece in range(CHIPS)]

    def halve():
        tail_ref[:PADDED, :PADDED - BLOCK] = image_ref[:, BLOCK:]
        whole = TALL - 16
        for first, width, source in ((0, BLOCK, image_ref), (BLOCK, TILE, tail_ref)):
            lanes = slice(first, first + width)
            high_ref[:whole, lanes], low_ref[:whole, lanes] = split(source[:whole, :width])
            last = jnp.concatenate(
                [source[whole:PADDED, :width], jnp.zeros((8, width), f32)], axis=0
            )
            high_ref[whole:, lanes], low_ref[whole:, lanes] = split(last)

    def transform_across(column):
        lanes = slice(column * TILE, column * TILE + pair)
        high, low = high_ref[:, lanes], low_ref[:, lanes]
        wave_ref[column] = jnp.dot(
            jnp.concatenate([high, low, high], axis=1), forward, preferred_element_type=f32
        )

    def prepare():
        same, cross = kernel_spectrum(
            filters, index_ref[0, block], table_ref, down_taps_ref, along_ref
        )
        factor_ref[0] = same.reshape(SPAN // 8, 8, pair)
        factor_ref[1] = cross.reshape(SPAN // 8, 8, pair)
        weight_ref[...] = exact_dot(cell_weights(var_ref[block], bits_ref[block]), spread)
        info = item_info(var_ref, bits_ref, owner_ref, slot_ref)
        out_ref[:, TILES_BLK] = jnp.broadcast_to(info[None], (CHIPS, INFO, TILE))

    def stack(tile):
        column, line = divmod(tile, SIDE)
        stack_ref[tile] = stacked_halves(wave_ref[column, line * TILE:line * TILE + SPAN, :])

    def transform_down(tile):
        turn_ref[tile] = against_halves(down_ref[...], stack_ref.at[tile])

    def multiply(tile):
        wave = turn_ref[tile, :SPAN].reshape(SPAN // 8, 8, pair)
        turned = pltpu.roll(wave, 4, 1)
        wave_c, wave_s = wave[..., :TILE], wave[..., TILE:]
        turned_c, turned_s = turned[..., :TILE], turned[..., TILE:]
        same_c, same_s = factor_ref[0, :, :, :TILE], factor_ref[0, :, :, TILE:]
        cross_c, cross_s = factor_ref[1, :, :, :TILE], factor_ref[1, :, :, TILE:]
        result_c = wave_c * same_c + turned_c * cross_c - wave_s * same_s - turned_s * cross_s
        result_s = wave_s * same_c + turned_s * cross_c + wave_c * same_s + turned_c * cross_s
        result = jnp.concatenate(
            [result_c.reshape(SPAN, TILE), result_s.reshape(SPAN, TILE)], axis=1
        )
        result_ref[tile] = stacked_halves(result)

    def back_down(tile):
        column, line = divmod(tile, SIDE)
        high, low = split(against_halves(back_down_ref[...], result_ref.at[tile]))
        rows_ref[column, line * TILE:(line + 1) * TILE, :pair] = high
        rows_ref[column, line * TILE:(line + 1) * TILE, pair:] = low

    def back_across(column):
        matched = jnp.dot(rows_ref[column], backward, preferred_element_type=f32)
        matched = matched[:, :TILE] + matched[:, TILE:]
        weight = weight_ref[:, column * TILE:(column + 1) * TILE]
        weighted = matched.reshape(CELLS, CELL, TILE) * weight[:, None, :]
        weighted = weighted.reshape(SIDE, CHIPS, PIECE, TILE)
        for line in range(SIDE):
            item = line * SIDE + column
            for piece in range(CHIPS):
                out_ref[spots[piece], item] = weighted[line, piece]

    halve()
    transform_across(0)
    prepare()
    for step in range(TILES_BLK + 5):
        if step % SIDE == 0 and step // SIDE + 1 < SIDE:
            transform_across(step // SIDE + 1)
        for delay, stage in enumerate((stack, transform_down, multiply, back_down)):
            if 0 <= step - delay < TILES_BLK:
                stage(step - delay)
        column, rest = divmod(step - 4, SIDE)
        if rest == SIDE - 1 and 0 <= column < SIDE:
            back_across(column)
    each = CHIPS // count
    sends = [
        pltpu.make_async_copy(out_ref.at[way * each:(way + 1) * each], out_hbm, out_sems.at[way])
        for way, out_hbm in enumerate(outs)
    ]
    for send in reversed(sends):
        send.start()
    for send in sends:
        send.wait()


def match_block(block, place, exposures, variance, bits, table, index, owner, slot):
    blocks = exposures.shape[1]
    items = blocks * TILES_BLK
    groups = TILES_BLK + 1
    count = 4 if block == 0 else 1
    matrices = transforms()
    return pl.pallas_call(
        functools.partial(match_kernel, block=block),
        out_shape=[jax.ShapeDtypeStruct((CHIPS // count, groups, PIECE, TILE), f32)] * count,
        in_specs=[pl.BlockSpec(memory_space=pltpu.SMEM)]
        + [pl.BlockSpec(memory_space=pltpu.HBM)] * (7 + len(matrices)),
        out_specs=[pl.BlockSpec(memory_space=pltpu.HBM)] * count,
        scratch_shapes=[
            pltpu.SMEM((1, blocks), jnp.int32),
            pltpu.SMEM(table.shape, f32),
            pltpu.VMEM((PADDED, PADDED), f32),
            pltpu.VMEM((blocks, CELLS, CELLS), f32),
            pltpu.VMEM((blocks, CELLS, CELLS), jnp.int32),
            pltpu.VMEM((1, items), jnp.int32),
            pltpu.VMEM((1, items), jnp.int32),
            *[pltpu.VMEM(matrix.shape, matrix.dtype) for matrix in matrices],
            pltpu.SemaphoreType.DMA((7 + len(matrices),)),
            pltpu.SemaphoreType.DMA((4,)),
            pltpu.VMEM((TALL, TILE), f32),
            pltpu.VMEM((TALL, WIDE), bf16),
            pltpu.VMEM((TALL, WIDE), bf16),
            pltpu.VMEM((SIDE, TALL, 2 * TILE), f32),
            pltpu.VMEM((TILES_BLK, 2 * SPAN, 2 * TILE), bf16),
            pltpu.VMEM((TILES_BLK, SPAN + 8, 2 * TILE), f32),
            pltpu.VMEM((TILES_BLK, 2 * SPAN, 2 * TILE), bf16),
            pltpu.VMEM((SIDE, BLOCK, 4 * TILE), bf16),
            pltpu.VMEM((2, SPAN // 8, 8, 2 * TILE), f32),
            pltpu.VMEM((CELLS, BLOCK), f32),
            pltpu.VMEM((CHIPS, groups, PIECE, TILE), f32),
        ],
        compiler_params=pltpu.CompilerParams(vmem_limit_bytes=59 << 20),
        cost_estimate=pl.CostEstimate(
            flops=2 * 256 * 256 * 40000, bytes_accessed=3 << 20, transcendentals=0
        ),
        name="match_block",
    )(place, index, table, exposures, variance, bits, owner, slot, *matrices)


WAYS = (0, 3, 1, 2)


def keep_kernel(part_hbm, out_ref, sem):
    copy = pltpu.make_async_copy(part_hbm, out_ref, sem)
    copy.start()
    copy.wait()


def turn_kernel(*refs):
    for first, part_ref in zip(WAYS, refs[:4]):
        for second, out_ref in enumerate(refs[4:]):
            out_ref[first] = part_ref[second]


def partial_kernel(place_ref, *refs):
    first_refs, second_ref, mine_ref, other_ref = refs[:4], *refs[4:]
    core = place_ref[0] % 2
    per_group = TILE // TILES_BLK
    lane = lax.broadcasted_iota(jnp.int32, (INFO, TILE), 1)
    infos = (
        [first_refs[source // 4][source % 4, TILES_BLK * PIECE:, :] for source in range(CHIPS)],
        [second_ref[source, TILES_BLK * PIECE:, :] for source in range(CHIPS)],
    )
    tables = []
    for block, info in enumerate(infos):
        rows = []
        for m in range(PER_TILE):
            groups = []
            for group in range(CHIPS // per_group):
                total = None
                for member in range(per_group):
                    goal = member * TILES_BLK
                    shift = (goal - (m * 2 + block) * TILES_BLK) % TILE
                    value = info[group * per_group + member]
                    value = pltpu.roll(value, shift, 1) if shift else value
                    here = (lane >= goal) & (lane < goal + TILES_BLK)
                    total = value if total is None else jnp.where(here, value, total)
                groups.append(total)
            rows.append(jnp.concatenate(groups, axis=1))
        tables.append(rows)

    targets = VISITS * OWN_DEV
    owned = targets // 2
    items = CHIPS * TILES_BLK
    row = lax.broadcasted_iota(jnp.int32, (targets, items), 0)
    side = (row // owned + core) % 2
    inner = row % owned
    wanted = ((inner // OWN_DEV) * 2 + side) * OWN_DEV + inner % OWN_DEV
    routes = []
    sums = None
    over_items = (((1,), (1,)), ((), ()))
    for block in range(2):
        target = tables[block][0][PER_TILE:PER_TILE + 1, :].astype(jnp.int32)
        route = jnp.where(wanted == target, 1.0, 0.0).astype(bf16)
        routes.append(route)
        weights = jnp.concatenate(
            tables[block] + [jnp.zeros((TILE - INFO * PER_TILE, items), f32)], axis=0
        )
        for half in split(weights):
            term = lax.dot_general(route, half, over_items, preferred_element_type=f32)
            sums = term if sums is None else sums + term
    mine_ref[owned * PIECE:, :] = sums[:owned]
    other_ref[owned * PIECE:, :] = sums[owned:]
    for line in range(PIECE):
        total = None
        rows = pl.ds(line, TILES_BLK, PIECE)
        for route, part_refs in zip(routes, (first_refs, (second_ref,))):
            part = jnp.concatenate(
                [part_ref[:, rows, :].reshape(-1, TILE) for part_ref in part_refs], axis=0
            )
            high, low = split(part)
            term = jnp.dot(
                route, jnp.concatenate([high, low], axis=1), preferred_element_type=f32
            )
            total = term if total is None else total + term
        total = total[:, :TILE] + total[:, TILE:]
        mine_ref[pl.ds(line, owned, PIECE), :] = total[:owned]
        other_ref[pl.ds(line, owned, PIECE), :] = total[owned:]


def spread_cells(sums, cell_row):
    pattern = (
        lax.broadcasted_iota(jnp.int32, (TILE, TILE), 1) // CELL + cell_row * INFO
        == lax.broadcasted_iota(jnp.int32, (TILE, TILE), 0)
    ).astype(f32)
    return jnp.dot(sums, pattern, precision=lax.Precision.HIGHEST, preferred_element_type=f32)


def merge_kernel(place_ref, mine_ref, other_ref, out_ref):
    owned = VISITS * OWN_DEV // 2
    cell_row = (place_ref[0] // 2) // (CELL // PIECE)
    sums = mine_ref[owned * PIECE:, :] + other_ref[owned * PIECE:, :]
    scale = 1.0 / (spread_cells(sums, cell_row) + prior_weight)
    total = mine_ref[:owned * PIECE, :] + other_ref[:owned * PIECE, :]
    total = total.reshape(owned, PIECE, TILE) * scale[:, None, :]
    out_ref[...] = total.reshape(owned * PIECE, TILE)


def chi_kernel(place_ref, mine_ref, other_ref, part_ref, upper_ref, lower_ref):
    owned = VISITS * OWN_DEV // 2
    first = owned * PIECE + (place_ref[0] // 2) * OWN_DEV
    rows = pl.ds(pl.multiple_of(first, OWN_DEV), OWN_DEV)
    sums = mine_ref[rows, :] + other_ref[rows, :]
    per_cell = CELL // PIECE
    for m in range(PER_TILE):
        weight = spread_cells(sums, m) + prior_weight
        weight = jnp.broadcast_to(weight[:, None, :], (OWN_DEV, PIECE, TILE))
        part = part_ref[m * per_cell:(m + 1) * per_cell]
        chi_ref = upper_ref if m < PER_TILE // 2 else lower_ref
        place = m % (PER_TILE // 2) * per_cell
        chi_ref[place:place + per_cell] = part * part * weight.reshape(1, OWN_DEV * PIECE, TILE)


def image_kernel(part_ref, image_ref):
    for slot in range(OWN_DEV):
        rows = slice(slot * PIECE, (slot + 1) * PIECE)
        image_ref[slot] = part_ref[:, rows, :].reshape(TILE, TILE)


def detection_kernel(upper_ref, more_upper_ref, lower_ref, more_lower_ref, out_ref):
    for slot in range(OWN_DEV):
        rows = slice(slot * PIECE, (slot + 1) * PIECE)
        upper = upper_ref[:, rows, :] + more_upper_ref[:, rows, :]
        lower = lower_ref[:, rows, :] + more_lower_ref[:, rows, :]
        out_ref[slot, :TILE // 2] = upper.reshape(TILE // 2, TILE)
        out_ref[slot, TILE // 2:] = lower.reshape(TILE // 2, TILE)


def local(exposures, variance, mask_planes, kernel_table, kernel_index, tile_owner, tile_slot):
    place = lax.axis_index("visit").astype(jnp.int32).reshape(1)
    smem = pl.BlockSpec(memory_space=pltpu.SMEM)
    vmem = pl.BlockSpec(memory_space=pltpu.VMEM)
    params = pltpu.CompilerParams(vmem_limit_bytes=32 << 20)
    owned = VISITS * OWN_DEV // 2

    def exchange(parts):
        for phase in range(2):
            parts = [
                lax.ppermute(parts[way], "visit", phase_partners(phase, way)) if way else parts[0]
                for way in WAYS
            ]
            if phase == 0:
                parts = pl.pallas_call(
                    turn_kernel,
                    out_shape=[jax.ShapeDtypeStruct(parts[0].shape, f32)] * 4,
                    in_specs=[vmem] * 4,
                    out_specs=[vmem] * 4,
                    compiler_params=params,
                    name="turn",
                )(*parts)
        return parts

    table = kernel_table.T
    owner = tile_owner.reshape(tile_slot.shape)
    def spread_tiles(pieces):
        return lax.all_to_all(pieces, "visit", 0, 0, axis_index_groups=same_core, tiled=True)

    same_core = [list(range(core, VISITS, 2)) for core in range(2)]
    operands = (place, exposures, variance, mask_planes, table, kernel_index, owner, tile_slot)
    pieces = match_block(0, *operands)
    own = pl.pallas_call(
        keep_kernel,
        out_shape=jax.ShapeDtypeStruct(pieces[0].shape, f32),
        in_specs=[pl.BlockSpec(memory_space=pltpu.HBM)],
        out_specs=vmem,
        scratch_shapes=[pltpu.SemaphoreType.DMA],
        compiler_params=params,
        name="keep",
    )(pieces[0])
    parts = [part.reshape(4, -1, TILE) for part in exchange([own, *pieces[1:]])]
    (pieces,) = match_block(1, *operands)
    parts.append(spread_tiles(pieces.reshape(CHIPS, -1, TILE)))

    mine, other = pl.pallas_call(
        partial_kernel,
        out_shape=[jax.ShapeDtypeStruct((owned * (PIECE + 1), TILE), f32)] * 2,
        in_specs=[smem] + [vmem] * 5,
        out_specs=[vmem, vmem],
        compiler_params=params,
        name="partial_sums",
    )(place, *parts)
    other = lax.ppermute(other, "visit", [(device, device ^ 1) for device in range(VISITS)])
    pieces = pl.pallas_call(
        merge_kernel,
        out_shape=jax.ShapeDtypeStruct((owned * PIECE, TILE), f32),
        in_specs=[smem, vmem, vmem],
        out_specs=vmem,
        compiler_params=params,
        name="merge_cores",
    )(place, mine, other)
    pieces = spread_tiles(pieces.reshape(CHIPS, OWN_DEV * PIECE, TILE))
    halves = pl.pallas_call(
        chi_kernel,
        out_shape=[jax.ShapeDtypeStruct((CHIPS // 2, OWN_DEV * PIECE, TILE), f32)] * 2,
        in_specs=[smem, vmem, vmem, vmem],
        out_specs=[vmem, vmem],
        compiler_params=params,
        name="chi",
    )(place, mine, other, pieces)
    tiles = jax.ShapeDtypeStruct((OWN_DEV, TILE, TILE), f32)
    image = pl.pallas_call(
        image_kernel,
        out_shape=tiles,
        in_specs=[vmem],
        out_specs=vmem,
        compiler_params=params,
        name="image",
    )(pieces)

    pairings = ([(0, 1), (1, 0), (2, 3), (3, 2)], [(0, 3), (3, 0), (1, 2), (2, 1)])
    halves = [
        half + lax.ppermute(half, "band", pairings[number]) for number, half in enumerate(halves)
    ]
    terms = []
    for number, half in enumerate(halves):
        terms.extend((half, lax.ppermute(half, "band", pairings[1 - number])))
    detection = pl.pallas_call(
        detection_kernel,
        out_shape=tiles,
        in_specs=[vmem] * 4,
        out_specs=vmem,
        compiler_params=params,
        name="detection",
    )(*terms)
    return image[None], detection


def solution(mesh):
    placed = (
        P("band", "visit", None, None),
        P("band", "visit", None, None),
        P("band", "visit", None, None),
        P(),
        P("band", "visit"),
        P("band", "visit", None),
        P("band", "visit"),
    )
    return jax.shard_map(
        local,
        mesh=mesh,
        in_specs=placed,
        out_specs=(P("band", "visit", None, None), P("visit", None, None)),
        check_vma=False,
    )
```

```python
import functools

import jax
import jax.numpy as jnp
import numpy as np
from jax import lax
from jax.experimental import pallas as pl
from jax.experimental.pallas import tpu as pltpu
from jax.sharding import PartitionSpec as P

BLOCK = 512
TILE = 128
CELL = 32
KSIZE = 41
OWN_DEV = 8
PADDED = BLOCK + KSIZE - 1
WIDE = 640
NFILT = 11
VISITS = 32
SIDE = BLOCK // TILE
CELLS = BLOCK // CELL
PER_TILE = TILE // CELL
TILES_BLK = SIDE * SIDE
CHIPS = VISITS // 2
PIECE = TILE // CHIPS
INFO = 8
SPAN = TILE + KSIZE - 1
HALF = SPAN // 2
TALL = 560
TAPS = 48

width_fractions = (0.075, 0.15, 0.3)
family_degrees = (4, 2, 2)
prior_weight = 0.05
reject_planes = 3

f32 = jnp.float32
bf16 = jnp.bfloat16


def as_halves(matrix):
    high = matrix.astype(np.float32).astype(bf16)
    low = (matrix - high.astype(np.float64)).astype(np.float32).astype(bf16)
    return high, low


def transforms():
    number = np.arange(HALF)
    angle = 2 * np.pi * (number + 0.5) / SPAN
    taps = np.arange(SPAN)
    cosine, sine = np.cos(angle[:, None] * taps), np.sin(angle[:, None] * taps)
    spot = 8 * (number // 4) + number % 4

    by_row = np.zeros((SPAN, SPAN))
    by_row[spot], by_row[spot + 4] = cosine, sine
    by_lane = np.zeros((2 * TILE, SPAN))
    by_lane[:HALF], by_lane[TILE:TILE + HALF] = cosine, sine

    across = np.zeros((2 * TILE, 2 * TILE))
    across[:SPAN] = by_lane.T
    down = np.zeros((SPAN + 8, SPAN))
    down[:SPAN] = by_row
    back_down = by_row.T[:TILE] * (2 / SPAN)
    back_across = by_lane[:, :TILE] * (2 / SPAN)

    def three(matrix, width=512):
        high, low = as_halves(matrix)
        rest = np.zeros((matrix.shape[0], width - 3 * matrix.shape[1]), bf16)
        return np.concatenate([high, high, low, rest], axis=1)

    same = np.zeros((SPAN + 8, TAPS))
    cross = np.zeros((SPAN + 8, TAPS))
    same[spot, :KSIZE] = same[spot + 4, :KSIZE] = cosine[:, :KSIZE]
    cross[spot, :KSIZE], cross[spot + 4, :KSIZE] = sine[:, :KSIZE], -sine[:, :KSIZE]
    along = np.zeros((TILE, 2 * TILE), np.float32)
    along[:KSIZE, :HALF], along[:KSIZE, TILE:TILE + HALF] = cosine[:, :KSIZE].T, -sine[:, :KSIZE].T
    return (
        np.concatenate(as_halves(across), axis=0),
        three(down),
        three(back_down),
        np.concatenate(as_halves(back_across), axis=1),
        np.concatenate([three(same, 256), three(cross, 256)], axis=0),
        along,
    )


def filter_terms():
    starts = (0, 5, 8)
    terms = []
    for family in range(3):
        for first in range(family_degrees[family] + 1):
            for second in range(family_degrees[family] + 1 - first):
                terms.append((starts[family] + first, starts[family] + second))
    return terms


def profiles_at(offset):
    half_width = (KSIZE - 1) // 2
    inside = (offset >= 0) & (offset < KSIZE)
    taps = offset.astype(f32) - half_width
    values = []
    for family in range(3):
        scaled = taps / (width_fractions[family] * half_width)
        value = jnp.where(inside, jnp.exp(-0.5 * scaled * scaled), 0.0)
        for degree in range(family_degrees[family] + 1):
            values.append(value)
            value = value * scaled
    return values


def split(value):
    high = value.astype(bf16)
    return high, (value - high.astype(f32)).astype(bf16)


def cell_weights(variance, bits):
    usable = (jnp.bitwise_and(bits, reject_planes) != reject_planes).astype(f32)
    return usable / variance


def item_info(var_ref, bits_ref, owner_ref, slot_ref):
    exact = lax.Precision.HIGHEST
    lane = lax.broadcasted_iota(jnp.int32, (1, TILE), 1)
    row = lax.broadcasted_iota(jnp.int32, (CELLS, TILE), 0)
    item = lane % TILES_BLK
    cell_row = (item // SIDE) * PER_TILE + lane // (2 * TILES_BLK)
    columns = None
    for block in range(2):
        picked = ((row == cell_row) & ((lane // TILES_BLK) % 2 == block)).astype(f32)
        term = lax.dot_general(
            cell_weights(var_ref[block], bits_ref[block]), picked,
            (((0,), (0,)), ((), ())), precision=exact, preferred_element_type=f32,
        )
        columns = term if columns is None else columns + term
    rows = []
    for n in range(PER_TILE):
        chosen = row == (item % SIDE) * PER_TILE + n
        rows.append(jnp.sum(jnp.where(chosen, columns, 0.0), axis=0, keepdims=True))
    target = (owner_ref[...] * OWN_DEV + slot_ref[...]).astype(f32)
    rows.append(jnp.concatenate([target, jnp.zeros((1, TILE - 2 * TILES_BLK), f32)], axis=1))
    rows.append(jnp.zeros((INFO - PER_TILE - 1, TILE), f32))
    return jnp.concatenate(rows, axis=0)


def phase_masks(core):
    return (1, 3) if core == 0 else (3, 1)


def way_to(place, piece):
    core, offset = place % 2, jnp.bitwise_xor(place // 2, piece)
    first, second = 0, 0
    for coordinate in (offset // 4, offset % 4):
        high = coordinate // 2
        both = jnp.bitwise_xor(high, coordinate % 2)
        first = 2 * first + jnp.where(core == 0, both, high)
        second = 2 * second + jnp.where(core == 0, high, both)
    return 4 * first + second


def phase_partners(phase, way):
    partners = []
    for device in range(VISITS):
        mask = phase_masks(device % 2)[phase]
        partners.append((device, device ^ (2 * (4 * mask * (way // 2) + mask * (way % 2)))))
    return partners


def exact_dot(left, right, sides=((1,), (0,))):
    return lax.dot_general(
        left, right, (sides, ((), ())), precision=lax.Precision.HIGHEST, preferred_element_type=f32
    )


def stacked_halves(value):
    high = value.astype(bf16).astype(f32)
    return jnp.concatenate([high, value - high], axis=0).astype(bf16)


def against_halves(matrix, halves_ref):
    rows = jnp.concatenate([halves_ref[...], halves_ref[:SPAN + 8, :]], axis=0)
    return jnp.dot(matrix, rows, preferred_element_type=f32)


def filter_bank():
    taps = lax.broadcasted_iota(jnp.int32, (1, TILE), 1)
    values = profiles_at(taps)
    norms = [jnp.sqrt(jnp.sum(value * value, axis=1, keepdims=True)) for value in values]
    rows = [value / norm for value, norm in zip(values, norms)]
    wide = jnp.concatenate(rows + [jnp.zeros((16 - NFILT, TILE), f32)], axis=0)
    lane = lax.broadcasted_iota(jnp.int32, (TAPS, TILE), 1)
    tall = jnp.zeros((TAPS, TILE), f32)
    for number, (value, norm) in enumerate(
        zip(profiles_at(lax.broadcasted_iota(jnp.int32, (TAPS, TILE), 0)), norms)
    ):
        tall = jnp.where(lane == number, value / norm, tall)
    return wide, tall


def kernel_spectrum(filters, which, table_ref, down_taps_ref, along_ref):
    first = lax.broadcasted_iota(jnp.int32, (16, 16), 0)
    second = lax.broadcasted_iota(jnp.int32, (16, 16), 1)
    mixing = jnp.zeros((16, 16), f32)
    for number, (p, q) in enumerate(filter_terms()):
        mixing = jnp.where((first == p) & (second == q), table_ref[number, which], mixing)
    wide, tall = filters
    across = exact_dot(mixing, exact_dot(wide, along_ref[...]))
    across = jnp.concatenate([across, jnp.zeros((TILE - 16, 2 * TILE), f32)], axis=0)
    mixed = exact_dot(tall, across)
    high = mixed.astype(bf16).astype(f32)
    rest = jnp.zeros((256 - 3 * TAPS, 2 * TILE), f32)
    mixed = jnp.concatenate([high, mixed - high, high, rest], axis=0).astype(bf16)
    both = jnp.dot(down_taps_ref[...], mixed, preferred_element_type=f32)
    return both[:SPAN], both[SPAN + 8:2 * SPAN + 8]


def match_kernel(
    place_ref, index_hbm, table_hbm, image_hbm, var_hbm, bits_hbm, owner_hbm, slot_hbm,
    across_hbm, down_hbm, back_down_hbm, back_across_hbm, down_taps_hbm, along_hbm,
    *rest, block,
):
    count = 4
    outs = rest[:count]
    (
        index_ref, table_ref, image_ref, var_ref, bits_ref, owner_ref, slot_ref,
        across_ref, down_ref, back_down_ref, back_across_ref, down_taps_ref, along_ref, sems,
        out_sems, tail_ref, high_ref, low_ref, wave_ref, stack_ref, turn_ref, result_ref, rows_ref,
        factor_ref, weight_ref, out_ref,
    ) = rest[count:]
    copies = [
        pltpu.make_async_copy(source, goal, sems.at[number])
        for number, (source, goal) in enumerate((
            (index_hbm, index_ref),
            (table_hbm, table_ref),
            (down_taps_hbm, down_taps_ref),
            (along_hbm, along_ref),
            (image_hbm.at[0, block], image_ref),
            (across_hbm, across_ref),
            (var_hbm.at[0], var_ref),
            (bits_hbm.at[0], bits_ref),
            (owner_hbm, owner_ref),
            (slot_hbm, slot_ref),
            (down_hbm, down_ref),
            (back_down_hbm, back_down_ref),
            (back_across_hbm, back_across_ref),
        ))
    ]
    for copy in copies:
        copy.start()
    tail_ref[...] = jnp.zeros_like(tail_ref)
    filters = filter_bank()
    spread = (
        lax.broadcasted_iota(jnp.int32, (CELLS, BLOCK), 1) // CELL
        == lax.broadcasted_iota(jnp.int32, (CELLS, BLOCK), 0)
    ).astype(f32)
    for copy in copies:
        copy.wait()

    pair = 2 * TILE
    forward = jnp.concatenate([across_ref[:pair], across_ref[...]], axis=0)
    backward = jnp.concatenate([back_across_ref[...], back_across_ref[...]], axis=0)
    spots = [way_to(place_ref[0], piece) for piece in range(CHIPS)]

    def halve():
        tail_ref[:PADDED, :PADDED - BLOCK] = image_ref[:, BLOCK:]
        whole = TALL - 16
        for first, width, source in ((0, BLOCK, image_ref), (BLOCK, TILE, tail_ref)):
            lanes = slice(first, first + width)
            high_ref[:whole, lanes], low_ref[:whole, lanes] = split(source[:whole, :width])
            last = jnp.concatenate(
                [source[whole:PADDED, :width], jnp.zeros((8, width), f32)], axis=0
            )
            high_ref[whole:, lanes], low_ref[whole:, lanes] = split(last)

    def transform_across(column):
        lanes = slice(column * TILE, column * TILE + pair)
        high, low = high_ref[:, lanes], low_ref[:, lanes]
        wave_ref[column] = jnp.dot(
            jnp.concatenate([high, low, high], axis=1), forward, preferred_element_type=f32
        )

    def prepare():
        same, cross = kernel_spectrum(
            filters, index_ref[0, block], table_ref, down_taps_ref, along_ref
        )
        factor_ref[0] = same.reshape(SPAN // 8, 8, pair)
        factor_ref[1] = cross.reshape(SPAN // 8, 8, pair)
        weight_ref[...] = exact_dot(cell_weights(var_ref[block], bits_ref[block]), spread)
        info = item_info(var_ref, bits_ref, owner_ref, slot_ref)
        out_ref[:, TILES_BLK] = jnp.broadcast_to(info[None], (CHIPS, INFO, TILE))

    def stack(tile):
        column, line = divmod(tile, SIDE)
        stack_ref[tile] = stacked_halves(wave_ref[column, line * TILE:line * TILE + SPAN, :])

    def transform_down(tile):
        turn_ref[tile] = against_halves(down_ref[...], stack_ref.at[tile])

    def multiply(tile):
        wave = turn_ref[tile, :SPAN].reshape(SPAN // 8, 8, pair)
        turned = pltpu.roll(wave, 4, 1)
        wave_c, wave_s = wave[..., :TILE], wave[..., TILE:]
        turned_c, turned_s = turned[..., :TILE], turned[..., TILE:]
        same_c, same_s = factor_ref[0, :, :, :TILE], factor_ref[0, :, :, TILE:]
        cross_c, cross_s = factor_ref[1, :, :, :TILE], factor_ref[1, :, :, TILE:]
        result_c = wave_c * same_c + turned_c * cross_c - wave_s * same_s - turned_s * cross_s
        result_s = wave_s * same_c + turned_s * cross_c + wave_c * same_s + turned_c * cross_s
        result = jnp.concatenate(
            [result_c.reshape(SPAN, TILE), result_s.reshape(SPAN, TILE)], axis=1
        )
        result_ref[tile] = stacked_halves(result)

    def back_down(tile):
        column, line = divmod(tile, SIDE)
        high, low = split(against_halves(back_down_ref[...], result_ref.at[tile]))
        rows_ref[column, line * TILE:(line + 1) * TILE, :pair] = high
        rows_ref[column, line * TILE:(line + 1) * TILE, pair:] = low

    def back_across(column):
        matched = jnp.dot(rows_ref[column], backward, preferred_element_type=f32)
        matched = matched[:, :TILE] + matched[:, TILE:]
        weight = weight_ref[:, column * TILE:(column + 1) * TILE]
        weighted = matched.reshape(CELLS, CELL, TILE) * weight[:, None, :]
        weighted = weighted.reshape(SIDE, CHIPS, PIECE, TILE)
        for line in range(SIDE):
            item = line * SIDE + column
            for piece in range(CHIPS):
                out_ref[spots[piece], item] = weighted[line, piece]

    halve()
    transform_across(0)
    prepare()
    for step in range(TILES_BLK + 5):
        if step % SIDE == 0 and step // SIDE + 1 < SIDE:
            transform_across(step // SIDE + 1)
        for delay, stage in enumerate((stack, transform_down, multiply, back_down)):
            if 0 <= step - delay < TILES_BLK:
                stage(step - delay)
        column, rest = divmod(step - 4, SIDE)
        if rest == SIDE - 1 and 0 <= column < SIDE:
            back_across(column)
    each = CHIPS // count
    sends = [
        pltpu.make_async_copy(out_ref.at[way * each:(way + 1) * each], out_hbm, out_sems.at[way])
        for way, out_hbm in enumerate(outs)
    ]
    for send in reversed(sends):
        send.start()
    for send in sends:
        send.wait()


def match_block(block, place, exposures, variance, bits, table, index, owner, slot):
    blocks = exposures.shape[1]
    items = blocks * TILES_BLK
    groups = TILES_BLK + 1
    count = 4
    matrices = transforms()
    return pl.pallas_call(
        functools.partial(match_kernel, block=block),
        out_shape=[jax.ShapeDtypeStruct((CHIPS // count, groups, PIECE, TILE), f32)] * count,
        in_specs=[pl.BlockSpec(memory_space=pltpu.SMEM)]
        + [pl.BlockSpec(memory_space=pltpu.HBM)] * (7 + len(matrices)),
        out_specs=[pl.BlockSpec(memory_space=pltpu.HBM)] * count,
        scratch_shapes=[
            pltpu.SMEM((1, blocks), jnp.int32),
            pltpu.SMEM(table.shape, f32),
            pltpu.VMEM((PADDED, PADDED), f32),
            pltpu.VMEM((blocks, CELLS, CELLS), f32),
            pltpu.VMEM((blocks, CELLS, CELLS), jnp.int32),
            pltpu.VMEM((1, items), jnp.int32),
            pltpu.VMEM((1, items), jnp.int32),
            *[pltpu.VMEM(matrix.shape, matrix.dtype) for matrix in matrices],
            pltpu.SemaphoreType.DMA((7 + len(matrices),)),
            pltpu.SemaphoreType.DMA((4,)),
            pltpu.VMEM((TALL, TILE), f32),
            pltpu.VMEM((TALL, WIDE), bf16),
            pltpu.VMEM((TALL, WIDE), bf16),
            pltpu.VMEM((SIDE, TALL, 2 * TILE), f32),
            pltpu.VMEM((TILES_BLK, 2 * SPAN, 2 * TILE), bf16),
            pltpu.VMEM((TILES_BLK, SPAN + 8, 2 * TILE), f32),
            pltpu.VMEM((TILES_BLK, 2 * SPAN, 2 * TILE), bf16),
            pltpu.VMEM((SIDE, BLOCK, 4 * TILE), bf16),
            pltpu.VMEM((2, SPAN // 8, 8, 2 * TILE), f32),
            pltpu.VMEM((CELLS, BLOCK), f32),
            pltpu.VMEM((CHIPS, groups, PIECE, TILE), f32),
        ],
        compiler_params=pltpu.CompilerParams(vmem_limit_bytes=59 << 20),
        cost_estimate=pl.CostEstimate(
            flops=2 * 256 * 256 * 40000, bytes_accessed=3 << 20, transcendentals=0
        ),
        name="match_block",
    )(place, index, table, exposures, variance, bits, owner, slot, *matrices)


WAYS = (0, 3, 1, 2)


def keep_kernel(part_hbm, out_ref, sem):
    copy = pltpu.make_async_copy(part_hbm, out_ref, sem)
    copy.start()
    copy.wait()


def turn_kernel(*refs):
    for first, part_ref in zip(WAYS, refs[:4]):
        for second, out_ref in enumerate(refs[4:]):
            out_ref[first] = part_ref[second]


def partial_kernel(place_ref, *refs, block):
    part_refs, before, (mine_ref, other_ref) = refs[:4], refs[4:-2], refs[-2:]
    core = place_ref[0] % 2
    per_group = TILE // TILES_BLK
    lane = lax.broadcasted_iota(jnp.int32, (INFO, TILE), 1)
    info = [
        part_refs[source // 4][source % 4, TILES_BLK * PIECE:, :] for source in range(CHIPS)
    ]
    rows = []
    for m in range(PER_TILE):
        groups = []
        for group in range(CHIPS // per_group):
            total = None
            for member in range(per_group):
                goal = member * TILES_BLK
                shift = (goal - (m * 2 + block) * TILES_BLK) % TILE
                value = info[group * per_group + member]
                value = pltpu.roll(value, shift, 1) if shift else value
                here = (lane >= goal) & (lane < goal + TILES_BLK)
                total = value if total is None else jnp.where(here, value, total)
            groups.append(total)
        rows.append(jnp.concatenate(groups, axis=1))

    targets = VISITS * OWN_DEV
    owned = targets // 2
    items = CHIPS * TILES_BLK
    row = lax.broadcasted_iota(jnp.int32, (targets, items), 0)
    side = (row // owned + core) % 2
    inner = row % owned
    wanted = ((inner // OWN_DEV) * 2 + side) * OWN_DEV + inner % OWN_DEV
    target = rows[0][PER_TILE:PER_TILE + 1, :].astype(jnp.int32)
    route = jnp.where(wanted == target, 1.0, 0.0).astype(bf16)
    weights = jnp.concatenate(rows + [jnp.zeros((TILE - INFO * PER_TILE, items), f32)], axis=0)

    def store(spot, total):
        for number, goal_ref in enumerate((mine_ref, other_ref)):
            value = total[number * owned:(number + 1) * owned]
            goal_ref[spot, :] = value + before[number][spot, :] if before else value

    sums = 0.0
    for half in split(weights):
        sums = sums + lax.dot_general(
            route, half, (((1,), (1,)), ((), ())), preferred_element_type=f32
        )
    store(pl.ds(owned * PIECE, owned), sums)
    for line in range(PIECE):
        part = jnp.concatenate(
            [
                part_ref[:, pl.ds(line, TILES_BLK, PIECE), :].reshape(items // 4, TILE)
                for part_ref in part_refs
            ],
            axis=0,
        )
        high, low = split(part)
        total = jnp.dot(route, jnp.concatenate([high, low], axis=1), preferred_element_type=f32)
        store(pl.ds(line, owned, PIECE), total[:, :TILE] + total[:, TILE:])


def spread_cells(sums, cell_row):
    pattern = (
        lax.broadcasted_iota(jnp.int32, (TILE, TILE), 1) // CELL + cell_row * INFO
        == lax.broadcasted_iota(jnp.int32, (TILE, TILE), 0)
    ).astype(f32)
    return jnp.dot(sums, pattern, precision=lax.Precision.HIGHEST, preferred_element_type=f32)


def merge_kernel(place_ref, mine_ref, other_ref, out_ref):
    owned = VISITS * OWN_DEV // 2
    cell_row = (place_ref[0] // 2) // (CELL // PIECE)
    sums = mine_ref[owned * PIECE:, :] + other_ref[owned * PIECE:, :]
    scale = 1.0 / (spread_cells(sums, cell_row) + prior_weight)
    total = mine_ref[:owned * PIECE, :] + other_ref[:owned * PIECE, :]
    total = total.reshape(owned, PIECE, TILE) * scale[:, None, :]
    out_ref[...] = total.reshape(owned * PIECE, TILE)


def chi_kernel(place_ref, mine_ref, other_ref, part_ref, upper_ref, lower_ref):
    owned = VISITS * OWN_DEV // 2
    first = owned * PIECE + (place_ref[0] // 2) * OWN_DEV
    rows = pl.ds(pl.multiple_of(first, OWN_DEV), OWN_DEV)
    sums = mine_ref[rows, :] + other_ref[rows, :]
    per_cell = CELL // PIECE
    for m in range(PER_TILE):
        weight = spread_cells(sums, m) + prior_weight
        weight = jnp.broadcast_to(weight[:, None, :], (OWN_DEV, PIECE, TILE))
        part = part_ref[m * per_cell:(m + 1) * per_cell]
        chi_ref = upper_ref if m < PER_TILE // 2 else lower_ref
        place = m % (PER_TILE // 2) * per_cell
        chi_ref[place:place + per_cell] = part * part * weight.reshape(1, OWN_DEV * PIECE, TILE)


def image_kernel(part_ref, image_ref):
    for slot in range(OWN_DEV):
        rows = slice(slot * PIECE, (slot + 1) * PIECE)
        image_ref[slot] = part_ref[:, rows, :].reshape(TILE, TILE)


def detection_kernel(upper_ref, more_upper_ref, lower_ref, more_lower_ref, out_ref):
    for slot in range(OWN_DEV):
        rows = slice(slot * PIECE, (slot + 1) * PIECE)
        upper = upper_ref[:, rows, :] + more_upper_ref[:, rows, :]
        lower = lower_ref[:, rows, :] + more_lower_ref[:, rows, :]
        out_ref[slot, :TILE // 2] = upper.reshape(TILE // 2, TILE)
        out_ref[slot, TILE // 2:] = lower.reshape(TILE // 2, TILE)


def local(exposures, variance, mask_planes, kernel_table, kernel_index, tile_owner, tile_slot):
    place = lax.axis_index("visit").astype(jnp.int32).reshape(1)
    smem = pl.BlockSpec(memory_space=pltpu.SMEM)
    vmem = pl.BlockSpec(memory_space=pltpu.VMEM)
    params = pltpu.CompilerParams(vmem_limit_bytes=32 << 20)
    owned = VISITS * OWN_DEV // 2

    def exchange(parts):
        for phase in range(2):
            parts = [
                lax.ppermute(parts[way], "visit", phase_partners(phase, way)) if way else parts[0]
                for way in WAYS
            ]
            if phase == 0:
                parts = pl.pallas_call(
                    turn_kernel,
                    out_shape=[jax.ShapeDtypeStruct(parts[0].shape, f32)] * 4,
                    in_specs=[vmem] * 4,
                    out_specs=[vmem] * 4,
                    compiler_params=params,
                    name="turn",
                )(*parts)
        return parts

    table = kernel_table.T
    owner = tile_owner.reshape(tile_slot.shape)
    def spread_tiles(pieces):
        return lax.all_to_all(pieces, "visit", 0, 0, axis_index_groups=same_core, tiled=True)

    same_core = [list(range(core, VISITS, 2)) for core in range(2)]
    operands = (place, exposures, variance, mask_planes, table, kernel_index, owner, tile_slot)
    partial = ()
    for block in range(exposures.shape[1]):
        pieces = match_block(block, *operands)
        own = pl.pallas_call(
            keep_kernel,
            out_shape=jax.ShapeDtypeStruct(pieces[0].shape, f32),
            in_specs=[pl.BlockSpec(memory_space=pltpu.HBM)],
            out_specs=vmem,
            scratch_shapes=[pltpu.SemaphoreType.DMA],
            compiler_params=params,
            name="keep",
        )(pieces[0])
        parts = [part.reshape(4, -1, TILE) for part in exchange([own, *pieces[1:]])]
        partial = pl.pallas_call(
            functools.partial(partial_kernel, block=block),
            out_shape=[jax.ShapeDtypeStruct((owned * (PIECE + 1), TILE), f32)] * 2,
            in_specs=[smem] + [vmem] * (4 + len(partial)),
            out_specs=[vmem, vmem],
            compiler_params=params,
            name="partial_sums",
        )(place, *parts, *partial)
    mine, other = partial
    other = lax.ppermute(other, "visit", [(device, device ^ 1) for device in range(VISITS)])
    pieces = pl.pallas_call(
        merge_kernel,
        out_shape=jax.ShapeDtypeStruct((owned * PIECE, TILE), f32),
        in_specs=[smem, vmem, vmem],
        out_specs=vmem,
        compiler_params=params,
        name="merge_cores",
    )(place, mine, other)
    pieces = spread_tiles(pieces.reshape(CHIPS, OWN_DEV * PIECE, TILE))
    halves = pl.pallas_call(
        chi_kernel,
        out_shape=[jax.ShapeDtypeStruct((CHIPS // 2, OWN_DEV * PIECE, TILE), f32)] * 2,
        in_specs=[smem, vmem, vmem, vmem],
        out_specs=[vmem, vmem],
        compiler_params=params,
        name="chi",
    )(place, mine, other, pieces)
    tiles = jax.ShapeDtypeStruct((OWN_DEV, TILE, TILE), f32)
    image = pl.pallas_call(
        image_kernel,
        out_shape=tiles,
        in_specs=[vmem],
        out_specs=vmem,
        compiler_params=params,
        name="image",
    )(pieces)

    pairings = ([(0, 1), (1, 0), (2, 3), (3, 2)], [(0, 3), (3, 0), (1, 2), (2, 1)])
    halves = [
        half + lax.ppermute(half, "band", pairings[number]) for number, half in enumerate(halves)
    ]
    terms = []
    for number, half in enumerate(halves):
        terms.extend((half, lax.ppermute(half, "band", pairings[1 - number])))
    detection = pl.pallas_call(
        detection_kernel,
        out_shape=tiles,
        in_specs=[vmem] * 4,
        out_specs=vmem,
        compiler_params=params,
        name="detection",
    )(*terms)
    return image[None], detection


def solution(mesh):
    placed = (
        P("band", "visit", None, None),
        P("band", "visit", None, None),
        P("band", "visit", None, None),
        P(),
        P("band", "visit"),
        P("band", "visit", None),
        P("band", "visit"),
    )
    return jax.shard_map(
        local,
        mesh=mesh,
        in_specs=placed,
        out_specs=(P("band", "visit", None, None), P("visit", None, None)),
        check_vma=False,
    )
```

```python
import functools

import jax
import jax.numpy as jnp
import numpy as np
from jax import lax
from jax.experimental import pallas as pl
from jax.experimental.pallas import tpu as pltpu
from jax.sharding import PartitionSpec as P

BLOCK = 512
TILE = 128
CELL = 32
KSIZE = 41
OWN_DEV = 8
PADDED = BLOCK + KSIZE - 1
NFILT = 11
VISITS = 32
SIDE = BLOCK // TILE
CELLS = BLOCK // CELL
PER_TILE = TILE // CELL
TILES_BLK = SIDE * SIDE
CHIPS = VISITS // 2
PIECE = TILE // CHIPS
INFO = 8
SPAN = TILE + KSIZE - 1
HALF = SPAN // 2
TALL = 560
TAPS = 48
WIDTH = 256
KEPT = 176
WINDOWS = 3

width_fractions = (0.075, 0.15, 0.3)
family_degrees = (4, 2, 2)
prior_weight = 0.05
reject_planes = 3

f32 = jnp.float32
bf16 = jnp.bfloat16


def as_halves(matrix):
    high = matrix.astype(np.float32).astype(bf16)
    low = (matrix - high.astype(np.float64)).astype(np.float32).astype(bf16)
    return high, low


def waves(length):
    angle = 2 * np.pi * (np.arange(length // 2) + 0.5) / length
    phase = angle[:, None] * np.arange(length)
    return np.cos(phase), np.sin(phase)


def transforms():
    cosine, sine = waves(WIDTH)
    by_lane = np.concatenate([cosine, sine], axis=0)
    back_across = np.zeros((WIDTH, WIDTH))
    back_across[:, :KEPT] = by_lane[:, :KEPT] * (2 / WIDTH)
    along = np.zeros((TILE, WIDTH), np.float32)
    along[:KSIZE] = np.concatenate([cosine, -sine], axis=0)[:, :KSIZE].T

    cosine, sine = waves(SPAN)
    number = np.arange(HALF)
    spot = 8 * (number // 4) + number % 4
    by_row = np.zeros((SPAN, SPAN))
    by_row[spot], by_row[spot + 4] = cosine, sine
    down = np.zeros((SPAN + 8, SPAN))
    down[:SPAN] = by_row
    back_down = by_row.T[:TILE] * (2 / SPAN)

    def three(matrix, width=512):
        high, low = as_halves(matrix)
        rest = np.zeros((matrix.shape[0], width - 3 * matrix.shape[1]), bf16)
        return np.concatenate([high, high, low, rest], axis=1)

    same = np.zeros((SPAN + 8, TAPS))
    cross = np.zeros((SPAN + 8, TAPS))
    same[spot, :KSIZE] = same[spot + 4, :KSIZE] = cosine[:, :KSIZE]
    cross[spot, :KSIZE], cross[spot + 4, :KSIZE] = sine[:, :KSIZE], -sine[:, :KSIZE]
    return (
        np.concatenate(as_halves(by_lane.T), axis=0),
        three(down),
        three(back_down),
        np.concatenate(as_halves(back_across), axis=0),
        np.concatenate([three(same, 256), three(cross, 256)], axis=0),
        along,
    )


def filter_terms():
    starts = (0, 5, 8)
    terms = []
    for family in range(3):
        for first in range(family_degrees[family] + 1):
            for second in range(family_degrees[family] + 1 - first):
                terms.append((starts[family] + first, starts[family] + second))
    return terms


def profiles_at(offset):
    half_width = (KSIZE - 1) // 2
    inside = (offset >= 0) & (offset < KSIZE)
    taps = offset.astype(f32) - half_width
    values = []
    for family in range(3):
        scaled = taps / (width_fractions[family] * half_width)
        value = jnp.where(inside, jnp.exp(-0.5 * scaled * scaled), 0.0)
        for degree in range(family_degrees[family] + 1):
            values.append(value)
            value = value * scaled
    return values


def split(value):
    high = value.astype(bf16)
    return high, (value - high.astype(f32)).astype(bf16)


def cell_weights(variance, bits):
    usable = (jnp.bitwise_and(bits, reject_planes) != reject_planes).astype(f32)
    return usable / variance


def item_info(var_ref, bits_ref, owner_ref, slot_ref):
    exact = lax.Precision.HIGHEST
    lane = lax.broadcasted_iota(jnp.int32, (1, TILE), 1)
    row = lax.broadcasted_iota(jnp.int32, (CELLS, TILE), 0)
    item = lane % TILES_BLK
    cell_row = (item // SIDE) * PER_TILE + lane // (2 * TILES_BLK)
    columns = None
    for block in range(2):
        picked = ((row == cell_row) & ((lane // TILES_BLK) % 2 == block)).astype(f32)
        term = lax.dot_general(
            cell_weights(var_ref[block], bits_ref[block]), picked,
            (((0,), (0,)), ((), ())), precision=exact, preferred_element_type=f32,
        )
        columns = term if columns is None else columns + term
    rows = []
    for n in range(PER_TILE):
        chosen = row == (item % SIDE) * PER_TILE + n
        rows.append(jnp.sum(jnp.where(chosen, columns, 0.0), axis=0, keepdims=True))
    target = (owner_ref[...] * OWN_DEV + slot_ref[...]).astype(f32)
    rows.append(jnp.concatenate([target, jnp.zeros((1, TILE - 2 * TILES_BLK), f32)], axis=1))
    rows.append(jnp.zeros((INFO - PER_TILE - 1, TILE), f32))
    return jnp.concatenate(rows, axis=0)


def phase_masks(core):
    return (1, 3) if core == 0 else (3, 1)


def way_to(place, piece):
    core, offset = place % 2, jnp.bitwise_xor(place // 2, piece)
    first, second = 0, 0
    for coordinate in (offset // 4, offset % 4):
        high = coordinate // 2
        both = jnp.bitwise_xor(high, coordinate % 2)
        first = 2 * first + jnp.where(core == 0, both, high)
        second = 2 * second + jnp.where(core == 0, high, both)
    return 4 * first + second


def phase_partners(phase, way):
    partners = []
    for device in range(VISITS):
        mask = phase_masks(device % 2)[phase]
        partners.append((device, device ^ (2 * (4 * mask * (way // 2) + mask * (way % 2)))))
    return partners


def exact_dot(left, right, sides=((1,), (0,))):
    return lax.dot_general(
        left, right, (sides, ((), ())), precision=lax.Precision.HIGHEST, preferred_element_type=f32
    )


def stacked_halves(value):
    high = value.astype(bf16).astype(f32)
    return jnp.concatenate([high, value - high], axis=0).astype(bf16)


def against_halves(matrix, halves_ref):
    rows = jnp.concatenate([halves_ref[...], halves_ref[:SPAN + 8, :]], axis=0)
    return jnp.dot(matrix, rows, preferred_element_type=f32)


def filter_bank():
    taps = lax.broadcasted_iota(jnp.int32, (1, TILE), 1)
    values = profiles_at(taps)
    norms = [jnp.sqrt(jnp.sum(value * value, axis=1, keepdims=True)) for value in values]
    rows = [value / norm for value, norm in zip(values, norms)]
    wide = jnp.concatenate(rows + [jnp.zeros((16 - NFILT, TILE), f32)], axis=0)
    lane = lax.broadcasted_iota(jnp.int32, (TAPS, TILE), 1)
    tall = jnp.zeros((TAPS, TILE), f32)
    for number, (value, norm) in enumerate(
        zip(profiles_at(lax.broadcasted_iota(jnp.int32, (TAPS, TILE), 0)), norms)
    ):
        tall = jnp.where(lane == number, value / norm, tall)
    return wide, tall


def kernel_spectrum(filters, which, table_ref, down_taps_ref, along_ref):
    first = lax.broadcasted_iota(jnp.int32, (16, 16), 0)
    second = lax.broadcasted_iota(jnp.int32, (16, 16), 1)
    mixing = jnp.zeros((16, 16), f32)
    for number, (p, q) in enumerate(filter_terms()):
        mixing = jnp.where((first == p) & (second == q), table_ref[number, which], mixing)
    wide, tall = filters
    across = exact_dot(mixing, exact_dot(wide, along_ref[...]))
    across = jnp.concatenate([across, jnp.zeros((TILE - 16, 2 * TILE), f32)], axis=0)
    mixed = exact_dot(tall, across)
    high = mixed.astype(bf16).astype(f32)
    rest = jnp.zeros((256 - 3 * TAPS, 2 * TILE), f32)
    mixed = jnp.concatenate([high, mixed - high, high, rest], axis=0).astype(bf16)
    both = jnp.dot(down_taps_ref[...], mixed, preferred_element_type=f32)
    return both[:SPAN], both[SPAN + 8:2 * SPAN + 8]


def match_kernel(
    place_ref, index_hbm, table_hbm, image_hbm, var_hbm, bits_hbm, owner_hbm, slot_hbm,
    across_hbm, down_hbm, back_down_hbm, back_across_hbm, down_taps_hbm, along_hbm,
    *rest, block,
):
    count = 4
    outs = rest[:count]
    (
        index_ref, table_ref, image_ref, var_ref, bits_ref, owner_ref, slot_ref,
        across_ref, down_ref, back_down_ref, back_across_ref, down_taps_ref, along_ref, sems,
        out_sems, tail_ref, high_ref, low_ref, wave_ref, stack_ref, turn_ref, result_ref, rows_ref,
        matched_ref, factor_ref, weight_ref, out_ref,
    ) = rest[count:]
    copies = [
        pltpu.make_async_copy(source, goal, sems.at[number])
        for number, (source, goal) in enumerate((
            (index_hbm, index_ref),
            (table_hbm, table_ref),
            (down_taps_hbm, down_taps_ref),
            (along_hbm, along_ref),
            (image_hbm.at[0, block], image_ref),
            (across_hbm, across_ref),
            (var_hbm.at[0], var_ref),
            (bits_hbm.at[0], bits_ref),
            (owner_hbm, owner_ref),
            (slot_hbm, slot_ref),
            (down_hbm, down_ref),
            (back_down_hbm, back_down_ref),
            (back_across_hbm, back_across_ref),
        ))
    ]
    for copy in copies:
        copy.start()
    tail_ref[...] = jnp.zeros_like(tail_ref)
    filters = filter_bank()
    spread = (
        lax.broadcasted_iota(jnp.int32, (CELLS, BLOCK), 1) // CELL
        == lax.broadcasted_iota(jnp.int32, (CELLS, BLOCK), 0)
    ).astype(f32)
    for copy in copies:
        copy.wait()

    pair = 2 * TILE
    forward = jnp.concatenate([across_ref[:pair], across_ref[...]], axis=0)
    backward = jnp.concatenate([back_across_ref[:pair], back_across_ref[...]], axis=0)
    spots = [way_to(place_ref[0], piece) for piece in range(CHIPS)]

    def windows(rows):
        tiles = [image_ref[rows, place:place + TILE] for place in range(0, BLOCK, TILE)]
        tiles.append(tail_ref[rows, :])
        lane = lax.broadcasted_iota(jnp.int32, tiles[0].shape, 1)
        second = [pltpu.roll(tile, 80, 1) for tile in tiles[1:4]]
        third = [pltpu.roll(tile, 32, 1) for tile in tiles[2:5]]
        return (
            tiles[:2],
            [jnp.where(lane < 80, second[spot], second[spot + 1]) for spot in range(2)],
            [jnp.where(lane < 32, third[spot], third[spot + 1]) for spot in range(2)],
        )

    def halve():
        tail_ref[:PADDED, :PADDED - BLOCK] = image_ref[:, BLOCK:]
        whole = TALL - 16
        for window, tiles in enumerate(windows(slice(0, whole))):
            for spot, tile in enumerate(tiles):
                lanes = slice(spot * TILE, (spot + 1) * TILE)
                high_ref[window, :whole, lanes], low_ref[window, :whole, lanes] = split(tile)
        for window, tiles in enumerate(windows(slice(whole, PADDED))):
            for spot, tile in enumerate(tiles):
                lanes = slice(spot * TILE, (spot + 1) * TILE)
                last = jnp.concatenate([tile, jnp.zeros((8, TILE), f32)], axis=0)
                high_ref[window, whole:, lanes], low_ref[window, whole:, lanes] = split(last)

    def transform_across(window):
        high, low = high_ref[window], low_ref[window]
        wave_ref[window] = jnp.dot(
            jnp.concatenate([high, low, high], axis=1), forward, preferred_element_type=f32
        )

    def prepare():
        same, cross = kernel_spectrum(
            filters, index_ref[0, block], table_ref, down_taps_ref, along_ref
        )
        factor_ref[0] = same.reshape(SPAN // 8, 8, pair)
        factor_ref[1] = cross.reshape(SPAN // 8, 8, pair)
        weight_ref[...] = exact_dot(cell_weights(var_ref[block], bits_ref[block]), spread)
        info = item_info(var_ref, bits_ref, owner_ref, slot_ref)
        out_ref[:, TILES_BLK] = jnp.broadcast_to(info[None], (CHIPS, INFO, TILE))

    def stack(tile):
        column, line = divmod(tile, SIDE)
        stack_ref[tile] = stacked_halves(wave_ref[column, line * TILE:line * TILE + SPAN, :])

    def transform_down(tile):
        turn_ref[tile] = against_halves(down_ref[...], stack_ref.at[tile])

    def multiply(tile):
        wave = turn_ref[tile, :SPAN].reshape(SPAN // 8, 8, pair)
        turned = pltpu.roll(wave, 4, 1)
        wave_c, wave_s = wave[..., :TILE], wave[..., TILE:]
        turned_c, turned_s = turned[..., :TILE], turned[..., TILE:]
        same_c, same_s = factor_ref[0, :, :, :TILE], factor_ref[0, :, :, TILE:]
        cross_c, cross_s = factor_ref[1, :, :, :TILE], factor_ref[1, :, :, TILE:]
        result_c = wave_c * same_c + turned_c * cross_c - wave_s * same_s - turned_s * cross_s
        result_s = wave_s * same_c + turned_s * cross_c + wave_c * same_s + turned_c * cross_s
        result = jnp.concatenate(
            [result_c.reshape(SPAN, TILE), result_s.reshape(SPAN, TILE)], axis=1
        )
        result_ref[tile] = stacked_halves(result)

    def back_down(tile):
        column, line = divmod(tile, SIDE)
        high, low = split(against_halves(back_down_ref[...], result_ref.at[tile]))
        rows_ref[column, line * TILE:(line + 1) * TILE, :pair] = high
        rows_ref[column, line * TILE:(line + 1) * TILE, pair:] = low

    def back_across(window):
        high, low = rows_ref[window, :, :pair], rows_ref[window, :, pair:]
        matched_ref[window] = jnp.dot(
            jnp.concatenate([high, low, high], axis=1), backward, preferred_element_type=f32
        )
        if window == 1:
            finish(0)
            finish(1)
        if window == 2:
            finish(2)
            finish(3)

    def finish(column):
        lane = lax.broadcasted_iota(jnp.int32, (BLOCK, TILE), 1)

        def part(window, spot, shift):
            value = matched_ref[window, :, spot * TILE:(spot + 1) * TILE]
            return pltpu.roll(value, shift, 1) if shift else value

        if column == 0:
            matched = part(0, 0, 0)
        elif column == 1:
            matched = jnp.where(lane < 48, part(0, 1, 0), part(1, 0, 48))
        elif column == 2:
            matched = jnp.where(lane < 96, part(1, 1, 48), part(2, 0, 96))
            matched = jnp.where(lane < 48, part(1, 0, 48), matched)
        else:
            matched = jnp.where(lane < 96, part(2, 0, 96), part(2, 1, 96))
        weight = weight_ref[:, column * TILE:(column + 1) * TILE]
        weighted = matched.reshape(CELLS, CELL, TILE) * weight[:, None, :]
        weighted = weighted.reshape(SIDE, CHIPS, PIECE, TILE)
        for line in range(SIDE):
            item = line * SIDE + column
            for piece in range(CHIPS):
                out_ref[spots[piece], item] = weighted[line, piece]

    halve()
    transform_across(0)
    prepare()
    tiles = WINDOWS * SIDE
    for step in range(tiles + 5):
        if step % SIDE == 0 and step // SIDE + 1 < WINDOWS:
            transform_across(step // SIDE + 1)
        for delay, stage in enumerate((stack, transform_down, multiply, back_down)):
            if 0 <= step - delay < tiles:
                stage(step - delay)
        column, rest = divmod(step - 4, SIDE)
        if rest == SIDE - 1 and 0 <= column < WINDOWS:
            back_across(column)
    each = CHIPS // count
    sends = [
        pltpu.make_async_copy(out_ref.at[way * each:(way + 1) * each], out_hbm, out_sems.at[way])
        for way, out_hbm in enumerate(outs)
    ]
    for send in reversed(sends):
        send.start()
    for send in sends:
        send.wait()


def match_block(block, place, exposures, variance, bits, table, index, owner, slot):
    blocks = exposures.shape[1]
    items = blocks * TILES_BLK
    groups = TILES_BLK + 1
    count = 4
    matrices = transforms()
    return pl.pallas_call(
        functools.partial(match_kernel, block=block),
        out_shape=[jax.ShapeDtypeStruct((CHIPS // count, groups, PIECE, TILE), f32)] * count,
        in_specs=[pl.BlockSpec(memory_space=pltpu.SMEM)]
        + [pl.BlockSpec(memory_space=pltpu.HBM)] * (7 + len(matrices)),
        out_specs=[pl.BlockSpec(memory_space=pltpu.HBM)] * count,
        scratch_shapes=[
            pltpu.SMEM((1, blocks), jnp.int32),
            pltpu.SMEM(table.shape, f32),
            pltpu.VMEM((PADDED, PADDED), f32),
            pltpu.VMEM((blocks, CELLS, CELLS), f32),
            pltpu.VMEM((blocks, CELLS, CELLS), jnp.int32),
            pltpu.VMEM((1, items), jnp.int32),
            pltpu.VMEM((1, items), jnp.int32),
            *[pltpu.VMEM(matrix.shape, matrix.dtype) for matrix in matrices],
            pltpu.SemaphoreType.DMA((7 + len(matrices),)),
            pltpu.SemaphoreType.DMA((4,)),
            pltpu.VMEM((TALL, TILE), f32),
            pltpu.VMEM((WINDOWS, TALL, WIDTH), bf16),
            pltpu.VMEM((WINDOWS, TALL, WIDTH), bf16),
            pltpu.VMEM((WINDOWS, TALL, WIDTH), f32),
            pltpu.VMEM((WINDOWS * SIDE, 2 * SPAN, WIDTH), bf16),
            pltpu.VMEM((WINDOWS * SIDE, SPAN + 8, WIDTH), f32),
            pltpu.VMEM((WINDOWS * SIDE, 2 * SPAN, WIDTH), bf16),
            pltpu.VMEM((WINDOWS, BLOCK, 2 * WIDTH), bf16),
            pltpu.VMEM((WINDOWS, BLOCK, WIDTH), f32),
            pltpu.VMEM((2, SPAN // 8, 8, 2 * TILE), f32),
            pltpu.VMEM((CELLS, BLOCK), f32),
            pltpu.VMEM((CHIPS, groups, PIECE, TILE), f32),
        ],
        compiler_params=pltpu.CompilerParams(vmem_limit_bytes=59 << 20),
        cost_estimate=pl.CostEstimate(
            flops=2 * 256 * 256 * 40000, bytes_accessed=3 << 20, transcendentals=0
        ),
        name="match_block",
    )(place, index, table, exposures, variance, bits, owner, slot, *matrices)


WAYS = (0, 3, 1, 2)


def keep_kernel(part_hbm, out_ref, sem):
    copy = pltpu.make_async_copy(part_hbm, out_ref, sem)
    copy.start()
    copy.wait()


def turn_kernel(*refs):
    for first, part_ref in zip(WAYS, refs[:4]):
        for second, out_ref in enumerate(refs[4:]):
            out_ref[first] = part_ref[second]


def partial_kernel(place_ref, *refs, block):
    part_refs, before, (mine_ref, other_ref) = refs[:4], refs[4:-2], refs[-2:]
    core = place_ref[0] % 2
    per_group = TILE // TILES_BLK
    lane = lax.broadcasted_iota(jnp.int32, (INFO, TILE), 1)
    info = [
        part_refs[source // 4][source % 4, TILES_BLK * PIECE:, :] for source in range(CHIPS)
    ]
    rows = []
    for m in range(PER_TILE):
        groups = []
        for group in range(CHIPS // per_group):
            total = None
            for member in range(per_group):
                goal = member * TILES_BLK
                shift = (goal - (m * 2 + block) * TILES_BLK) % TILE
                value = info[group * per_group + member]
                value = pltpu.roll(value, shift, 1) if shift else value
                here = (lane >= goal) & (lane < goal + TILES_BLK)
                total = value if total is None else jnp.where(here, value, total)
            groups.append(total)
        rows.append(jnp.concatenate(groups, axis=1))

    targets = VISITS * OWN_DEV
    owned = targets // 2
    items = CHIPS * TILES_BLK
    row = lax.broadcasted_iota(jnp.int32, (targets, items), 0)
    side = (row // owned + core) % 2
    inner = row % owned
    wanted = ((inner // OWN_DEV) * 2 + side) * OWN_DEV + inner % OWN_DEV
    target = rows[0][PER_TILE:PER_TILE + 1, :].astype(jnp.int32)
    route = jnp.where(wanted == target, 1.0, 0.0).astype(bf16)
    weights = jnp.concatenate(rows + [jnp.zeros((TILE - INFO * PER_TILE, items), f32)], axis=0)

    def store(spot, total):
        for number, goal_ref in enumerate((mine_ref, other_ref)):
            value = total[number * owned:(number + 1) * owned]
            goal_ref[spot, :] = value + before[number][spot, :] if before else value

    sums = 0.0
    for half in split(weights):
        sums = sums + lax.dot_general(
            route, half, (((1,), (1,)), ((), ())), preferred_element_type=f32
        )
    store(pl.ds(owned * PIECE, owned), sums)
    for line in range(PIECE):
        part = jnp.concatenate(
            [
                part_ref[:, pl.ds(line, TILES_BLK, PIECE), :].reshape(items // 4, TILE)
                for part_ref in part_refs
            ],
            axis=0,
        )
        high, low = split(part)
        total = jnp.dot(route, jnp.concatenate([high, low], axis=1), preferred_element_type=f32)
        store(pl.ds(line, owned, PIECE), total[:, :TILE] + total[:, TILE:])


def spread_cells(sums, cell_row):
    pattern = (
        lax.broadcasted_iota(jnp.int32, (TILE, TILE), 1) // CELL + cell_row * INFO
        == lax.broadcasted_iota(jnp.int32, (TILE, TILE), 0)
    ).astype(f32)
    return jnp.dot(sums, pattern, precision=lax.Precision.HIGHEST, preferred_element_type=f32)


def merge_kernel(place_ref, mine_ref, other_ref, out_ref):
    owned = VISITS * OWN_DEV // 2
    cell_row = (place_ref[0] // 2) // (CELL // PIECE)
    sums = mine_ref[owned * PIECE:, :] + other_ref[owned * PIECE:, :]
    scale = 1.0 / (spread_cells(sums, cell_row) + prior_weight)
    total = mine_ref[:owned * PIECE, :] + other_ref[:owned * PIECE, :]
    total = total.reshape(owned, PIECE, TILE) * scale[:, None, :]
    out_ref[...] = total.reshape(owned * PIECE, TILE)


def chi_kernel(place_ref, mine_ref, other_ref, part_ref, upper_ref, lower_ref):
    owned = VISITS * OWN_DEV // 2
    first = owned * PIECE + (place_ref[0] // 2) * OWN_DEV
    rows = pl.ds(pl.multiple_of(first, OWN_DEV), OWN_DEV)
    sums = mine_ref[rows, :] + other_ref[rows, :]
    per_cell = CELL // PIECE
    for m in range(PER_TILE):
        weight = spread_cells(sums, m) + prior_weight
        weight = jnp.broadcast_to(weight[:, None, :], (OWN_DEV, PIECE, TILE))
        part = part_ref[m * per_cell:(m + 1) * per_cell]
        chi_ref = upper_ref if m < PER_TILE // 2 else lower_ref
        place = m % (PER_TILE // 2) * per_cell
        chi_ref[place:place + per_cell] = part * part * weight.reshape(1, OWN_DEV * PIECE, TILE)


def image_kernel(part_ref, image_ref):
    for slot in range(OWN_DEV):
        rows = slice(slot * PIECE, (slot + 1) * PIECE)
        image_ref[slot] = part_ref[:, rows, :].reshape(TILE, TILE)


def detection_kernel(upper_ref, more_upper_ref, lower_ref, more_lower_ref, out_ref):
    for slot in range(OWN_DEV):
        rows = slice(slot * PIECE, (slot + 1) * PIECE)
        upper = upper_ref[:, rows, :] + more_upper_ref[:, rows, :]
        lower = lower_ref[:, rows, :] + more_lower_ref[:, rows, :]
        out_ref[slot, :TILE // 2] = upper.reshape(TILE // 2, TILE)
        out_ref[slot, TILE // 2:] = lower.reshape(TILE // 2, TILE)


def local(exposures, variance, mask_planes, kernel_table, kernel_index, tile_owner, tile_slot):
    place = lax.axis_index("visit").astype(jnp.int32).reshape(1)
    smem = pl.BlockSpec(memory_space=pltpu.SMEM)
    vmem = pl.BlockSpec(memory_space=pltpu.VMEM)
    params = pltpu.CompilerParams(vmem_limit_bytes=32 << 20)
    owned = VISITS * OWN_DEV // 2

    def exchange(parts):
        for phase in range(2):
            parts = [
                lax.ppermute(parts[way], "visit", phase_partners(phase, way)) if way else parts[0]
                for way in WAYS
            ]
            if phase == 0:
                parts = pl.pallas_call(
                    turn_kernel,
                    out_shape=[jax.ShapeDtypeStruct(parts[0].shape, f32)] * 4,
                    in_specs=[vmem] * 4,
                    out_specs=[vmem] * 4,
                    compiler_params=params,
                    name="turn",
                )(*parts)
        return parts

    table = kernel_table.T
    owner = tile_owner.reshape(tile_slot.shape)
    def spread_tiles(pieces):
        return lax.all_to_all(pieces, "visit", 0, 0, axis_index_groups=same_core, tiled=True)

    same_core = [list(range(core, VISITS, 2)) for core in range(2)]
    operands = (place, exposures, variance, mask_planes, table, kernel_index, owner, tile_slot)
    partial = ()
    for block in range(exposures.shape[1]):
        pieces = match_block(block, *operands)
        own = pl.pallas_call(
            keep_kernel,
            out_shape=jax.ShapeDtypeStruct(pieces[0].shape, f32),
            in_specs=[pl.BlockSpec(memory_space=pltpu.HBM)],
            out_specs=vmem,
            scratch_shapes=[pltpu.SemaphoreType.DMA],
            compiler_params=params,
            name="keep",
        )(pieces[0])
        parts = [part.reshape(4, -1, TILE) for part in exchange([own, *pieces[1:]])]
        partial = pl.pallas_call(
            functools.partial(partial_kernel, block=block),
            out_shape=[jax.ShapeDtypeStruct((owned * (PIECE + 1), TILE), f32)] * 2,
            in_specs=[smem] + [vmem] * (4 + len(partial)),
            out_specs=[vmem, vmem],
            compiler_params=params,
            name="partial_sums",
        )(place, *parts, *partial)
    mine, other = partial
    other = lax.ppermute(other, "visit", [(device, device ^ 1) for device in range(VISITS)])
    pieces = pl.pallas_call(
        merge_kernel,
        out_shape=jax.ShapeDtypeStruct((owned * PIECE, TILE), f32),
        in_specs=[smem, vmem, vmem],
        out_specs=vmem,
        compiler_params=params,
        name="merge_cores",
    )(place, mine, other)
    pieces = spread_tiles(pieces.reshape(CHIPS, OWN_DEV * PIECE, TILE))
    halves = pl.pallas_call(
        chi_kernel,
        out_shape=[jax.ShapeDtypeStruct((CHIPS // 2, OWN_DEV * PIECE, TILE), f32)] * 2,
        in_specs=[smem, vmem, vmem, vmem],
        out_specs=[vmem, vmem],
        compiler_params=params,
        name="chi",
    )(place, mine, other, pieces)
    tiles = jax.ShapeDtypeStruct((OWN_DEV, TILE, TILE), f32)
    image = pl.pallas_call(
        image_kernel,
        out_shape=tiles,
        in_specs=[vmem],
        out_specs=vmem,
        compiler_params=params,
        name="image",
    )(pieces)

    pairings = ([(0, 1), (1, 0), (2, 3), (3, 2)], [(0, 3), (3, 0), (1, 2), (2, 1)])
    halves = [
        half + lax.ppermute(half, "band", pairings[number]) for number, half in enumerate(halves)
    ]
    terms = []
    for number, half in enumerate(halves):
        terms.extend((half, lax.ppermute(half, "band", pairings[1 - number])))
    detection = pl.pallas_call(
        detection_kernel,
        out_shape=tiles,
        in_specs=[vmem] * 4,
        out_specs=vmem,
        compiler_params=params,
        name="detection",
    )(*terms)
    return image[None], detection


def solution(mesh):
    placed = (
        P("band", "visit", None, None),
        P("band", "visit", None, None),
        P("band", "visit", None, None),
        P(),
        P("band", "visit"),
        P("band", "visit", None),
        P("band", "visit"),
    )
    return jax.shard_map(
        local,
        mesh=mesh,
        in_specs=placed,
        out_specs=(P("band", "visit", None, None), P("visit", None, None)),
        check_vma=False,
    )
```

```python
import functools

import jax
import jax.numpy as jnp
import numpy as np
from jax import lax
from jax.experimental import pallas as pl
from jax.experimental.pallas import tpu as pltpu
from jax.sharding import PartitionSpec as P

BLOCK = 512
TILE = 128
CELL = 32
KSIZE = 41
OWN_DEV = 8
PADDED = BLOCK + KSIZE - 1
NFILT = 11
VISITS = 32
SIDE = BLOCK // TILE
CELLS = BLOCK // CELL
PER_TILE = TILE // CELL
TILES_BLK = SIDE * SIDE
CHIPS = VISITS // 2
PIECE = TILE // CHIPS
INFO = 8
SPAN = TILE + KSIZE - 1
HALF = SPAN // 2
TALL = 560
TAPS = 48
WIDTH = 256
KEPT = 176
WINDOWS = 3

width_fractions = (0.075, 0.15, 0.3)
family_degrees = (4, 2, 2)
prior_weight = 0.05
reject_planes = 3

f32 = jnp.float32
bf16 = jnp.bfloat16


def as_halves(matrix):
    high = matrix.astype(np.float32).astype(bf16)
    low = (matrix - high.astype(np.float64)).astype(np.float32).astype(bf16)
    return high, low


def waves(length):
    angle = 2 * np.pi * (np.arange(length // 2) + 0.5) / length
    phase = angle[:, None] * np.arange(length)
    return np.cos(phase), np.sin(phase)


def transforms():
    cosine, sine = waves(WIDTH)
    by_lane = np.concatenate([cosine, sine], axis=0)
    back_across = np.zeros((WIDTH, WIDTH))
    back_across[:, :KEPT] = by_lane[:, :KEPT] * (2 / WIDTH)
    along = np.zeros((TILE, WIDTH))
    along[:KSIZE] = np.concatenate([cosine, -sine], axis=0)[:, :KSIZE].T

    cosine, sine = waves(SPAN)
    number = np.arange(HALF)
    spot = 8 * (number // 4) + number % 4
    by_row = np.zeros((SPAN, SPAN))
    by_row[spot], by_row[spot + 4] = cosine, sine
    down = np.zeros((SPAN + 8, SPAN))
    down[:SPAN] = by_row
    back_down = by_row.T[:TILE] * (2 / SPAN)

    def three(matrix, width=512):
        high, low = as_halves(matrix)
        rest = np.zeros((matrix.shape[0], width - 3 * matrix.shape[1]), bf16)
        return np.concatenate([high, high, low, rest], axis=1)

    same = np.zeros((SPAN + 8, TAPS))
    cross = np.zeros((SPAN + 8, TAPS))
    same[spot, :KSIZE] = same[spot + 4, :KSIZE] = cosine[:, :KSIZE]
    cross[spot, :KSIZE], cross[spot + 4, :KSIZE] = sine[:, :KSIZE], -sine[:, :KSIZE]
    return (
        np.concatenate(as_halves(by_lane.T), axis=0),
        three(down),
        three(back_down),
        np.concatenate(as_halves(back_across), axis=0),
        np.concatenate([three(same, 256), three(cross, 256)], axis=0),
        np.concatenate([as_halves(along)[part] for part in (0, 0, 1)], axis=0),
    )


def filter_terms():
    starts = (0, 5, 8)
    terms = []
    for family in range(3):
        for first in range(family_degrees[family] + 1):
            for second in range(family_degrees[family] + 1 - first):
                terms.append((starts[family] + first, starts[family] + second))
    return terms


def profiles_at(offset):
    half_width = (KSIZE - 1) // 2
    inside = (offset >= 0) & (offset < KSIZE)
    taps = offset.astype(f32) - half_width
    values = []
    for family in range(3):
        scaled = taps / (width_fractions[family] * half_width)
        value = jnp.where(inside, jnp.exp(-0.5 * scaled * scaled), 0.0)
        for degree in range(family_degrees[family] + 1):
            values.append(value)
            value = value * scaled
    return values


def split(value):
    high = value.astype(bf16)
    return high, (value - high.astype(f32)).astype(bf16)


def cell_weights(variance, bits):
    usable = (jnp.bitwise_and(bits, reject_planes) != reject_planes).astype(f32)
    return usable / variance


def item_info(var_ref, bits_ref, owner_ref, slot_ref):
    exact = lax.Precision.HIGHEST
    lane = lax.broadcasted_iota(jnp.int32, (1, TILE), 1)
    row = lax.broadcasted_iota(jnp.int32, (CELLS, TILE), 0)
    item = lane % TILES_BLK
    cell_row = (item // SIDE) * PER_TILE + lane // (2 * TILES_BLK)
    columns = None
    for block in range(2):
        picked = ((row == cell_row) & ((lane // TILES_BLK) % 2 == block)).astype(f32)
        term = lax.dot_general(
            cell_weights(var_ref[block], bits_ref[block]), picked,
            (((0,), (0,)), ((), ())), precision=exact, preferred_element_type=f32,
        )
        columns = term if columns is None else columns + term
    rows = []
    for n in range(PER_TILE):
        chosen = row == (item % SIDE) * PER_TILE + n
        rows.append(jnp.sum(jnp.where(chosen, columns, 0.0), axis=0, keepdims=True))
    target = (owner_ref[...] * OWN_DEV + slot_ref[...]).astype(f32)
    rows.append(jnp.concatenate([target, jnp.zeros((1, TILE - 2 * TILES_BLK), f32)], axis=1))
    rows.append(jnp.zeros((INFO - PER_TILE - 1, TILE), f32))
    return jnp.concatenate(rows, axis=0)


def phase_masks(core):
    return (1, 3) if core == 0 else (3, 1)


def way_to(place, piece):
    core, offset = place % 2, jnp.bitwise_xor(place // 2, piece)
    first, second = 0, 0
    for coordinate in (offset // 4, offset % 4):
        high = coordinate // 2
        both = jnp.bitwise_xor(high, coordinate % 2)
        first = 2 * first + jnp.where(core == 0, both, high)
        second = 2 * second + jnp.where(core == 0, high, both)
    return 4 * first + second


def phase_partners(phase, way):
    partners = []
    for device in range(VISITS):
        mask = phase_masks(device % 2)[phase]
        partners.append((device, device ^ (2 * (4 * mask * (way // 2) + mask * (way % 2)))))
    return partners


def exact_dot(left, right, sides=((1,), (0,))):
    return lax.dot_general(
        left, right, (sides, ((), ())), precision=lax.Precision.HIGHEST, preferred_element_type=f32
    )


def stacked_halves(value):
    high = value.astype(bf16).astype(f32)
    return jnp.concatenate([high, value - high], axis=0).astype(bf16)


def against_halves(matrix, halves_ref):
    rows = jnp.concatenate([halves_ref[...], halves_ref[:SPAN + 8, :]], axis=0)
    return jnp.dot(matrix, rows, preferred_element_type=f32)


def filter_bank():
    values = profiles_at(lax.broadcasted_iota(jnp.int32, (1, TILE), 1))
    scales = [1.0 / jnp.sqrt(jnp.sum(value * value, axis=1, keepdims=True)) for value in values]
    wide = [value * scale for value, scale in zip(values, scales)]
    tall = profiles_at(lax.broadcasted_iota(jnp.int32, (TAPS, TILE), 0))
    return wide, [value * scale for value, scale in zip(tall, scales)]


def kernel_spectrum(filters, which, table_ref, down_taps_ref, along_ref):
    wide, tall = filters
    mixed = [0.0] * NFILT
    for number, (first, second) in enumerate(filter_terms()):
        mixed[first] = mixed[first] + table_ref[number, which] * wide[second]
    kernel = 0.0
    for down, across in zip(tall, mixed):
        kernel = kernel + down * across
    high, low = split(kernel)
    half_way = jnp.dot(
        jnp.concatenate([high, low, high], axis=1), along_ref[...], preferred_element_type=f32
    )
    high = half_way.astype(bf16).astype(f32)
    rest = jnp.zeros((256 - 3 * TAPS, WIDTH), f32)
    half_way = jnp.concatenate([high, half_way - high, high, rest], axis=0).astype(bf16)
    both = jnp.dot(down_taps_ref[...], half_way, preferred_element_type=f32)
    return both[:SPAN], both[SPAN + 8:2 * SPAN + 8]


def match_kernel(
    place_ref, index_hbm, table_hbm, image_hbm, var_hbm, bits_hbm, owner_hbm, slot_hbm,
    across_hbm, down_hbm, back_down_hbm, back_across_hbm, down_taps_hbm, along_hbm,
    *rest, block,
):
    count = 4
    outs = rest[:count]
    (
        index_ref, table_ref, image_ref, var_ref, bits_ref, owner_ref, slot_ref,
        across_ref, down_ref, back_down_ref, back_across_ref, down_taps_ref, along_ref, sems,
        out_sems, tail_ref, high_ref, low_ref, wave_ref, stack_ref, turn_ref, result_ref, rows_ref,
        matched_ref, factor_ref, weight_ref, out_ref,
    ) = rest[count:]
    copies = [
        pltpu.make_async_copy(source, goal, sems.at[number])
        for number, (source, goal) in enumerate((
            (index_hbm, index_ref),
            (table_hbm, table_ref),
            (down_taps_hbm, down_taps_ref),
            (along_hbm, along_ref),
            (image_hbm.at[0, block], image_ref),
            (across_hbm, across_ref),
            (var_hbm.at[0], var_ref),
            (bits_hbm.at[0], bits_ref),
            (owner_hbm, owner_ref),
            (slot_hbm, slot_ref),
            (down_hbm, down_ref),
            (back_down_hbm, back_down_ref),
            (back_across_hbm, back_across_ref),
        ))
    ]
    for copy in copies:
        copy.start()
    tail_ref[...] = jnp.zeros_like(tail_ref)
    filters = filter_bank()
    spread = (
        lax.broadcasted_iota(jnp.int32, (CELLS, BLOCK), 1) // CELL
        == lax.broadcasted_iota(jnp.int32, (CELLS, BLOCK), 0)
    ).astype(f32)
    for copy in copies:
        copy.wait()

    pair = 2 * TILE
    forward = jnp.concatenate([across_ref[:pair], across_ref[...]], axis=0)
    backward = jnp.concatenate([back_across_ref[:pair], back_across_ref[...]], axis=0)
    spots = [way_to(place_ref[0], piece) for piece in range(CHIPS)]

    def windows(rows):
        tiles = [image_ref[rows, place:place + TILE] for place in range(0, BLOCK, TILE)]
        tiles.append(tail_ref[rows, :])
        lane = lax.broadcasted_iota(jnp.int32, tiles[0].shape, 1)
        second = [pltpu.roll(tile, 80, 1) for tile in tiles[1:4]]
        third = [pltpu.roll(tile, 32, 1) for tile in tiles[2:5]]
        return (
            tiles[:2],
            [jnp.where(lane < 80, second[spot], second[spot + 1]) for spot in range(2)],
            [jnp.where(lane < 32, third[spot], third[spot + 1]) for spot in range(2)],
        )

    def halve():
        tail_ref[:PADDED, :PADDED - BLOCK] = image_ref[:, BLOCK:]
        whole = TALL - 16
        for window, tiles in enumerate(windows(slice(0, whole))):
            for spot, tile in enumerate(tiles):
                lanes = slice(spot * TILE, (spot + 1) * TILE)
                high_ref[window, :whole, lanes], low_ref[window, :whole, lanes] = split(tile)
        for window, tiles in enumerate(windows(slice(whole, PADDED))):
            for spot, tile in enumerate(tiles):
                lanes = slice(spot * TILE, (spot + 1) * TILE)
                last = jnp.concatenate([tile, jnp.zeros((8, TILE), f32)], axis=0)
                high_ref[window, whole:, lanes], low_ref[window, whole:, lanes] = split(last)

    def transform_across(window):
        high, low = high_ref[window], low_ref[window]
        wave_ref[window] = jnp.dot(
            jnp.concatenate([high, low, high], axis=1), forward, preferred_element_type=f32
        )

    def prepare():
        same, cross = kernel_spectrum(
            filters, index_ref[0, block], table_ref, down_taps_ref, along_ref
        )
        factor_ref[0] = same.reshape(SPAN // 8, 8, pair)
        factor_ref[1] = cross.reshape(SPAN // 8, 8, pair)
        weight_ref[...] = exact_dot(cell_weights(var_ref[block], bits_ref[block]), spread)
        info = item_info(var_ref, bits_ref, owner_ref, slot_ref)
        out_ref[:, TILES_BLK] = jnp.broadcast_to(info[None], (CHIPS, INFO, TILE))

    def stack(tile):
        column, line = divmod(tile, SIDE)
        stack_ref[tile] = stacked_halves(wave_ref[column, line * TILE:line * TILE + SPAN, :])

    def transform_down(tile):
        turn_ref[tile] = against_halves(down_ref[...], stack_ref.at[tile])

    def multiply(tile):
        wave = turn_ref[tile, :SPAN].reshape(SPAN // 8, 8, pair)
        turned = pltpu.roll(wave, 4, 1)
        wave_c, wave_s = wave[..., :TILE], wave[..., TILE:]
        turned_c, turned_s = turned[..., :TILE], turned[..., TILE:]
        same_c, same_s = factor_ref[0, :, :, :TILE], factor_ref[0, :, :, TILE:]
        cross_c, cross_s = factor_ref[1, :, :, :TILE], factor_ref[1, :, :, TILE:]
        result_c = wave_c * same_c + turned_c * cross_c - wave_s * same_s - turned_s * cross_s
        result_s = wave_s * same_c + turned_s * cross_c + wave_c * same_s + turned_c * cross_s
        result = jnp.concatenate(
            [result_c.reshape(SPAN, TILE), result_s.reshape(SPAN, TILE)], axis=1
        )
        result_ref[tile] = stacked_halves(result)

    def back_down(tile):
        column, line = divmod(tile, SIDE)
        high, low = split(against_halves(back_down_ref[...], result_ref.at[tile]))
        rows_ref[column, line * TILE:(line + 1) * TILE, :pair] = high
        rows_ref[column, line * TILE:(line + 1) * TILE, pair:] = low

    def back_across(window):
        high, low = rows_ref[window, :, :pair], rows_ref[window, :, pair:]
        matched_ref[window] = jnp.dot(
            jnp.concatenate([high, low, high], axis=1), backward, preferred_element_type=f32
        )
        if window == 1:
            finish(0)
            finish(1)
        if window == 2:
            finish(2)
            finish(3)

    def finish(column):
        lane = lax.broadcasted_iota(jnp.int32, (BLOCK, TILE), 1)

        def part(window, spot, shift):
            value = matched_ref[window, :, spot * TILE:(spot + 1) * TILE]
            return pltpu.roll(value, shift, 1) if shift else value

        if column == 0:
            matched = part(0, 0, 0)
        elif column == 1:
            matched = jnp.where(lane < 48, part(0, 1, 0), part(1, 0, 48))
        elif column == 2:
            matched = jnp.where(lane < 96, part(1, 1, 48), part(2, 0, 96))
            matched = jnp.where(lane < 48, part(1, 0, 48), matched)
        else:
            matched = jnp.where(lane < 96, part(2, 0, 96), part(2, 1, 96))
        weight = weight_ref[:, column * TILE:(column + 1) * TILE]
        weighted = matched.reshape(CELLS, CELL, TILE) * weight[:, None, :]
        weighted = weighted.reshape(SIDE, CHIPS, PIECE, TILE)
        for line in range(SIDE):
            item = line * SIDE + column
            for piece in range(CHIPS):
                out_ref[spots[piece], item] = weighted[line, piece]

    halve()
    transform_across(0)
    prepare()
    tiles = WINDOWS * SIDE
    for step in range(tiles + 5):
        if step % SIDE == 0 and step // SIDE + 1 < WINDOWS:
            transform_across(step // SIDE + 1)
        for delay, stage in enumerate((stack, transform_down, multiply, back_down)):
            if 0 <= step - delay < tiles:
                stage(step - delay)
        column, rest = divmod(step - 4, SIDE)
        if rest == SIDE - 1 and 0 <= column < WINDOWS:
            back_across(column)
    each = CHIPS // count
    sends = [
        pltpu.make_async_copy(out_ref.at[way * each:(way + 1) * each], out_hbm, out_sems.at[way])
        for way, out_hbm in enumerate(outs)
    ]
    for send in reversed(sends):
        send.start()
    for send in sends:
        send.wait()


def match_block(block, place, exposures, variance, bits, table, index, owner, slot):
    blocks = exposures.shape[1]
    items = blocks * TILES_BLK
    groups = TILES_BLK + 1
    count = 4
    matrices = transforms()
    return pl.pallas_call(
        functools.partial(match_kernel, block=block),
        out_shape=[jax.ShapeDtypeStruct((CHIPS // count, groups, PIECE, TILE), f32)] * count,
        in_specs=[pl.BlockSpec(memory_space=pltpu.SMEM)]
        + [pl.BlockSpec(memory_space=pltpu.HBM)] * (7 + len(matrices)),
        out_specs=[pl.BlockSpec(memory_space=pltpu.HBM)] * count,
        scratch_shapes=[
            pltpu.SMEM((1, blocks), jnp.int32),
            pltpu.SMEM(table.shape, f32),
            pltpu.VMEM((PADDED, PADDED), f32),
            pltpu.VMEM((blocks, CELLS, CELLS), f32),
            pltpu.VMEM((blocks, CELLS, CELLS), jnp.int32),
            pltpu.VMEM((1, items), jnp.int32),
            pltpu.VMEM((1, items), jnp.int32),
            *[pltpu.VMEM(matrix.shape, matrix.dtype) for matrix in matrices],
            pltpu.SemaphoreType.DMA((7 + len(matrices),)),
            pltpu.SemaphoreType.DMA((4,)),
            pltpu.VMEM((TALL, TILE), f32),
            pltpu.VMEM((WINDOWS, TALL, WIDTH), bf16),
            pltpu.VMEM((WINDOWS, TALL, WIDTH), bf16),
            pltpu.VMEM((WINDOWS, TALL, WIDTH), f32),
            pltpu.VMEM((WINDOWS * SIDE, 2 * SPAN, WIDTH), bf16),
            pltpu.VMEM((WINDOWS * SIDE, SPAN + 8, WIDTH), f32),
            pltpu.VMEM((WINDOWS * SIDE, 2 * SPAN, WIDTH), bf16),
            pltpu.VMEM((WINDOWS, BLOCK, 2 * WIDTH), bf16),
            pltpu.VMEM((WINDOWS, BLOCK, WIDTH), f32),
            pltpu.VMEM((2, SPAN // 8, 8, 2 * TILE), f32),
            pltpu.VMEM((CELLS, BLOCK), f32),
            pltpu.VMEM((CHIPS, groups, PIECE, TILE), f32),
        ],
        compiler_params=pltpu.CompilerParams(vmem_limit_bytes=59 << 20),
        cost_estimate=pl.CostEstimate(
            flops=2 * 256 * 256 * 40000, bytes_accessed=3 << 20, transcendentals=0
        ),
        name="match_block",
    )(place, index, table, exposures, variance, bits, owner, slot, *matrices)


WAYS = (0, 3, 1, 2)


def keep_kernel(part_hbm, out_ref, sem):
    copy = pltpu.make_async_copy(part_hbm, out_ref, sem)
    copy.start()
    copy.wait()


def turn_kernel(*refs):
    for first, part_ref in zip(WAYS, refs[:4]):
        for second, out_ref in enumerate(refs[4:]):
            out_ref[first] = part_ref[second]


def partial_kernel(place_ref, *refs, block):
    part_refs, before, (mine_ref, other_ref) = refs[:4], refs[4:-2], refs[-2:]
    core = place_ref[0] % 2
    per_group = TILE // TILES_BLK
    lane = lax.broadcasted_iota(jnp.int32, (INFO, TILE), 1)
    info = [
        part_refs[source // 4][source % 4, TILES_BLK * PIECE:, :] for source in range(CHIPS)
    ]
    rows = []
    for m in range(PER_TILE):
        groups = []
        for group in range(CHIPS // per_group):
            total = None
            for member in range(per_group):
                goal = member * TILES_BLK
                shift = (goal - (m * 2 + block) * TILES_BLK) % TILE
                value = info[group * per_group + member]
                value = pltpu.roll(value, shift, 1) if shift else value
                here = (lane >= goal) & (lane < goal + TILES_BLK)
                total = value if total is None else jnp.where(here, value, total)
            groups.append(total)
        rows.append(jnp.concatenate(groups, axis=1))

    targets = VISITS * OWN_DEV
    owned = targets // 2
    items = CHIPS * TILES_BLK
    row = lax.broadcasted_iota(jnp.int32, (targets, items), 0)
    side = (row // owned + core) % 2
    inner = row % owned
    wanted = ((inner // OWN_DEV) * 2 + side) * OWN_DEV + inner % OWN_DEV
    target = rows[0][PER_TILE:PER_TILE + 1, :].astype(jnp.int32)
    route = jnp.where(wanted == target, 1.0, 0.0).astype(bf16)
    weights = jnp.concatenate(rows + [jnp.zeros((TILE - INFO * PER_TILE, items), f32)], axis=0)

    def store(spot, total):
        for number, goal_ref in enumerate((mine_ref, other_ref)):
            value = total[number * owned:(number + 1) * owned]
            goal_ref[spot, :] = value + before[number][spot, :] if before else value

    sums = 0.0
    for half in split(weights):
        sums = sums + lax.dot_general(
            route, half, (((1,), (1,)), ((), ())), preferred_element_type=f32
        )
    store(pl.ds(owned * PIECE, owned), sums)
    for line in range(PIECE):
        part = jnp.concatenate(
            [
                part_ref[:, pl.ds(line, TILES_BLK, PIECE), :].reshape(items // 4, TILE)
                for part_ref in part_refs
            ],
            axis=0,
        )
        high, low = split(part)
        total = jnp.dot(route, jnp.concatenate([high, low], axis=1), preferred_element_type=f32)
        store(pl.ds(line, owned, PIECE), total[:, :TILE] + total[:, TILE:])


def spread_cells(sums, cell_row):
    pattern = (
        lax.broadcasted_iota(jnp.int32, (TILE, TILE), 1) // CELL + cell_row * INFO
        == lax.broadcasted_iota(jnp.int32, (TILE, TILE), 0)
    ).astype(f32)
    return jnp.dot(sums, pattern, precision=lax.Precision.HIGHEST, preferred_element_type=f32)


def merge_kernel(place_ref, mine_ref, other_ref, out_ref):
    owned = VISITS * OWN_DEV // 2
    cell_row = (place_ref[0] // 2) // (CELL // PIECE)
    sums = mine_ref[owned * PIECE:, :] + other_ref[owned * PIECE:, :]
    scale = 1.0 / (spread_cells(sums, cell_row) + prior_weight)
    total = mine_ref[:owned * PIECE, :] + other_ref[:owned * PIECE, :]
    total = total.reshape(owned, PIECE, TILE) * scale[:, None, :]
    out_ref[...] = total.reshape(owned * PIECE, TILE)


def chi_kernel(place_ref, mine_ref, other_ref, part_ref, upper_ref, lower_ref):
    owned = VISITS * OWN_DEV // 2
    first = owned * PIECE + (place_ref[0] // 2) * OWN_DEV
    rows = pl.ds(pl.multiple_of(first, OWN_DEV), OWN_DEV)
    sums = mine_ref[rows, :] + other_ref[rows, :]
    per_cell = CELL // PIECE
    for m in range(PER_TILE):
        weight = spread_cells(sums, m) + prior_weight
        weight = jnp.broadcast_to(weight[:, None, :], (OWN_DEV, PIECE, TILE))
        part = part_ref[m * per_cell:(m + 1) * per_cell]
        chi_ref = upper_ref if m < PER_TILE // 2 else lower_ref
        place = m % (PER_TILE // 2) * per_cell
        chi_ref[place:place + per_cell] = part * part * weight.reshape(1, OWN_DEV * PIECE, TILE)


def image_kernel(part_ref, image_ref):
    for slot in range(OWN_DEV):
        rows = slice(slot * PIECE, (slot + 1) * PIECE)
        image_ref[slot] = part_ref[:, rows, :].reshape(TILE, TILE)


def detection_kernel(upper_ref, more_upper_ref, lower_ref, more_lower_ref, out_ref):
    for slot in range(OWN_DEV):
        rows = slice(slot * PIECE, (slot + 1) * PIECE)
        upper = upper_ref[:, rows, :] + more_upper_ref[:, rows, :]
        lower = lower_ref[:, rows, :] + more_lower_ref[:, rows, :]
        out_ref[slot, :TILE // 2] = upper.reshape(TILE // 2, TILE)
        out_ref[slot, TILE // 2:] = lower.reshape(TILE // 2, TILE)


def local(exposures, variance, mask_planes, kernel_table, kernel_index, tile_owner, tile_slot):
    place = lax.axis_index("visit").astype(jnp.int32).reshape(1)
    smem = pl.BlockSpec(memory_space=pltpu.SMEM)
    vmem = pl.BlockSpec(memory_space=pltpu.VMEM)
    params = pltpu.CompilerParams(vmem_limit_bytes=32 << 20)
    owned = VISITS * OWN_DEV // 2

    def exchange(parts):
        for phase in range(2):
            parts = [
                lax.ppermute(parts[way], "visit", phase_partners(phase, way)) if way else parts[0]
                for way in WAYS
            ]
            if phase == 0:
                parts = pl.pallas_call(
                    turn_kernel,
                    out_shape=[jax.ShapeDtypeStruct(parts[0].shape, f32)] * 4,
                    in_specs=[vmem] * 4,
                    out_specs=[vmem] * 4,
                    compiler_params=params,
                    name="turn",
                )(*parts)
        return parts

    table = kernel_table.T
    owner = tile_owner.reshape(tile_slot.shape)
    def spread_tiles(pieces):
        return lax.all_to_all(pieces, "visit", 0, 0, axis_index_groups=same_core, tiled=True)

    same_core = [list(range(core, VISITS, 2)) for core in range(2)]
    operands = (place, exposures, variance, mask_planes, table, kernel_index, owner, tile_slot)
    partial = ()
    for block in range(exposures.shape[1]):
        pieces = match_block(block, *operands)
        own = pl.pallas_call(
            keep_kernel,
            out_shape=jax.ShapeDtypeStruct(pieces[0].shape, f32),
            in_specs=[pl.BlockSpec(memory_space=pltpu.HBM)],
            out_specs=vmem,
            scratch_shapes=[pltpu.SemaphoreType.DMA],
            compiler_params=params,
            name="keep",
        )(pieces[0])
        parts = [part.reshape(4, -1, TILE) for part in exchange([own, *pieces[1:]])]
        partial = pl.pallas_call(
            functools.partial(partial_kernel, block=block),
            out_shape=[jax.ShapeDtypeStruct((owned * (PIECE + 1), TILE), f32)] * 2,
            in_specs=[smem] + [vmem] * (4 + len(partial)),
            out_specs=[vmem, vmem],
            compiler_params=params,
            name="partial_sums",
        )(place, *parts, *partial)
    mine, other = partial
    other = lax.ppermute(other, "visit", [(device, device ^ 1) for device in range(VISITS)])
    pieces = pl.pallas_call(
        merge_kernel,
        out_shape=jax.ShapeDtypeStruct((owned * PIECE, TILE), f32),
        in_specs=[smem, vmem, vmem],
        out_specs=vmem,
        compiler_params=params,
        name="merge_cores",
    )(place, mine, other)
    pieces = spread_tiles(pieces.reshape(CHIPS, OWN_DEV * PIECE, TILE))
    halves = pl.pallas_call(
        chi_kernel,
        out_shape=[jax.ShapeDtypeStruct((CHIPS // 2, OWN_DEV * PIECE, TILE), f32)] * 2,
        in_specs=[smem, vmem, vmem, vmem],
        out_specs=[vmem, vmem],
        compiler_params=params,
        name="chi",
    )(place, mine, other, pieces)
    tiles = jax.ShapeDtypeStruct((OWN_DEV, TILE, TILE), f32)
    image = pl.pallas_call(
        image_kernel,
        out_shape=tiles,
        in_specs=[vmem],
        out_specs=vmem,
        compiler_params=params,
        name="image",
    )(pieces)

    pairings = ([(0, 1), (1, 0), (2, 3), (3, 2)], [(0, 3), (3, 0), (1, 2), (2, 1)])
    halves = [
        half + lax.ppermute(half, "band", pairings[number]) for number, half in enumerate(halves)
    ]
    terms = []
    for number, half in enumerate(halves):
        terms.extend((half, lax.ppermute(half, "band", pairings[1 - number])))
    detection = pl.pallas_call(
        detection_kernel,
        out_shape=tiles,
        in_specs=[vmem] * 4,
        out_specs=vmem,
        compiler_params=params,
        name="detection",
    )(*terms)
    return image[None], detection


def solution(mesh):
    placed = (
        P("band", "visit", None, None),
        P("band", "visit", None, None),
        P("band", "visit", None, None),
        P(),
        P("band", "visit"),
        P("band", "visit", None),
        P("band", "visit"),
    )
    return jax.shard_map(
        local,
        mesh=mesh,
        in_specs=placed,
        out_specs=(P("band", "visit", None, None), P("visit", None, None)),
        check_vma=False,
    )
```

```python
import functools

import jax
import jax.numpy as jnp
import numpy as np
from jax import lax
from jax.experimental import pallas as pl
from jax.experimental.pallas import tpu as pltpu
from jax.sharding import PartitionSpec as P

BLOCK = 512
TILE = 128
CELL = 32
KSIZE = 41
OWN_DEV = 8
PADDED = BLOCK + KSIZE - 1
NFILT = 11
VISITS = 32
SIDE = BLOCK // TILE
CELLS = BLOCK // CELL
PER_TILE = TILE // CELL
TILES_BLK = SIDE * SIDE
CHIPS = VISITS // 2
PIECE = TILE // CHIPS
INFO = 8
SPAN = TILE + KSIZE - 1
HALF = SPAN // 2
TALL = 560
TAPS = 48
WIDTH = 256
KEPT = 176
WINDOWS = 3

width_fractions = (0.075, 0.15, 0.3)
family_degrees = (4, 2, 2)
prior_weight = 0.05
reject_planes = 3

f32 = jnp.float32
bf16 = jnp.bfloat16


def as_halves(matrix):
    high = matrix.astype(np.float32).astype(bf16)
    low = (matrix - high.astype(np.float64)).astype(np.float32).astype(bf16)
    return high, low


def waves(length):
    angle = 2 * np.pi * (np.arange(length // 2) + 0.5) / length
    phase = angle[:, None] * np.arange(length)
    return np.cos(phase), np.sin(phase)


def transforms():
    cosine, sine = waves(WIDTH)
    by_lane = np.concatenate([cosine, sine], axis=0)
    back_across = np.zeros((WIDTH, WIDTH))
    back_across[:, :KEPT] = by_lane[:, :KEPT] * (2 / WIDTH)
    along = np.zeros((TILE, WIDTH))
    along[:KSIZE] = np.concatenate([cosine, -sine], axis=0)[:, :KSIZE].T

    cosine, sine = waves(SPAN)
    number = np.arange(HALF)
    spot = 8 * (number // 4) + number % 4
    by_row = np.zeros((SPAN, SPAN))
    by_row[spot], by_row[spot + 4] = cosine, sine
    down = np.zeros((SPAN + 8, SPAN))
    down[:SPAN] = by_row
    back_down = by_row.T[:TILE] * (2 / SPAN)

    def three(matrix, width=512):
        high, low = as_halves(matrix)
        rest = np.zeros((matrix.shape[0], width - 3 * matrix.shape[1]), bf16)
        return np.concatenate([high, high, low, rest], axis=1)

    same = np.zeros((SPAN + 8, TAPS))
    cross = np.zeros((SPAN + 8, TAPS))
    same[spot, :KSIZE] = same[spot + 4, :KSIZE] = cosine[:, :KSIZE]
    cross[spot, :KSIZE], cross[spot + 4, :KSIZE] = sine[:, :KSIZE], -sine[:, :KSIZE]
    return (
        np.concatenate(as_halves(by_lane.T), axis=0),
        three(down),
        three(back_down),
        np.concatenate(as_halves(back_across), axis=0),
        np.concatenate([three(same, 256), three(cross, 256)], axis=0),
        np.concatenate([as_halves(along)[part] for part in (0, 0, 1)], axis=0),
    )


def filter_terms():
    starts = (0, 5, 8)
    terms = []
    for family in range(3):
        for first in range(family_degrees[family] + 1):
            for second in range(family_degrees[family] + 1 - first):
                terms.append((starts[family] + first, starts[family] + second))
    return terms


def profiles_at(offset):
    half_width = (KSIZE - 1) // 2
    inside = (offset >= 0) & (offset < KSIZE)
    taps = offset.astype(f32) - half_width
    values = []
    for family in range(3):
        scaled = taps / (width_fractions[family] * half_width)
        value = jnp.where(inside, jnp.exp(-0.5 * scaled * scaled), 0.0)
        for degree in range(family_degrees[family] + 1):
            values.append(value)
            value = value * scaled
    return values


def split(value):
    high = value.astype(bf16)
    return high, (value - high.astype(f32)).astype(bf16)


def cell_weights(variance, bits):
    usable = (jnp.bitwise_and(bits, reject_planes) != reject_planes).astype(f32)
    return usable / variance


def item_info(block, var_ref, bits_ref, owner_ref, slot_ref):
    exact = lax.Precision.HIGHEST
    lane = lax.broadcasted_iota(jnp.int32, (1, TILE), 1)
    row = lax.broadcasted_iota(jnp.int32, (CELLS, TILE), 0)
    item = lane % TILES_BLK
    cell_row = (item // SIDE) * PER_TILE + lane // (2 * TILES_BLK)
    picked = (row == cell_row).astype(f32)
    columns = lax.dot_general(
        cell_weights(var_ref[block], bits_ref[block]), picked,
        (((0,), (0,)), ((), ())), precision=exact, preferred_element_type=f32,
    )
    rows = []
    for n in range(PER_TILE):
        chosen = row == (item % SIDE) * PER_TILE + n
        rows.append(jnp.sum(jnp.where(chosen, columns, 0.0), axis=0, keepdims=True))
    target = (owner_ref[...] * OWN_DEV + slot_ref[...]).astype(f32)
    rows.append(jnp.concatenate([target, jnp.zeros((1, TILE - 2 * TILES_BLK), f32)], axis=1))
    rows.append(jnp.zeros((INFO - PER_TILE - 1, TILE), f32))
    return jnp.concatenate(rows, axis=0)


def phase_masks(core):
    return (1, 3) if core == 0 else (3, 1)


def way_to(place, piece):
    core, offset = place % 2, jnp.bitwise_xor(place // 2, piece)
    first, second = 0, 0
    for coordinate in (offset // 4, offset % 4):
        high = coordinate // 2
        both = jnp.bitwise_xor(high, coordinate % 2)
        first = 2 * first + jnp.where(core == 0, both, high)
        second = 2 * second + jnp.where(core == 0, high, both)
    return 4 * first + second


def phase_partners(phase, way):
    partners = []
    for device in range(VISITS):
        mask = phase_masks(device % 2)[phase]
        partners.append((device, device ^ (2 * (4 * mask * (way // 2) + mask * (way % 2)))))
    return partners


def exact_dot(left, right, sides=((1,), (0,))):
    return lax.dot_general(
        left, right, (sides, ((), ())), precision=lax.Precision.HIGHEST, preferred_element_type=f32
    )


def stacked_halves(value):
    high = value.astype(bf16).astype(f32)
    return jnp.concatenate([high, value - high], axis=0).astype(bf16)


def against_halves(matrix, halves_ref):
    rows = jnp.concatenate([halves_ref[...], halves_ref[:SPAN + 8, :]], axis=0)
    return jnp.dot(matrix, rows, preferred_element_type=f32)


def filter_bank():
    values = profiles_at(lax.broadcasted_iota(jnp.int32, (1, TILE), 1))
    scales = [1.0 / jnp.sqrt(jnp.sum(value * value, axis=1, keepdims=True)) for value in values]
    wide = [value * scale for value, scale in zip(values, scales)]
    tall = profiles_at(lax.broadcasted_iota(jnp.int32, (TAPS, TILE), 0))
    return wide, [value * scale for value, scale in zip(tall, scales)]


def kernel_spectrum(filters, which, table_ref, down_taps_ref, along_ref):
    wide, tall = filters
    mixed = [0.0] * NFILT
    for number, (first, second) in enumerate(filter_terms()):
        mixed[first] = mixed[first] + table_ref[number, which] * wide[second]
    kernel = 0.0
    for down, across in zip(tall, mixed):
        kernel = kernel + down * across
    high, low = split(kernel)
    half_way = jnp.dot(
        jnp.concatenate([high, low, high], axis=1), along_ref[...], preferred_element_type=f32
    )
    high = half_way.astype(bf16).astype(f32)
    rest = jnp.zeros((256 - 3 * TAPS, WIDTH), f32)
    half_way = jnp.concatenate([high, half_way - high, high, rest], axis=0).astype(bf16)
    both = jnp.dot(down_taps_ref[...], half_way, preferred_element_type=f32)
    return both[:SPAN], both[SPAN + 8:2 * SPAN + 8]


def match_kernel(
    place_ref, index_hbm, table_hbm, image_hbm, var_hbm, bits_hbm, owner_hbm, slot_hbm,
    across_hbm, down_hbm, back_down_hbm, back_across_hbm, down_taps_hbm, along_hbm,
    *rest, block,
):
    count = 4
    outs = rest[:count]
    (
        index_ref, table_ref, image_ref, var_ref, bits_ref, owner_ref, slot_ref,
        across_ref, down_ref, back_down_ref, back_across_ref, down_taps_ref, along_ref, sems,
        out_sems, tail_ref, high_ref, low_ref, wave_ref, stack_ref, turn_ref, result_ref, rows_ref,
        matched_ref, factor_ref, weight_ref, out_ref,
    ) = rest[count:]
    copies = [
        pltpu.make_async_copy(source, goal, sems.at[number])
        for number, (source, goal) in enumerate((
            (index_hbm, index_ref),
            (table_hbm, table_ref),
            (down_taps_hbm, down_taps_ref),
            (along_hbm, along_ref),
            (image_hbm.at[0, block], image_ref),
            (across_hbm, across_ref),
            (var_hbm.at[0], var_ref),
            (bits_hbm.at[0], bits_ref),
            (owner_hbm, owner_ref),
            (slot_hbm, slot_ref),
            (down_hbm, down_ref),
            (back_down_hbm, back_down_ref),
            (back_across_hbm, back_across_ref),
        ))
    ]
    for copy in copies:
        copy.start()
    tail_ref[...] = jnp.zeros_like(tail_ref)
    filters = filter_bank()
    spread = (
        lax.broadcasted_iota(jnp.int32, (CELLS, BLOCK), 1) // CELL
        == lax.broadcasted_iota(jnp.int32, (CELLS, BLOCK), 0)
    ).astype(f32)
    for copy in copies:
        copy.wait()

    pair = 2 * TILE
    forward = jnp.concatenate([across_ref[:pair], across_ref[...]], axis=0)
    backward = jnp.concatenate([back_across_ref[:pair], back_across_ref[...]], axis=0)
    spots = [way_to(place_ref[0], piece) for piece in range(CHIPS)]

    def window_of(window, rows):
        first, shift = ((0, 0), (1, 80), (2, 32))[window]
        tiles = []
        for spot in range(first, first + (3 if shift else 2)):
            tile = tail_ref[rows, :] if spot == SIDE else image_ref[rows, spot * TILE:(spot + 1) * TILE]
            tiles.append(pltpu.roll(tile, shift, 1) if shift else tile)
        if not shift:
            return tiles
        lane = lax.broadcasted_iota(jnp.int32, tiles[0].shape, 1)
        return [jnp.where(lane < shift, tiles[spot], tiles[spot + 1]) for spot in range(2)]

    def halve(window):
        if window == WINDOWS - 1:
            tail_ref[:PADDED, :PADDED - BLOCK] = image_ref[:, BLOCK:]
        whole = TALL - 16
        for spot, tile in enumerate(window_of(window, slice(0, whole))):
            lanes = slice(spot * TILE, (spot + 1) * TILE)
            high_ref[window, :whole, lanes], low_ref[window, :whole, lanes] = split(tile)
        for spot, tile in enumerate(window_of(window, slice(whole, PADDED))):
            lanes = slice(spot * TILE, (spot + 1) * TILE)
            last = jnp.concatenate([tile, jnp.zeros((8, TILE), f32)], axis=0)
            high_ref[window, whole:, lanes], low_ref[window, whole:, lanes] = split(last)

    def transform_across(window):
        high, low = high_ref[window], low_ref[window]
        wave_ref[window] = jnp.dot(
            jnp.concatenate([high, low, high], axis=1), forward, preferred_element_type=f32
        )

    def prepare():
        same, cross = kernel_spectrum(
            filters, index_ref[0, block], table_ref, down_taps_ref, along_ref
        )
        factor_ref[0] = same.reshape(SPAN // 8, 8, pair)
        factor_ref[1] = cross.reshape(SPAN // 8, 8, pair)
        weight_ref[...] = exact_dot(cell_weights(var_ref[block], bits_ref[block]), spread)
        info = item_info(block, var_ref, bits_ref, owner_ref, slot_ref)
        out_ref[:, TILES_BLK] = jnp.broadcast_to(info[None], (CHIPS, INFO, TILE))

    def stack(tile):
        column, line = divmod(tile, SIDE)
        stack_ref[tile] = stacked_halves(wave_ref[column, line * TILE:line * TILE + SPAN, :])

    def transform_down(tile):
        turn_ref[tile] = against_halves(down_ref[...], stack_ref.at[tile])

    def multiply(tile):
        wave = turn_ref[tile, :SPAN].reshape(SPAN // 8, 8, pair)
        turned = pltpu.roll(wave, 4, 1)
        wave_c, wave_s = wave[..., :TILE], wave[..., TILE:]
        turned_c, turned_s = turned[..., :TILE], turned[..., TILE:]
        same_c, same_s = factor_ref[0, :, :, :TILE], factor_ref[0, :, :, TILE:]
        cross_c, cross_s = factor_ref[1, :, :, :TILE], factor_ref[1, :, :, TILE:]
        result_c = wave_c * same_c + turned_c * cross_c - wave_s * same_s - turned_s * cross_s
        result_s = wave_s * same_c + turned_s * cross_c + wave_c * same_s + turned_c * cross_s
        result = jnp.concatenate(
            [result_c.reshape(SPAN, TILE), result_s.reshape(SPAN, TILE)], axis=1
        )
        result_ref[tile] = stacked_halves(result)

    def back_down(tile):
        column, line = divmod(tile, SIDE)
        high, low = split(against_halves(back_down_ref[...], result_ref.at[tile]))
        rows_ref[column, line * TILE:(line + 1) * TILE, :pair] = high
        rows_ref[column, line * TILE:(line + 1) * TILE, pair:] = low

    def back_across(window):
        high, low = rows_ref[window, :, :pair], rows_ref[window, :, pair:]
        matched_ref[window] = jnp.dot(
            jnp.concatenate([high, low, high], axis=1), backward, preferred_element_type=f32
        )
        if window == 1:
            finish(0)
            finish(1)
        if window == 2:
            finish(2)
            finish(3)

    def finish(column):
        lane = lax.broadcasted_iota(jnp.int32, (BLOCK, TILE), 1)

        def part(window, spot, shift):
            value = matched_ref[window, :, spot * TILE:(spot + 1) * TILE]
            return pltpu.roll(value, shift, 1) if shift else value

        if column == 0:
            matched = part(0, 0, 0)
        elif column == 1:
            matched = jnp.where(lane < 48, part(0, 1, 0), part(1, 0, 48))
        elif column == 2:
            matched = jnp.where(lane < 96, part(1, 1, 48), part(2, 0, 96))
            matched = jnp.where(lane < 48, part(1, 0, 48), matched)
        else:
            matched = jnp.where(lane < 96, part(2, 0, 96), part(2, 1, 96))
        weight = weight_ref[:, column * TILE:(column + 1) * TILE]
        weighted = matched.reshape(CELLS, CELL, TILE) * weight[:, None, :]
        weighted = weighted.reshape(SIDE, CHIPS, PIECE, TILE)
        for line in range(SIDE):
            item = line * SIDE + column
            for piece in range(CHIPS):
                out_ref[spots[piece], item] = weighted[line, piece]

    halve(0)
    transform_across(0)
    prepare()
    halve(1)
    halve(2)
    tiles = WINDOWS * SIDE
    for step in range(tiles + 5):
        if step % SIDE == 0 and step // SIDE + 1 < WINDOWS:
            transform_across(step // SIDE + 1)
        for delay, stage in enumerate((stack, transform_down, multiply, back_down)):
            if 0 <= step - delay < tiles:
                stage(step - delay)
        column, rest = divmod(step - 4, SIDE)
        if rest == SIDE - 1 and 0 <= column < WINDOWS:
            back_across(column)
    each = CHIPS // count
    sends = [
        pltpu.make_async_copy(out_ref.at[way * each:(way + 1) * each], out_hbm, out_sems.at[way])
        for way, out_hbm in enumerate(outs)
    ]
    for send in reversed(sends):
        send.start()
    for send in sends:
        send.wait()


def match_block(block, place, exposures, variance, bits, table, index, owner, slot):
    blocks = exposures.shape[1]
    items = blocks * TILES_BLK
    groups = TILES_BLK + 1
    count = 4
    matrices = transforms()
    return pl.pallas_call(
        functools.partial(match_kernel, block=block),
        out_shape=[jax.ShapeDtypeStruct((CHIPS // count, groups, PIECE, TILE), f32)] * count,
        in_specs=[pl.BlockSpec(memory_space=pltpu.SMEM)]
        + [pl.BlockSpec(memory_space=pltpu.HBM)] * (7 + len(matrices)),
        out_specs=[pl.BlockSpec(memory_space=pltpu.HBM)] * count,
        scratch_shapes=[
            pltpu.SMEM((1, blocks), jnp.int32),
            pltpu.SMEM(table.shape, f32),
            pltpu.VMEM((PADDED, PADDED), f32),
            pltpu.VMEM((blocks, CELLS, CELLS), f32),
            pltpu.VMEM((blocks, CELLS, CELLS), jnp.int32),
            pltpu.VMEM((1, items), jnp.int32),
            pltpu.VMEM((1, items), jnp.int32),
            *[pltpu.VMEM(matrix.shape, matrix.dtype) for matrix in matrices],
            pltpu.SemaphoreType.DMA((7 + len(matrices),)),
            pltpu.SemaphoreType.DMA((4,)),
            pltpu.VMEM((TALL, TILE), f32),
            pltpu.VMEM((WINDOWS, TALL, WIDTH), bf16),
            pltpu.VMEM((WINDOWS, TALL, WIDTH), bf16),
            pltpu.VMEM((WINDOWS, TALL, WIDTH), f32),
            pltpu.VMEM((WINDOWS * SIDE, 2 * SPAN, WIDTH), bf16),
            pltpu.VMEM((WINDOWS * SIDE, SPAN + 8, WIDTH), f32),
            pltpu.VMEM((WINDOWS * SIDE, 2 * SPAN, WIDTH), bf16),
            pltpu.VMEM((WINDOWS, BLOCK, 2 * WIDTH), bf16),
            pltpu.VMEM((WINDOWS, BLOCK, WIDTH), f32),
            pltpu.VMEM((2, SPAN // 8, 8, 2 * TILE), f32),
            pltpu.VMEM((CELLS, BLOCK), f32),
            pltpu.VMEM((CHIPS, groups, PIECE, TILE), f32),
        ],
        compiler_params=pltpu.CompilerParams(vmem_limit_bytes=59 << 20),
        cost_estimate=pl.CostEstimate(
            flops=2 * 256 * 256 * 40000, bytes_accessed=3 << 20, transcendentals=0
        ),
        name="match_block",
    )(place, index, table, exposures, variance, bits, owner, slot, *matrices)


WAYS = (0, 3, 1, 2)


def keep_kernel(part_hbm, out_ref, sem):
    copy = pltpu.make_async_copy(part_hbm, out_ref, sem)
    copy.start()
    copy.wait()


def turn_kernel(*refs):
    for first, part_ref in zip(WAYS, refs[:4]):
        for second, out_ref in enumerate(refs[4:]):
            out_ref[first] = part_ref[second]


def partial_kernel(place_ref, *refs, block):
    part_refs, before, (mine_ref, other_ref) = refs[:4], refs[4:-2], refs[-2:]
    core = place_ref[0] % 2
    per_group = TILE // TILES_BLK
    lane = lax.broadcasted_iota(jnp.int32, (INFO, TILE), 1)
    info = [
        part_refs[source // 4][source % 4, TILES_BLK * PIECE:, :] for source in range(CHIPS)
    ]
    rows = []
    for m in range(PER_TILE):
        groups = []
        for group in range(CHIPS // per_group):
            total = None
            for member in range(per_group):
                goal = member * TILES_BLK
                shift = (goal - (m * 2 + block) * TILES_BLK) % TILE
                value = info[group * per_group + member]
                value = pltpu.roll(value, shift, 1) if shift else value
                here = (lane >= goal) & (lane < goal + TILES_BLK)
                total = value if total is None else jnp.where(here, value, total)
            groups.append(total)
        rows.append(jnp.concatenate(groups, axis=1))

    targets = VISITS * OWN_DEV
    owned = targets // 2
    items = CHIPS * TILES_BLK
    row = lax.broadcasted_iota(jnp.int32, (targets, items), 0)
    side = (row // owned + core) % 2
    inner = row % owned
    wanted = ((inner // OWN_DEV) * 2 + side) * OWN_DEV + inner % OWN_DEV
    target = rows[0][PER_TILE:PER_TILE + 1, :].astype(jnp.int32)
    route = jnp.where(wanted == target, 1.0, 0.0).astype(bf16)
    weights = jnp.concatenate(rows + [jnp.zeros((TILE - INFO * PER_TILE, items), f32)], axis=0)

    def store(spot, total):
        for number, goal_ref in enumerate((mine_ref, other_ref)):
            value = total[number * owned:(number + 1) * owned]
            goal_ref[spot, :] = value + before[number][spot, :] if before else value

    sums = 0.0
    for half in split(weights):
        sums = sums + lax.dot_general(
            route, half, (((1,), (1,)), ((), ())), preferred_element_type=f32
        )
    store(pl.ds(owned * PIECE, owned), sums)
    for line in range(PIECE):
        part = jnp.concatenate(
            [
                part_ref[:, pl.ds(line, TILES_BLK, PIECE), :].reshape(items // 4, TILE)
                for part_ref in part_refs
            ],
            axis=0,
        )
        high, low = split(part)
        total = jnp.dot(route, jnp.concatenate([high, low], axis=1), preferred_element_type=f32)
        store(pl.ds(line, owned, PIECE), total[:, :TILE] + total[:, TILE:])


def spread_cells(sums, cell_row):
    pattern = (
        lax.broadcasted_iota(jnp.int32, (TILE, TILE), 1) // CELL + cell_row * INFO
        == lax.broadcasted_iota(jnp.int32, (TILE, TILE), 0)
    ).astype(f32)
    return jnp.dot(sums, pattern, precision=lax.Precision.HIGHEST, preferred_element_type=f32)


def merge_kernel(place_ref, mine_ref, other_ref, out_ref):
    owned = VISITS * OWN_DEV // 2
    cell_row = (place_ref[0] // 2) // (CELL // PIECE)
    sums = mine_ref[owned * PIECE:, :] + other_ref[owned * PIECE:, :]
    scale = 1.0 / (spread_cells(sums, cell_row) + prior_weight)
    total = mine_ref[:owned * PIECE, :] + other_ref[:owned * PIECE, :]
    total = total.reshape(owned, PIECE, TILE) * scale[:, None, :]
    out_ref[...] = total.reshape(owned * PIECE, TILE)


def chi_kernel(place_ref, mine_ref, other_ref, part_ref, upper_ref, lower_ref):
    owned = VISITS * OWN_DEV // 2
    first = owned * PIECE + (place_ref[0] // 2) * OWN_DEV
    rows = pl.ds(pl.multiple_of(first, OWN_DEV), OWN_DEV)
    sums = mine_ref[rows, :] + other_ref[rows, :]
    per_cell = CELL // PIECE
    for m in range(PER_TILE):
        weight = spread_cells(sums, m) + prior_weight
        weight = jnp.broadcast_to(weight[:, None, :], (OWN_DEV, PIECE, TILE))
        part = part_ref[m * per_cell:(m + 1) * per_cell]
        chi_ref = upper_ref if m < PER_TILE // 2 else lower_ref
        place = m % (PER_TILE // 2) * per_cell
        chi_ref[place:place + per_cell] = part * part * weight.reshape(1, OWN_DEV * PIECE, TILE)


def image_kernel(part_ref, image_ref):
    for slot in range(OWN_DEV):
        rows = slice(slot * PIECE, (slot + 1) * PIECE)
        image_ref[slot] = part_ref[:, rows, :].reshape(TILE, TILE)


def detection_kernel(upper_ref, more_upper_ref, lower_ref, more_lower_ref, out_ref):
    for slot in range(OWN_DEV):
        rows = slice(slot * PIECE, (slot + 1) * PIECE)
        upper = upper_ref[:, rows, :] + more_upper_ref[:, rows, :]
        lower = lower_ref[:, rows, :] + more_lower_ref[:, rows, :]
        out_ref[slot, :TILE // 2] = upper.reshape(TILE // 2, TILE)
        out_ref[slot, TILE // 2:] = lower.reshape(TILE // 2, TILE)


def local(exposures, variance, mask_planes, kernel_table, kernel_index, tile_owner, tile_slot):
    place = lax.axis_index("visit").astype(jnp.int32).reshape(1)
    smem = pl.BlockSpec(memory_space=pltpu.SMEM)
    vmem = pl.BlockSpec(memory_space=pltpu.VMEM)
    params = pltpu.CompilerParams(vmem_limit_bytes=32 << 20)
    owned = VISITS * OWN_DEV // 2

    def exchange(parts):
        for phase in range(2):
            parts = [
                lax.ppermute(parts[way], "visit", phase_partners(phase, way)) if way else parts[0]
                for way in WAYS
            ]
            if phase == 0:
                parts = pl.pallas_call(
                    turn_kernel,
                    out_shape=[jax.ShapeDtypeStruct(parts[0].shape, f32)] * 4,
                    in_specs=[vmem] * 4,
                    out_specs=[vmem] * 4,
                    compiler_params=params,
                    name="turn",
                )(*parts)
        return parts

    table = kernel_table.T
    owner = tile_owner.reshape(tile_slot.shape)
    def spread_tiles(pieces):
        return lax.all_to_all(pieces, "visit", 0, 0, axis_index_groups=same_core, tiled=True)

    same_core = [list(range(core, VISITS, 2)) for core in range(2)]
    operands = (place, exposures, variance, mask_planes, table, kernel_index, owner, tile_slot)
    partial = ()
    for block in range(exposures.shape[1]):
        pieces = match_block(block, *operands)
        own = pl.pallas_call(
            keep_kernel,
            out_shape=jax.ShapeDtypeStruct(pieces[0].shape, f32),
            in_specs=[pl.BlockSpec(memory_space=pltpu.HBM)],
            out_specs=vmem,
            scratch_shapes=[pltpu.SemaphoreType.DMA],
            compiler_params=params,
            name="keep",
        )(pieces[0])
        parts = [part.reshape(4, -1, TILE) for part in exchange([own, *pieces[1:]])]
        partial = pl.pallas_call(
            functools.partial(partial_kernel, block=block),
            out_shape=[jax.ShapeDtypeStruct((owned * (PIECE + 1), TILE), f32)] * 2,
            in_specs=[smem] + [vmem] * (4 + len(partial)),
            out_specs=[vmem, vmem],
            compiler_params=params,
            name="partial_sums",
        )(place, *parts, *partial)
    mine, other = partial
    other = lax.ppermute(other, "visit", [(device, device ^ 1) for device in range(VISITS)])
    pieces = pl.pallas_call(
        merge_kernel,
        out_shape=jax.ShapeDtypeStruct((owned * PIECE, TILE), f32),
        in_specs=[smem, vmem, vmem],
        out_specs=vmem,
        compiler_params=params,
        name="merge_cores",
    )(place, mine, other)
    pieces = spread_tiles(pieces.reshape(CHIPS, OWN_DEV * PIECE, TILE))
    halves = pl.pallas_call(
        chi_kernel,
        out_shape=[jax.ShapeDtypeStruct((CHIPS // 2, OWN_DEV * PIECE, TILE), f32)] * 2,
        in_specs=[smem, vmem, vmem, vmem],
        out_specs=[vmem, vmem],
        compiler_params=params,
        name="chi",
    )(place, mine, other, pieces)
    tiles = jax.ShapeDtypeStruct((OWN_DEV, TILE, TILE), f32)
    image = pl.pallas_call(
        image_kernel,
        out_shape=tiles,
        in_specs=[vmem],
        out_specs=vmem,
        compiler_params=params,
        name="image",
    )(pieces)

    pairings = ([(0, 1), (1, 0), (2, 3), (3, 2)], [(0, 3), (3, 0), (1, 2), (2, 1)])
    halves = [
        half + lax.ppermute(half, "band", pairings[number]) for number, half in enumerate(halves)
    ]
    terms = []
    for number, half in enumerate(halves):
        terms.extend((half, lax.ppermute(half, "band", pairings[1 - number])))
    detection = pl.pallas_call(
        detection_kernel,
        out_shape=tiles,
        in_specs=[vmem] * 4,
        out_specs=vmem,
        compiler_params=params,
        name="detection",
    )(*terms)
    return image[None], detection


def solution(mesh):
    placed = (
        P("band", "visit", None, None),
        P("band", "visit", None, None),
        P("band", "visit", None, None),
        P(),
        P("band", "visit"),
        P("band", "visit", None),
        P("band", "visit"),
    )
    return jax.shard_map(
        local,
        mesh=mesh,
        in_specs=placed,
        out_specs=(P("band", "visit", None, None), P("visit", None, None)),
        check_vma=False,
    )
```

```python
import functools

import jax
import jax.numpy as jnp
import numpy as np
from jax import lax
from jax.experimental import pallas as pl
from jax.experimental.pallas import tpu as pltpu
from jax.sharding import PartitionSpec as P

BLOCK = 512
TILE = 128
CELL = 32
KSIZE = 41
OWN_DEV = 8
PADDED = BLOCK + KSIZE - 1
NFILT = 11
VISITS = 32
SIDE = BLOCK // TILE
CELLS = BLOCK // CELL
PER_TILE = TILE // CELL
TILES_BLK = SIDE * SIDE
CHIPS = VISITS // 2
PIECE = TILE // CHIPS
INFO = 8
SPAN = TILE + KSIZE - 1
HALF = SPAN // 2
TALL = 560
TAPS = 48
WIDTH = 256
KEPT = 176
WINDOWS = 3

width_fractions = (0.075, 0.15, 0.3)
family_degrees = (4, 2, 2)
prior_weight = 0.05
reject_planes = 3

f32 = jnp.float32
bf16 = jnp.bfloat16


def as_halves(matrix):
    high = matrix.astype(np.float32).astype(bf16)
    low = (matrix - high.astype(np.float64)).astype(np.float32).astype(bf16)
    return high, low


def waves(length):
    angle = 2 * np.pi * (np.arange(length // 2) + 0.5) / length
    phase = angle[:, None] * np.arange(length)
    return np.cos(phase), np.sin(phase)


def transforms():
    cosine, sine = waves(WIDTH)
    by_lane = np.concatenate([cosine, sine], axis=0)
    back_across = np.zeros((WIDTH, WIDTH))
    back_across[:, :KEPT] = by_lane[:, :KEPT] * (2 / WIDTH)
    along = np.zeros((TILE, WIDTH))
    along[:KSIZE] = np.concatenate([cosine, -sine], axis=0)[:, :KSIZE].T

    cosine, sine = waves(SPAN)
    number = np.arange(HALF)
    spot = 8 * (number // 4) + number % 4
    by_row = np.zeros((SPAN, SPAN))
    by_row[spot], by_row[spot + 4] = cosine, sine
    down = np.zeros((SPAN + 8, SPAN))
    down[:SPAN] = by_row
    back_down = by_row.T[:TILE] * (2 / SPAN)

    def three(matrix, width):
        high, low = as_halves(matrix)
        rest = np.zeros((matrix.shape[0], width - 3 * matrix.shape[1]), bf16)
        return np.concatenate([high, high, low, rest], axis=1)

    same = np.zeros((SPAN + 8, TAPS))
    cross = np.zeros((SPAN + 8, TAPS))
    same[spot, :KSIZE] = same[spot + 4, :KSIZE] = cosine[:, :KSIZE]
    cross[spot, :KSIZE], cross[spot + 4, :KSIZE] = sine[:, :KSIZE], -sine[:, :KSIZE]
    def against(matrix):
        high, low = as_halves(matrix)
        zeros = np.zeros((matrix.shape[0], 8), bf16)
        return np.concatenate([high, low[:, SPAN - 8:], high, zeros, low[:, :SPAN - 8]], axis=1)

    return (
        np.concatenate(as_halves(by_lane.T), axis=0),
        against(down),
        against(back_down),
        np.concatenate(as_halves(back_across), axis=0),
        np.concatenate([three(same, 256), three(cross, 256)], axis=0),
        np.concatenate([as_halves(along)[part] for part in (0, 0, 1)], axis=0),
    )


def filter_terms():
    starts = (0, 5, 8)
    terms = []
    for family in range(3):
        for first in range(family_degrees[family] + 1):
            for second in range(family_degrees[family] + 1 - first):
                terms.append((starts[family] + first, starts[family] + second))
    return terms


def profiles_at(offset):
    half_width = (KSIZE - 1) // 2
    inside = (offset >= 0) & (offset < KSIZE)
    taps = offset.astype(f32) - half_width
    values = []
    for family in range(3):
        scaled = taps / (width_fractions[family] * half_width)
        value = jnp.where(inside, jnp.exp(-0.5 * scaled * scaled), 0.0)
        for degree in range(family_degrees[family] + 1):
            values.append(value)
            value = value * scaled
    return values


def split(value):
    high = value.astype(bf16)
    return high, (value - high.astype(f32)).astype(bf16)


def cell_weights(variance, bits):
    usable = (jnp.bitwise_and(bits, reject_planes) != reject_planes).astype(f32)
    return usable / variance


def item_info(var_ref, bits_ref, owner_ref, slot_ref):
    exact = lax.Precision.HIGHEST
    lane = lax.broadcasted_iota(jnp.int32, (1, TILE), 1)
    row = lax.broadcasted_iota(jnp.int32, (CELLS, TILE), 0)
    item = lane % TILES_BLK
    cell_row = (item // SIDE) * PER_TILE + lane // (2 * TILES_BLK)
    columns = None
    for block in range(2):
        picked = ((row == cell_row) & ((lane // TILES_BLK) % 2 == block)).astype(f32)
        term = lax.dot_general(
            cell_weights(var_ref[block], bits_ref[block]), picked,
            (((0,), (0,)), ((), ())), precision=exact, preferred_element_type=f32,
        )
        columns = term if columns is None else columns + term
    rows = []
    for n in range(PER_TILE):
        chosen = row == (item % SIDE) * PER_TILE + n
        rows.append(jnp.sum(jnp.where(chosen, columns, 0.0), axis=0, keepdims=True))
    target = (owner_ref[...] * OWN_DEV + slot_ref[...]).astype(f32)
    rows.append(jnp.concatenate([target, jnp.zeros((1, TILE - 2 * TILES_BLK), f32)], axis=1))
    rows.append(jnp.zeros((INFO - PER_TILE - 1, TILE), f32))
    return jnp.concatenate(rows, axis=0)


def phase_masks(core):
    return (1, 3) if core == 0 else (3, 1)


def way_to(place, piece):
    core, offset = place % 2, jnp.bitwise_xor(place // 2, piece)
    first, second = 0, 0
    for coordinate in (offset // 4, offset % 4):
        high = coordinate // 2
        both = jnp.bitwise_xor(high, coordinate % 2)
        first = 2 * first + jnp.where(core == 0, both, high)
        second = 2 * second + jnp.where(core == 0, high, both)
    return 4 * first + second


def phase_partners(phase, way):
    partners = []
    for device in range(VISITS):
        mask = phase_masks(device % 2)[phase]
        partners.append((device, device ^ (2 * (4 * mask * (way // 2) + mask * (way % 2)))))
    return partners


def exact_dot(left, right, sides=((1,), (0,))):
    return lax.dot_general(
        left, right, (sides, ((), ())), precision=lax.Precision.HIGHEST, preferred_element_type=f32
    )


def store_halves(halves_ref, tile, first, value):
    high = value.astype(bf16).astype(f32)
    low = value - high
    if value.shape[0] < 16:
        high = jnp.concatenate([high, high], axis=0)
        low = jnp.concatenate([low, jnp.zeros_like(low)], axis=0)
    halves_ref[tile, first:first + 16, :] = high.astype(bf16)
    halves_ref[tile, SPAN + 8 + first:SPAN + 8 + first + 16, :] = low.astype(bf16)


def against_halves(matrix, halves_ref):
    rows = jnp.concatenate([halves_ref[...], halves_ref[:SPAN - 8, :]], axis=0)
    return jnp.dot(matrix, rows, preferred_element_type=f32)


def filter_bank():
    values = profiles_at(lax.broadcasted_iota(jnp.int32, (1, TILE), 1))
    scales = [1.0 / jnp.sqrt(jnp.sum(value * value, axis=1, keepdims=True)) for value in values]
    wide = [value * scale for value, scale in zip(values, scales)]
    tall = profiles_at(lax.broadcasted_iota(jnp.int32, (TAPS, TILE), 0))
    return wide, [value * scale for value, scale in zip(tall, scales)]


def kernel_spectrum(filters, which, table_ref, down_taps_ref, along_ref):
    wide, tall = filters
    mixed = [0.0] * NFILT
    for number, (first, second) in enumerate(filter_terms()):
        mixed[first] = mixed[first] + table_ref[number, which] * wide[second]
    kernel = 0.0
    for down, across in zip(tall, mixed):
        kernel = kernel + down * across
    high, low = split(kernel)
    half_way = jnp.dot(
        jnp.concatenate([high, low, high], axis=1), along_ref[...], preferred_element_type=f32
    )
    high = half_way.astype(bf16).astype(f32)
    rest = jnp.zeros((256 - 3 * TAPS, WIDTH), f32)
    half_way = jnp.concatenate([high, half_way - high, high, rest], axis=0).astype(bf16)
    both = jnp.dot(down_taps_ref[...], half_way, preferred_element_type=f32)
    return both[:SPAN], both[SPAN + 8:2 * SPAN + 8]


def match_kernel(
    place_ref, index_hbm, table_hbm, image_hbm, var_hbm, bits_hbm, owner_hbm, slot_hbm,
    across_hbm, down_hbm, back_down_hbm, back_across_hbm, down_taps_hbm, along_hbm,
    *rest, block,
):
    count = 4
    outs = rest[:count]
    (
        index_ref, table_ref, image_ref, var_ref, bits_ref, owner_ref, slot_ref,
        across_ref, down_ref, back_down_ref, back_across_ref, down_taps_ref, along_ref, sems,
        out_sems, tail_ref, high_ref, low_ref, wave_ref, stack_ref, turn_ref, result_ref, rows_ref,
        matched_ref, factor_ref, weight_ref, out_ref,
    ) = rest[count:]
    copies = [
        pltpu.make_async_copy(source, goal, sems.at[number])
        for number, (source, goal) in enumerate((
            (index_hbm, index_ref),
            (table_hbm, table_ref),
            (down_taps_hbm, down_taps_ref),
            (along_hbm, along_ref),
            (image_hbm.at[0, block], image_ref),
            (across_hbm, across_ref),
            (var_hbm.at[0], var_ref),
            (bits_hbm.at[0], bits_ref),
            (owner_hbm, owner_ref),
            (slot_hbm, slot_ref),
            (down_hbm, down_ref),
            (back_down_hbm, back_down_ref),
            (back_across_hbm, back_across_ref),
        ))
    ]
    for copy in copies:
        copy.start()
    tail_ref[...] = jnp.zeros_like(tail_ref)
    filters = filter_bank()
    spread = (
        lax.broadcasted_iota(jnp.int32, (CELLS, BLOCK), 1) // CELL
        == lax.broadcasted_iota(jnp.int32, (CELLS, BLOCK), 0)
    ).astype(f32)
    for copy in copies:
        copy.wait()

    pair = 2 * TILE
    forward = jnp.concatenate([across_ref[:pair], across_ref[...]], axis=0)
    backward = jnp.concatenate([back_across_ref[:pair], back_across_ref[...]], axis=0)
    spots = [way_to(place_ref[0], piece) for piece in range(CHIPS)]

    def windows(rows):
        tiles = [image_ref[rows, place:place + TILE] for place in range(0, BLOCK, TILE)]
        tiles.append(tail_ref[rows, :])
        lane = lax.broadcasted_iota(jnp.int32, tiles[0].shape, 1)
        second = [pltpu.roll(tile, 80, 1) for tile in tiles[1:4]]
        third = [pltpu.roll(tile, 32, 1) for tile in tiles[2:5]]
        return (
            tiles[:2],
            [jnp.where(lane < 80, second[spot], second[spot + 1]) for spot in range(2)],
            [jnp.where(lane < 32, third[spot], third[spot + 1]) for spot in range(2)],
        )

    def halve():
        tail_ref[:PADDED, :PADDED - BLOCK] = image_ref[:, BLOCK:]
        whole = TALL - 16
        for first in range(0, whole, 32):
            rows = slice(first, first + 32)
            for window, tiles in enumerate(windows(rows)):
                for spot, tile in enumerate(tiles):
                    lanes = slice(spot * TILE, (spot + 1) * TILE)
                    high_ref[window, rows, lanes], low_ref[window, rows, lanes] = split(tile)
        for window, tiles in enumerate(windows(slice(whole, PADDED))):
            for spot, tile in enumerate(tiles):
                lanes = slice(spot * TILE, (spot + 1) * TILE)
                last = jnp.concatenate([tile, jnp.zeros((8, TILE), f32)], axis=0)
                high_ref[window, whole:, lanes], low_ref[window, whole:, lanes] = split(last)

    def transform_across(window):
        high, low = high_ref[window], low_ref[window]
        wave_ref[window] = jnp.dot(
            jnp.concatenate([high, low, high], axis=1), forward, preferred_element_type=f32
        )

    def prepare():
        same, cross = kernel_spectrum(
            filters, index_ref[0, block], table_ref, down_taps_ref, along_ref
        )
        factor_ref[0] = same.reshape(SPAN // 8, 8, pair)
        factor_ref[1] = cross.reshape(SPAN // 8, 8, pair)
        weight_ref[...] = exact_dot(cell_weights(var_ref[block], bits_ref[block]), spread)
        info = item_info(var_ref, bits_ref, owner_ref, slot_ref)
        out_ref[:, TILES_BLK] = jnp.broadcast_to(info[None], (CHIPS, INFO, TILE))

    def stack(tile):
        window, line = divmod(tile, SIDE)
        for first in range(0, SPAN, 16):
            begin, end = line * TILE + first, line * TILE + min(first + 16, SPAN)
            store_halves(stack_ref, tile, first, wave_ref[window, begin:end, :])

    def transform_down(tile):
        turn_ref[tile] = against_halves(down_ref[...], stack_ref.at[tile])

    def multiply(tile):
        for first in range(0, SPAN, 16):
            end = min(first + 16, SPAN)
            groups = slice(first // 8, end // 8)
            wave = turn_ref[tile, first:end, :].reshape((end - first) // 8, 8, pair)
            turned = pltpu.roll(wave, 4, 1)
            wave_c, wave_s = wave[..., :TILE], wave[..., TILE:]
            turned_c, turned_s = turned[..., :TILE], turned[..., TILE:]
            same_c, same_s = factor_ref[0, groups, :, :TILE], factor_ref[0, groups, :, TILE:]
            cross_c, cross_s = factor_ref[1, groups, :, :TILE], factor_ref[1, groups, :, TILE:]
            result_c = wave_c * same_c + turned_c * cross_c - wave_s * same_s - turned_s * cross_s
            result_s = wave_s * same_c + turned_s * cross_c + wave_c * same_s + turned_c * cross_s
            result = jnp.concatenate(
                [result_c.reshape(end - first, TILE), result_s.reshape(end - first, TILE)], axis=1
            )
            store_halves(result_ref, tile, first, result)

    def back_down(tile):
        column, line = divmod(tile, SIDE)
        high, low = split(against_halves(back_down_ref[...], result_ref.at[tile]))
        rows_ref[column, line * TILE:(line + 1) * TILE, :pair] = high
        rows_ref[column, line * TILE:(line + 1) * TILE, pair:] = low

    def back_across(window):
        high, low = rows_ref[window, :, :pair], rows_ref[window, :, pair:]
        matched_ref[window] = jnp.dot(
            jnp.concatenate([high, low, high], axis=1), backward, preferred_element_type=f32
        )
        if window == 1:
            finish(0)
            finish(1)
        if window == 2:
            finish(2)
            finish(3)

    def finish(column):
        lane = lax.broadcasted_iota(jnp.int32, (BLOCK, TILE), 1)

        def part(window, spot, shift):
            value = matched_ref[window, :, spot * TILE:(spot + 1) * TILE]
            return pltpu.roll(value, shift, 1) if shift else value

        if column == 0:
            matched = part(0, 0, 0)
        elif column == 1:
            matched = jnp.where(lane < 48, part(0, 1, 0), part(1, 0, 48))
        elif column == 2:
            matched = jnp.where(lane < 96, part(1, 1, 48), part(2, 0, 96))
            matched = jnp.where(lane < 48, part(1, 0, 48), matched)
        else:
            matched = jnp.where(lane < 96, part(2, 0, 96), part(2, 1, 96))
        weight = weight_ref[:, column * TILE:(column + 1) * TILE]
        weighted = matched.reshape(CELLS, CELL, TILE) * weight[:, None, :]
        weighted = weighted.reshape(SIDE, CHIPS, PIECE, TILE)
        for line in range(SIDE):
            item = line * SIDE + column
            for piece in range(CHIPS):
                out_ref[spots[piece], item] = weighted[line, piece]

    halve()
    transform_across(0)
    prepare()
    tiles = WINDOWS * SIDE
    for step in range(tiles + 5):
        if step % SIDE == 0 and step // SIDE + 1 < WINDOWS:
            transform_across(step // SIDE + 1)
        for delay, stage in enumerate((stack, transform_down, multiply, back_down)):
            if 0 <= step - delay < tiles:
                stage(step - delay)
        column, rest = divmod(step - 4, SIDE)
        if rest == SIDE - 1 and 0 <= column < WINDOWS:
            back_across(column)
    each = CHIPS // count
    sends = [
        pltpu.make_async_copy(out_ref.at[way * each:(way + 1) * each], out_hbm, out_sems.at[way])
        for way, out_hbm in enumerate(outs)
    ]
    for send in reversed(sends):
        send.start()
    for send in sends:
        send.wait()


def match_block(block, place, exposures, variance, bits, table, index, owner, slot):
    blocks = exposures.shape[1]
    items = blocks * TILES_BLK
    groups = TILES_BLK + 1
    count = 4
    matrices = transforms()
    return pl.pallas_call(
        functools.partial(match_kernel, block=block),
        out_shape=[jax.ShapeDtypeStruct((CHIPS // count, groups, PIECE, TILE), f32)] * count,
        in_specs=[pl.BlockSpec(memory_space=pltpu.SMEM)]
        + [pl.BlockSpec(memory_space=pltpu.HBM)] * (7 + len(matrices)),
        out_specs=[pl.BlockSpec(memory_space=pltpu.HBM)] * count,
        scratch_shapes=[
            pltpu.SMEM((1, blocks), jnp.int32),
            pltpu.SMEM(table.shape, f32),
            pltpu.VMEM((PADDED, PADDED), f32),
            pltpu.VMEM((blocks, CELLS, CELLS), f32),
            pltpu.VMEM((blocks, CELLS, CELLS), jnp.int32),
            pltpu.VMEM((1, items), jnp.int32),
            pltpu.VMEM((1, items), jnp.int32),
            *[pltpu.VMEM(matrix.shape, matrix.dtype) for matrix in matrices],
            pltpu.SemaphoreType.DMA((7 + len(matrices),)),
            pltpu.SemaphoreType.DMA((4,)),
            pltpu.VMEM((TALL, TILE), f32),
            pltpu.VMEM((WINDOWS, TALL, WIDTH), bf16),
            pltpu.VMEM((WINDOWS, TALL, WIDTH), bf16),
            pltpu.VMEM((WINDOWS, TALL, WIDTH), f32),
            pltpu.VMEM((WINDOWS * SIDE, 2 * SPAN + 16, WIDTH), bf16),
            pltpu.VMEM((WINDOWS * SIDE, SPAN + 8, WIDTH), f32),
            pltpu.VMEM((WINDOWS * SIDE, 2 * SPAN + 16, WIDTH), bf16),
            pltpu.VMEM((WINDOWS, BLOCK, 2 * WIDTH), bf16),
            pltpu.VMEM((WINDOWS, BLOCK, WIDTH), f32),
            pltpu.VMEM((2, SPAN // 8, 8, 2 * TILE), f32),
            pltpu.VMEM((CELLS, BLOCK), f32),
            pltpu.VMEM((CHIPS, groups, PIECE, TILE), f32),
        ],
        compiler_params=pltpu.CompilerParams(vmem_limit_bytes=59 << 20),
        cost_estimate=pl.CostEstimate(
            flops=2 * 256 * 256 * 40000, bytes_accessed=3 << 20, transcendentals=0
        ),
        name="match_block",
    )(place, index, table, exposures, variance, bits, owner, slot, *matrices)


WAYS = (0, 3, 1, 2)


def keep_kernel(part_hbm, out_ref, sem):
    copy = pltpu.make_async_copy(part_hbm, out_ref, sem)
    copy.start()
    copy.wait()


def turn_kernel(*refs):
    for first, part_ref in zip(WAYS, refs[:4]):
        for second, out_ref in enumerate(refs[4:]):
            out_ref[first] = part_ref[second]


def partial_kernel(place_ref, *refs, block):
    part_refs, before, (mine_ref, other_ref) = refs[:4], refs[4:-2], refs[-2:]
    core = place_ref[0] % 2
    per_group = TILE // TILES_BLK
    lane = lax.broadcasted_iota(jnp.int32, (INFO, TILE), 1)
    info = [
        part_refs[source // 4][source % 4, TILES_BLK * PIECE:, :] for source in range(CHIPS)
    ]
    rows = []
    for m in range(PER_TILE):
        groups = []
        for group in range(CHIPS // per_group):
            total = None
            for member in range(per_group):
                goal = member * TILES_BLK
                shift = (goal - (m * 2 + block) * TILES_BLK) % TILE
                value = info[group * per_group + member]
                value = pltpu.roll(value, shift, 1) if shift else value
                here = (lane >= goal) & (lane < goal + TILES_BLK)
                total = value if total is None else jnp.where(here, value, total)
            groups.append(total)
        rows.append(jnp.concatenate(groups, axis=1))

    targets = VISITS * OWN_DEV
    owned = targets // 2
    items = CHIPS * TILES_BLK
    row = lax.broadcasted_iota(jnp.int32, (targets, items), 0)
    side = (row // owned + core) % 2
    inner = row % owned
    wanted = ((inner // OWN_DEV) * 2 + side) * OWN_DEV + inner % OWN_DEV
    target = rows[0][PER_TILE:PER_TILE + 1, :].astype(jnp.int32)
    route = jnp.where(wanted == target, 1.0, 0.0).astype(bf16)
    weights = jnp.concatenate(rows + [jnp.zeros((TILE - INFO * PER_TILE, items), f32)], axis=0)

    def store(spot, total):
        for number, goal_ref in enumerate((mine_ref, other_ref)):
            value = total[number * owned:(number + 1) * owned]
            goal_ref[spot, :] = value + before[number][spot, :] if before else value

    sums = 0.0
    for half in split(weights):
        sums = sums + lax.dot_general(
            route, half, (((1,), (1,)), ((), ())), preferred_element_type=f32
        )
    store(pl.ds(owned * PIECE, owned), sums)
    for line in range(PIECE):
        part = jnp.concatenate(
            [
                part_ref[:, pl.ds(line, TILES_BLK, PIECE), :].reshape(items // 4, TILE)
                for part_ref in part_refs
            ],
            axis=0,
        )
        high, low = split(part)
        total = jnp.dot(route, jnp.concatenate([high, low], axis=1), preferred_element_type=f32)
        store(pl.ds(line, owned, PIECE), total[:, :TILE] + total[:, TILE:])


def spread_cells(sums, cell_row):
    pattern = (
        lax.broadcasted_iota(jnp.int32, (TILE, TILE), 1) // CELL + cell_row * INFO
        == lax.broadcasted_iota(jnp.int32, (TILE, TILE), 0)
    ).astype(f32)
    return jnp.dot(sums, pattern, precision=lax.Precision.HIGHEST, preferred_element_type=f32)


def merge_kernel(place_ref, mine_ref, other_ref, out_ref):
    owned = VISITS * OWN_DEV // 2
    cell_row = (place_ref[0] // 2) // (CELL // PIECE)
    sums = mine_ref[owned * PIECE:, :] + other_ref[owned * PIECE:, :]
    scale = 1.0 / (spread_cells(sums, cell_row) + prior_weight)
    total = mine_ref[:owned * PIECE, :] + other_ref[:owned * PIECE, :]
    total = total.reshape(owned, PIECE, TILE) * scale[:, None, :]
    out_ref[...] = total.reshape(owned * PIECE, TILE)


def chi_kernel(place_ref, mine_ref, other_ref, part_ref, upper_ref, lower_ref):
    owned = VISITS * OWN_DEV // 2
    first = owned * PIECE + (place_ref[0] // 2) * OWN_DEV
    rows = pl.ds(pl.multiple_of(first, OWN_DEV), OWN_DEV)
    sums = mine_ref[rows, :] + other_ref[rows, :]
    per_cell = CELL // PIECE
    for m in range(PER_TILE):
        weight = spread_cells(sums, m) + prior_weight
        weight = jnp.broadcast_to(weight[:, None, :], (OWN_DEV, PIECE, TILE))
        part = part_ref[m * per_cell:(m + 1) * per_cell]
        chi_ref = upper_ref if m < PER_TILE // 2 else lower_ref
        place = m % (PER_TILE // 2) * per_cell
        chi_ref[place:place + per_cell] = part * part * weight.reshape(1, OWN_DEV * PIECE, TILE)


def image_kernel(part_ref, image_ref):
    for slot in range(OWN_DEV):
        rows = slice(slot * PIECE, (slot + 1) * PIECE)
        image_ref[slot] = part_ref[:, rows, :].reshape(TILE, TILE)


def detection_kernel(upper_ref, more_upper_ref, lower_ref, more_lower_ref, out_ref):
    for slot in range(OWN_DEV):
        rows = slice(slot * PIECE, (slot + 1) * PIECE)
        upper = upper_ref[:, rows, :] + more_upper_ref[:, rows, :]
        lower = lower_ref[:, rows, :] + more_lower_ref[:, rows, :]
        out_ref[slot, :TILE // 2] = upper.reshape(TILE // 2, TILE)
        out_ref[slot, TILE // 2:] = lower.reshape(TILE // 2, TILE)


def local(exposures, variance, mask_planes, kernel_table, kernel_index, tile_owner, tile_slot):
    place = lax.axis_index("visit").astype(jnp.int32).reshape(1)
    smem = pl.BlockSpec(memory_space=pltpu.SMEM)
    vmem = pl.BlockSpec(memory_space=pltpu.VMEM)
    params = pltpu.CompilerParams(vmem_limit_bytes=32 << 20)
    owned = VISITS * OWN_DEV // 2

    def exchange(parts):
        for phase in range(2):
            parts = [
                lax.ppermute(parts[way], "visit", phase_partners(phase, way)) if way else parts[0]
                for way in WAYS
            ]
            if phase == 0:
                parts = pl.pallas_call(
                    turn_kernel,
                    out_shape=[jax.ShapeDtypeStruct(parts[0].shape, f32)] * 4,
                    in_specs=[vmem] * 4,
                    out_specs=[vmem] * 4,
                    compiler_params=params,
                    name="turn",
                )(*parts)
        return parts

    table = kernel_table.T
    owner = tile_owner.reshape(tile_slot.shape)
    def spread_tiles(pieces):
        return lax.all_to_all(pieces, "visit", 0, 0, axis_index_groups=same_core, tiled=True)

    same_core = [list(range(core, VISITS, 2)) for core in range(2)]
    operands = (place, exposures, variance, mask_planes, table, kernel_index, owner, tile_slot)
    partial = ()
    for block in range(exposures.shape[1]):
        pieces = match_block(block, *operands)
        own = pl.pallas_call(
            keep_kernel,
            out_shape=jax.ShapeDtypeStruct(pieces[0].shape, f32),
            in_specs=[pl.BlockSpec(memory_space=pltpu.HBM)],
            out_specs=vmem,
            scratch_shapes=[pltpu.SemaphoreType.DMA],
            compiler_params=params,
            name="keep",
        )(pieces[0])
        parts = [part.reshape(4, -1, TILE) for part in exchange([own, *pieces[1:]])]
        partial = pl.pallas_call(
            functools.partial(partial_kernel, block=block),
            out_shape=[jax.ShapeDtypeStruct((owned * (PIECE + 1), TILE), f32)] * 2,
            in_specs=[smem] + [vmem] * (4 + len(partial)),
            out_specs=[vmem, vmem],
            compiler_params=params,
            name="partial_sums",
        )(place, *parts, *partial)
    mine, other = partial
    other = lax.ppermute(other, "visit", [(device, device ^ 1) for device in range(VISITS)])
    pieces = pl.pallas_call(
        merge_kernel,
        out_shape=jax.ShapeDtypeStruct((owned * PIECE, TILE), f32),
        in_specs=[smem, vmem, vmem],
        out_specs=vmem,
        compiler_params=params,
        name="merge_cores",
    )(place, mine, other)
    pieces = spread_tiles(pieces.reshape(CHIPS, OWN_DEV * PIECE, TILE))
    halves = pl.pallas_call(
        chi_kernel,
        out_shape=[jax.ShapeDtypeStruct((CHIPS // 2, OWN_DEV * PIECE, TILE), f32)] * 2,
        in_specs=[smem, vmem, vmem, vmem],
        out_specs=[vmem, vmem],
        compiler_params=params,
        name="chi",
    )(place, mine, other, pieces)
    tiles = jax.ShapeDtypeStruct((OWN_DEV, TILE, TILE), f32)
    image = pl.pallas_call(
        image_kernel,
        out_shape=tiles,
        in_specs=[vmem],
        out_specs=vmem,
        compiler_params=params,
        name="image",
    )(pieces)

    pairings = ([(0, 1), (1, 0), (2, 3), (3, 2)], [(0, 3), (3, 0), (1, 2), (2, 1)])
    halves = [
        half + lax.ppermute(half, "band", pairings[number]) for number, half in enumerate(halves)
    ]
    terms = []
    for number, half in enumerate(halves):
        terms.extend((half, lax.ppermute(half, "band", pairings[1 - number])))
    detection = pl.pallas_call(
        detection_kernel,
        out_shape=tiles,
        in_specs=[vmem] * 4,
        out_specs=vmem,
        compiler_params=params,
        name="detection",
    )(*terms)
    return image[None], detection


def solution(mesh):
    placed = (
        P("band", "visit", None, None),
        P("band", "visit", None, None),
        P("band", "visit", None, None),
        P(),
        P("band", "visit"),
        P("band", "visit", None),
        P("band", "visit"),
    )
    return jax.shard_map(
        local,
        mesh=mesh,
        in_specs=placed,
        out_specs=(P("band", "visit", None, None), P("visit", None, None)),
        check_vma=False,
    )
```

```python
import functools

import jax
import jax.numpy as jnp
import numpy as np
from jax import lax
from jax.experimental import pallas as pl
from jax.experimental.pallas import tpu as pltpu
from jax.sharding import PartitionSpec as P

BLOCK = 512
TILE = 128
CELL = 32
KSIZE = 41
OWN_DEV = 8
PADDED = BLOCK + KSIZE - 1
NFILT = 11
VISITS = 32
SIDE = BLOCK // TILE
CELLS = BLOCK // CELL
PER_TILE = TILE // CELL
TILES_BLK = SIDE * SIDE
CHIPS = VISITS // 2
PIECE = TILE // CHIPS
INFO = 8
SPAN = TILE + KSIZE - 1
HALF = SPAN // 2
TALL = 560
TAPS = 48
WIDTH = 256
KEPT = 176
WINDOWS = 3

width_fractions = (0.075, 0.15, 0.3)
family_degrees = (4, 2, 2)
prior_weight = 0.05
reject_planes = 3

f32 = jnp.float32
bf16 = jnp.bfloat16


def as_halves(matrix):
    high = matrix.astype(np.float32).astype(bf16)
    low = (matrix - high.astype(np.float64)).astype(np.float32).astype(bf16)
    return high, low


def waves(length):
    angle = 2 * np.pi * (np.arange(length // 2) + 0.5) / length
    phase = angle[:, None] * np.arange(length)
    return np.cos(phase), np.sin(phase)


def transforms():
    cosine, sine = waves(WIDTH)
    by_lane = np.concatenate([cosine, sine], axis=0)
    back_across = np.zeros((WIDTH, WIDTH))
    back_across[:, :KEPT] = by_lane[:, :KEPT] * (2 / WIDTH)
    along = np.zeros((TILE, WIDTH))
    along[:KSIZE] = np.concatenate([cosine, -sine], axis=0)[:, :KSIZE].T

    cosine, sine = waves(SPAN)
    number = np.arange(HALF)
    spot = 8 * (number // 4) + number % 4
    by_row = np.zeros((SPAN, SPAN))
    by_row[spot], by_row[spot + 4] = cosine, sine
    down = np.zeros((SPAN + 8, SPAN))
    down[:SPAN] = by_row
    back_down = by_row.T[:TILE] * (2 / SPAN)

    def three(matrix, width):
        high, low = as_halves(matrix)
        rest = np.zeros((matrix.shape[0], width - 3 * matrix.shape[1]), bf16)
        return np.concatenate([high, high, low, rest], axis=1)

    same = np.zeros((SPAN + 8, TAPS))
    cross = np.zeros((SPAN + 8, TAPS))
    same[spot, :KSIZE] = same[spot + 4, :KSIZE] = cosine[:, :KSIZE]
    cross[spot, :KSIZE], cross[spot + 4, :KSIZE] = sine[:, :KSIZE], -sine[:, :KSIZE]
    def against(matrix):
        high, low = as_halves(matrix)
        zeros = np.zeros((matrix.shape[0], 8), bf16)
        return np.concatenate([high, low[:, SPAN - 8:], high, zeros, low[:, :SPAN - 8]], axis=1)

    return (
        np.concatenate(as_halves(by_lane.T), axis=0),
        against(down),
        against(back_down),
        np.concatenate(as_halves(back_across), axis=0),
        np.concatenate([three(same, 256), three(cross, 256)], axis=0),
        np.concatenate([as_halves(along)[part] for part in (0, 0, 1)], axis=0),
    )


def filter_terms():
    starts = (0, 5, 8)
    terms = []
    for family in range(3):
        for first in range(family_degrees[family] + 1):
            for second in range(family_degrees[family] + 1 - first):
                terms.append((starts[family] + first, starts[family] + second))
    return terms


def profiles_at(offset):
    half_width = (KSIZE - 1) // 2
    inside = (offset >= 0) & (offset < KSIZE)
    taps = offset.astype(f32) - half_width
    values = []
    for family in range(3):
        scaled = taps / (width_fractions[family] * half_width)
        value = jnp.where(inside, jnp.exp(-0.5 * scaled * scaled), 0.0)
        for degree in range(family_degrees[family] + 1):
            values.append(value)
            value = value * scaled
    return values


def split(value):
    high = value.astype(bf16)
    return high, (value - high.astype(f32)).astype(bf16)


def cell_weights(variance, bits):
    usable = (jnp.bitwise_and(bits, reject_planes) != reject_planes).astype(f32)
    return usable / variance


def item_info(var_ref, bits_ref, owner_ref, slot_ref):
    exact = lax.Precision.HIGHEST
    lane = lax.broadcasted_iota(jnp.int32, (1, TILE), 1)
    row = lax.broadcasted_iota(jnp.int32, (CELLS, TILE), 0)
    item = lane % TILES_BLK
    cell_row = (item // SIDE) * PER_TILE + lane // (2 * TILES_BLK)
    columns = None
    for block in range(2):
        picked = ((row == cell_row) & ((lane // TILES_BLK) % 2 == block)).astype(f32)
        term = lax.dot_general(
            cell_weights(var_ref[block], bits_ref[block]), picked,
            (((0,), (0,)), ((), ())), precision=exact, preferred_element_type=f32,
        )
        columns = term if columns is None else columns + term
    rows = []
    for n in range(PER_TILE):
        chosen = row == (item % SIDE) * PER_TILE + n
        rows.append(jnp.sum(jnp.where(chosen, columns, 0.0), axis=0, keepdims=True))
    target = (owner_ref[...] * OWN_DEV + slot_ref[...]).astype(f32)
    rows.append(jnp.concatenate([target, jnp.zeros((1, TILE - 2 * TILES_BLK), f32)], axis=1))
    rows.append(jnp.zeros((INFO - PER_TILE - 1, TILE), f32))
    return jnp.concatenate(rows, axis=0)


def phase_masks(core):
    return (1, 3) if core == 0 else (3, 1)


def way_to(place, piece):
    core, offset = place % 2, jnp.bitwise_xor(place // 2, piece)
    first, second = 0, 0
    for coordinate in (offset // 4, offset % 4):
        high = coordinate // 2
        both = jnp.bitwise_xor(high, coordinate % 2)
        first = 2 * first + jnp.where(core == 0, both, high)
        second = 2 * second + jnp.where(core == 0, high, both)
    return 4 * first + second


def phase_partners(phase, way):
    partners = []
    for device in range(VISITS):
        mask = phase_masks(device % 2)[phase]
        partners.append((device, device ^ (2 * (4 * mask * (way // 2) + mask * (way % 2)))))
    return partners


def exact_dot(left, right, sides=((1,), (0,))):
    return lax.dot_general(
        left, right, (sides, ((), ())), precision=lax.Precision.HIGHEST, preferred_element_type=f32
    )


def store_halves(halves_ref, tile, first, value):
    high = value.astype(bf16).astype(f32)
    low = value - high
    if value.shape[0] < 16:
        high = jnp.concatenate([high, high], axis=0)
        low = jnp.concatenate([low, jnp.zeros_like(low)], axis=0)
    halves_ref[tile, first:first + 16, :] = high.astype(bf16)
    halves_ref[tile, SPAN + 8 + first:SPAN + 8 + first + 16, :] = low.astype(bf16)


def against_halves(matrix, halves_ref):
    rows = jnp.concatenate([halves_ref[...], halves_ref[:SPAN - 8, :]], axis=0)
    return jnp.dot(matrix, rows, preferred_element_type=f32)


def filter_bank():
    values = profiles_at(lax.broadcasted_iota(jnp.int32, (1, TILE), 1))
    scales = [1.0 / jnp.sqrt(jnp.sum(value * value, axis=1, keepdims=True)) for value in values]
    wide = [value * scale for value, scale in zip(values, scales)]
    tall = profiles_at(lax.broadcasted_iota(jnp.int32, (TAPS, TILE), 0))
    return wide, [value * scale for value, scale in zip(tall, scales)]


def kernel_spectrum(filters, which, table_ref, down_taps_ref, along_ref):
    wide, tall = filters
    mixed = [0.0] * NFILT
    for number, (first, second) in enumerate(filter_terms()):
        mixed[first] = mixed[first] + table_ref[number, which] * wide[second]
    kernel = 0.0
    for down, across in zip(tall, mixed):
        kernel = kernel + down * across
    high, low = split(kernel)
    half_way = jnp.dot(
        jnp.concatenate([high, low, high], axis=1), along_ref[...], preferred_element_type=f32
    )
    high = half_way.astype(bf16).astype(f32)
    rest = jnp.zeros((256 - 3 * TAPS, WIDTH), f32)
    half_way = jnp.concatenate([high, half_way - high, high, rest], axis=0).astype(bf16)
    both = jnp.dot(down_taps_ref[...], half_way, preferred_element_type=f32)
    return both[:SPAN], both[SPAN + 8:2 * SPAN + 8]


def match_kernel(
    place_ref, index_hbm, table_hbm, image_hbm, var_hbm, bits_hbm, owner_hbm, slot_hbm,
    across_hbm, down_hbm, back_down_hbm, back_across_hbm, down_taps_hbm, along_hbm,
    *rest, block,
):
    count = 4
    outs = rest[:count]
    (
        index_ref, table_ref, image_ref, var_ref, bits_ref, owner_ref, slot_ref,
        across_ref, down_ref, back_down_ref, back_across_ref, down_taps_ref, along_ref, sems,
        out_sems, tail_ref, high_ref, low_ref, wave_ref, stack_ref, turn_ref, result_ref, rows_ref,
        matched_ref, factor_ref, weight_ref, out_ref,
    ) = rest[count:]
    copies = [
        pltpu.make_async_copy(source, goal, sems.at[number])
        for number, (source, goal) in enumerate((
            (image_hbm.at[0, block], image_ref),
            (across_hbm, across_ref),
            (index_hbm, index_ref),
            (table_hbm, table_ref),
            (down_taps_hbm, down_taps_ref),
            (along_hbm, along_ref),
            (var_hbm.at[0], var_ref),
            (bits_hbm.at[0], bits_ref),
            (owner_hbm, owner_ref),
            (slot_hbm, slot_ref),
            (down_hbm, down_ref),
            (back_down_hbm, back_down_ref),
            (back_across_hbm, back_across_ref),
        ))
    ]
    for copy in copies:
        copy.start()
    tail_ref[...] = jnp.zeros_like(tail_ref)
    filters = filter_bank()
    spread = (
        lax.broadcasted_iota(jnp.int32, (CELLS, BLOCK), 1) // CELL
        == lax.broadcasted_iota(jnp.int32, (CELLS, BLOCK), 0)
    ).astype(f32)
    for copy in copies[:2]:
        copy.wait()

    pair = 2 * TILE
    forward = jnp.concatenate([across_ref[:pair], across_ref[...]], axis=0)
    spots = [way_to(place_ref[0], piece) for piece in range(CHIPS)]

    def windows(rows):
        tiles = [image_ref[rows, place:place + TILE] for place in range(0, BLOCK, TILE)]
        tiles.append(tail_ref[rows, :])
        lane = lax.broadcasted_iota(jnp.int32, tiles[0].shape, 1)
        second = [pltpu.roll(tile, 80, 1) for tile in tiles[1:4]]
        third = [pltpu.roll(tile, 32, 1) for tile in tiles[2:5]]
        return (
            tiles[:2],
            [jnp.where(lane < 80, second[spot], second[spot + 1]) for spot in range(2)],
            [jnp.where(lane < 32, third[spot], third[spot + 1]) for spot in range(2)],
        )

    def halve():
        tail_ref[:PADDED, :PADDED - BLOCK] = image_ref[:, BLOCK:]
        whole = TALL - 16
        for first in range(0, whole, 32):
            rows = slice(first, first + 32)
            for window, tiles in enumerate(windows(rows)):
                for spot, tile in enumerate(tiles):
                    lanes = slice(spot * TILE, (spot + 1) * TILE)
                    high_ref[window, rows, lanes], low_ref[window, rows, lanes] = split(tile)
        for window, tiles in enumerate(windows(slice(whole, PADDED))):
            for spot, tile in enumerate(tiles):
                lanes = slice(spot * TILE, (spot + 1) * TILE)
                last = jnp.concatenate([tile, jnp.zeros((8, TILE), f32)], axis=0)
                high_ref[window, whole:, lanes], low_ref[window, whole:, lanes] = split(last)

    def transform_across(window):
        high, low = high_ref[window], low_ref[window]
        wave_ref[window] = jnp.dot(
            jnp.concatenate([high, low, high], axis=1), forward, preferred_element_type=f32
        )

    def prepare():
        same, cross = kernel_spectrum(
            filters, index_ref[0, block], table_ref, down_taps_ref, along_ref
        )
        factor_ref[0] = same.reshape(SPAN // 8, 8, pair)
        factor_ref[1] = cross.reshape(SPAN // 8, 8, pair)
        weight_ref[...] = exact_dot(cell_weights(var_ref[block], bits_ref[block]), spread)
        info = item_info(var_ref, bits_ref, owner_ref, slot_ref)
        out_ref[:, TILES_BLK] = jnp.broadcast_to(info[None], (CHIPS, INFO, TILE))

    def stack(tile):
        window, line = divmod(tile, SIDE)
        for first in range(0, SPAN, 16):
            begin, end = line * TILE + first, line * TILE + min(first + 16, SPAN)
            store_halves(stack_ref, tile, first, wave_ref[window, begin:end, :])

    def transform_down(tile):
        turn_ref[tile] = against_halves(down_ref[...], stack_ref.at[tile])

    def multiply(tile):
        for first in range(0, SPAN, 16):
            end = min(first + 16, SPAN)
            groups = slice(first // 8, end // 8)
            wave = turn_ref[tile, first:end, :].reshape((end - first) // 8, 8, pair)
            turned = pltpu.roll(wave, 4, 1)
            wave_c, wave_s = wave[..., :TILE], wave[..., TILE:]
            turned_c, turned_s = turned[..., :TILE], turned[..., TILE:]
            same_c, same_s = factor_ref[0, groups, :, :TILE], factor_ref[0, groups, :, TILE:]
            cross_c, cross_s = factor_ref[1, groups, :, :TILE], factor_ref[1, groups, :, TILE:]
            result_c = wave_c * same_c + turned_c * cross_c - wave_s * same_s - turned_s * cross_s
            result_s = wave_s * same_c + turned_s * cross_c + wave_c * same_s + turned_c * cross_s
            result = jnp.concatenate(
                [result_c.reshape(end - first, TILE), result_s.reshape(end - first, TILE)], axis=1
            )
            store_halves(result_ref, tile, first, result)

    def back_down(tile):
        column, line = divmod(tile, SIDE)
        high, low = split(against_halves(back_down_ref[...], result_ref.at[tile]))
        rows_ref[column, line * TILE:(line + 1) * TILE, :pair] = high
        rows_ref[column, line * TILE:(line + 1) * TILE, pair:] = low

    def back_across(window):
        high, low = rows_ref[window, :, :pair], rows_ref[window, :, pair:]
        matched_ref[window] = jnp.dot(
            jnp.concatenate([high, low, high], axis=1), backward, preferred_element_type=f32
        )
        if window == 1:
            finish(0)
            finish(1)
        if window == 2:
            finish(2)
            finish(3)

    def finish(column):
        lane = lax.broadcasted_iota(jnp.int32, (BLOCK, TILE), 1)

        def part(window, spot, shift):
            value = matched_ref[window, :, spot * TILE:(spot + 1) * TILE]
            return pltpu.roll(value, shift, 1) if shift else value

        if column == 0:
            matched = part(0, 0, 0)
        elif column == 1:
            matched = jnp.where(lane < 48, part(0, 1, 0), part(1, 0, 48))
        elif column == 2:
            matched = jnp.where(lane < 96, part(1, 1, 48), part(2, 0, 96))
            matched = jnp.where(lane < 48, part(1, 0, 48), matched)
        else:
            matched = jnp.where(lane < 96, part(2, 0, 96), part(2, 1, 96))
        weight = weight_ref[:, column * TILE:(column + 1) * TILE]
        weighted = matched.reshape(CELLS, CELL, TILE) * weight[:, None, :]
        weighted = weighted.reshape(SIDE, CHIPS, PIECE, TILE)
        for line in range(SIDE):
            item = line * SIDE + column
            for piece in range(CHIPS):
                out_ref[spots[piece], item] = weighted[line, piece]

    halve()
    transform_across(0)
    for copy in copies[2:]:
        copy.wait()
    backward = jnp.concatenate([back_across_ref[:pair], back_across_ref[...]], axis=0)
    prepare()
    tiles = WINDOWS * SIDE
    for step in range(tiles + 5):
        if step % SIDE == 0 and step // SIDE + 1 < WINDOWS:
            transform_across(step // SIDE + 1)
        for delay, stage in enumerate((stack, transform_down, multiply, back_down)):
            if 0 <= step - delay < tiles:
                stage(step - delay)
        column, rest = divmod(step - 4, SIDE)
        if rest == SIDE - 1 and 0 <= column < WINDOWS:
            back_across(column)
    each = CHIPS // count
    sends = [
        pltpu.make_async_copy(out_ref.at[way * each:(way + 1) * each], out_hbm, out_sems.at[way])
        for way, out_hbm in enumerate(outs)
    ]
    for send in reversed(sends):
        send.start()
    for send in sends:
        send.wait()


def match_block(block, place, exposures, variance, bits, table, index, owner, slot):
    blocks = exposures.shape[1]
    items = blocks * TILES_BLK
    groups = TILES_BLK + 1
    count = 4
    matrices = transforms()
    return pl.pallas_call(
        functools.partial(match_kernel, block=block),
        out_shape=[jax.ShapeDtypeStruct((CHIPS // count, groups, PIECE, TILE), f32)] * count,
        in_specs=[pl.BlockSpec(memory_space=pltpu.SMEM)]
        + [pl.BlockSpec(memory_space=pltpu.HBM)] * (7 + len(matrices)),
        out_specs=[pl.BlockSpec(memory_space=pltpu.HBM)] * count,
        scratch_shapes=[
            pltpu.SMEM((1, blocks), jnp.int32),
            pltpu.SMEM(table.shape, f32),
            pltpu.VMEM((PADDED, PADDED), f32),
            pltpu.VMEM((blocks, CELLS, CELLS), f32),
            pltpu.VMEM((blocks, CELLS, CELLS), jnp.int32),
            pltpu.VMEM((1, items), jnp.int32),
            pltpu.VMEM((1, items), jnp.int32),
            *[pltpu.VMEM(matrix.shape, matrix.dtype) for matrix in matrices],
            pltpu.SemaphoreType.DMA((7 + len(matrices),)),
            pltpu.SemaphoreType.DMA((4,)),
            pltpu.VMEM((TALL, TILE), f32),
            pltpu.VMEM((WINDOWS, TALL, WIDTH), bf16),
            pltpu.VMEM((WINDOWS, TALL, WIDTH), bf16),
            pltpu.VMEM((WINDOWS, TALL, WIDTH), f32),
            pltpu.VMEM((WINDOWS * SIDE, 2 * SPAN + 16, WIDTH), bf16),
            pltpu.VMEM((WINDOWS * SIDE, SPAN + 8, WIDTH), f32),
            pltpu.VMEM((WINDOWS * SIDE, 2 * SPAN + 16, WIDTH), bf16),
            pltpu.VMEM((WINDOWS, BLOCK, 2 * WIDTH), bf16),
            pltpu.VMEM((WINDOWS, BLOCK, WIDTH), f32),
            pltpu.VMEM((2, SPAN // 8, 8, 2 * TILE), f32),
            pltpu.VMEM((CELLS, BLOCK), f32),
            pltpu.VMEM((CHIPS, groups, PIECE, TILE), f32),
        ],
        compiler_params=pltpu.CompilerParams(vmem_limit_bytes=59 << 20),
        cost_estimate=pl.CostEstimate(
            flops=2 * 256 * 256 * 40000, bytes_accessed=3 << 20, transcendentals=0
        ),
        name="match_block",
    )(place, index, table, exposures, variance, bits, owner, slot, *matrices)


WAYS = (0, 3, 1, 2)


def keep_kernel(part_hbm, out_ref, sem):
    copy = pltpu.make_async_copy(part_hbm, out_ref, sem)
    copy.start()
    copy.wait()


def turn_kernel(*refs):
    for first, part_ref in zip(WAYS, refs[:4]):
        for second, out_ref in enumerate(refs[4:]):
            out_ref[first] = part_ref[second]


def partial_kernel(place_ref, *refs, block):
    part_refs, before, (mine_ref, other_ref) = refs[:4], refs[4:-2], refs[-2:]
    core = place_ref[0] % 2
    per_group = TILE // TILES_BLK
    lane = lax.broadcasted_iota(jnp.int32, (INFO, TILE), 1)
    info = [
        part_refs[source // 4][source % 4, TILES_BLK * PIECE:, :] for source in range(CHIPS)
    ]
    rows = []
    for m in range(PER_TILE):
        groups = []
        for group in range(CHIPS // per_group):
            total = None
            for member in range(per_group):
                goal = member * TILES_BLK
                shift = (goal - (m * 2 + block) * TILES_BLK) % TILE
                value = info[group * per_group + member]
                value = pltpu.roll(value, shift, 1) if shift else value
                here = (lane >= goal) & (lane < goal + TILES_BLK)
                total = value if total is None else jnp.where(here, value, total)
            groups.append(total)
        rows.append(jnp.concatenate(groups, axis=1))

    targets = VISITS * OWN_DEV
    owned = targets // 2
    items = CHIPS * TILES_BLK
    row = lax.broadcasted_iota(jnp.int32, (targets, items), 0)
    side = (row // owned + core) % 2
    inner = row % owned
    wanted = ((inner // OWN_DEV) * 2 + side) * OWN_DEV + inner % OWN_DEV
    target = rows[0][PER_TILE:PER_TILE + 1, :].astype(jnp.int32)
    route = jnp.where(wanted == target, 1.0, 0.0).astype(bf16)
    weights = jnp.concatenate(rows + [jnp.zeros((TILE - INFO * PER_TILE, items), f32)], axis=0)

    def store(spot, total):
        for number, goal_ref in enumerate((mine_ref, other_ref)):
            value = total[number * owned:(number + 1) * owned]
            goal_ref[spot, :] = value + before[number][spot, :] if before else value

    sums = 0.0
    for half in split(weights):
        sums = sums + lax.dot_general(
            route, half, (((1,), (1,)), ((), ())), preferred_element_type=f32
        )
    store(pl.ds(owned * PIECE, owned), sums)
    for line in range(PIECE):
        part = jnp.concatenate(
            [
                part_ref[:, pl.ds(line, TILES_BLK, PIECE), :].reshape(items // 4, TILE)
                for part_ref in part_refs
            ],
            axis=0,
        )
        high, low = split(part)
        total = jnp.dot(route, jnp.concatenate([high, low], axis=1), preferred_element_type=f32)
        store(pl.ds(line, owned, PIECE), total[:, :TILE] + total[:, TILE:])


def spread_cells(sums, cell_row):
    pattern = (
        lax.broadcasted_iota(jnp.int32, (TILE, TILE), 1) // CELL + cell_row * INFO
        == lax.broadcasted_iota(jnp.int32, (TILE, TILE), 0)
    ).astype(f32)
    return jnp.dot(sums, pattern, precision=lax.Precision.HIGHEST, preferred_element_type=f32)


def merge_kernel(place_ref, mine_ref, other_ref, out_ref):
    owned = VISITS * OWN_DEV // 2
    cell_row = (place_ref[0] // 2) // (CELL // PIECE)
    sums = mine_ref[owned * PIECE:, :] + other_ref[owned * PIECE:, :]
    scale = 1.0 / (spread_cells(sums, cell_row) + prior_weight)
    total = mine_ref[:owned * PIECE, :] + other_ref[:owned * PIECE, :]
    total = total.reshape(owned, PIECE, TILE) * scale[:, None, :]
    out_ref[...] = total.reshape(owned * PIECE, TILE)


def chi_kernel(place_ref, mine_ref, other_ref, part_ref, upper_ref, lower_ref):
    owned = VISITS * OWN_DEV // 2
    first = owned * PIECE + (place_ref[0] // 2) * OWN_DEV
    rows = pl.ds(pl.multiple_of(first, OWN_DEV), OWN_DEV)
    sums = mine_ref[rows, :] + other_ref[rows, :]
    per_cell = CELL // PIECE
    for m in range(PER_TILE):
        weight = spread_cells(sums, m) + prior_weight
        weight = jnp.broadcast_to(weight[:, None, :], (OWN_DEV, PIECE, TILE))
        part = part_ref[m * per_cell:(m + 1) * per_cell]
        chi_ref = upper_ref if m < PER_TILE // 2 else lower_ref
        place = m % (PER_TILE // 2) * per_cell
        chi_ref[place:place + per_cell] = part * part * weight.reshape(1, OWN_DEV * PIECE, TILE)


def image_kernel(part_ref, image_ref):
    for slot in range(OWN_DEV):
        rows = slice(slot * PIECE, (slot + 1) * PIECE)
        image_ref[slot] = part_ref[:, rows, :].reshape(TILE, TILE)


def detection_kernel(upper_ref, more_upper_ref, lower_ref, more_lower_ref, out_ref):
    for slot in range(OWN_DEV):
        rows = slice(slot * PIECE, (slot + 1) * PIECE)
        upper = upper_ref[:, rows, :] + more_upper_ref[:, rows, :]
        lower = lower_ref[:, rows, :] + more_lower_ref[:, rows, :]
        out_ref[slot, :TILE // 2] = upper.reshape(TILE // 2, TILE)
        out_ref[slot, TILE // 2:] = lower.reshape(TILE // 2, TILE)


def local(exposures, variance, mask_planes, kernel_table, kernel_index, tile_owner, tile_slot):
    place = lax.axis_index("visit").astype(jnp.int32).reshape(1)
    smem = pl.BlockSpec(memory_space=pltpu.SMEM)
    vmem = pl.BlockSpec(memory_space=pltpu.VMEM)
    params = pltpu.CompilerParams(vmem_limit_bytes=32 << 20)
    owned = VISITS * OWN_DEV // 2

    def exchange(parts):
        for phase in range(2):
            parts = [
                lax.ppermute(parts[way], "visit", phase_partners(phase, way)) if way else parts[0]
                for way in WAYS
            ]
            if phase == 0:
                parts = pl.pallas_call(
                    turn_kernel,
                    out_shape=[jax.ShapeDtypeStruct(parts[0].shape, f32)] * 4,
                    in_specs=[vmem] * 4,
                    out_specs=[vmem] * 4,
                    compiler_params=params,
                    name="turn",
                )(*parts)
        return parts

    table = kernel_table.T
    owner = tile_owner.reshape(tile_slot.shape)
    def spread_tiles(pieces):
        return lax.all_to_all(pieces, "visit", 0, 0, axis_index_groups=same_core, tiled=True)

    same_core = [list(range(core, VISITS, 2)) for core in range(2)]
    operands = (place, exposures, variance, mask_planes, table, kernel_index, owner, tile_slot)
    partial = ()
    for block in range(exposures.shape[1]):
        pieces = match_block(block, *operands)
        own = pl.pallas_call(
            keep_kernel,
            out_shape=jax.ShapeDtypeStruct(pieces[0].shape, f32),
            in_specs=[pl.BlockSpec(memory_space=pltpu.HBM)],
            out_specs=vmem,
            scratch_shapes=[pltpu.SemaphoreType.DMA],
            compiler_params=params,
            name="keep",
        )(pieces[0])
        parts = [part.reshape(4, -1, TILE) for part in exchange([own, *pieces[1:]])]
        partial = pl.pallas_call(
            functools.partial(partial_kernel, block=block),
            out_shape=[jax.ShapeDtypeStruct((owned * (PIECE + 1), TILE), f32)] * 2,
            in_specs=[smem] + [vmem] * (4 + len(partial)),
            out_specs=[vmem, vmem],
            compiler_params=params,
            name="partial_sums",
        )(place, *parts, *partial)
    mine, other = partial
    other = lax.ppermute(other, "visit", [(device, device ^ 1) for device in range(VISITS)])
    pieces = pl.pallas_call(
        merge_kernel,
        out_shape=jax.ShapeDtypeStruct((owned * PIECE, TILE), f32),
        in_specs=[smem, vmem, vmem],
        out_specs=vmem,
        compiler_params=params,
        name="merge_cores",
    )(place, mine, other)
    pieces = spread_tiles(pieces.reshape(CHIPS, OWN_DEV * PIECE, TILE))
    halves = pl.pallas_call(
        chi_kernel,
        out_shape=[jax.ShapeDtypeStruct((CHIPS // 2, OWN_DEV * PIECE, TILE), f32)] * 2,
        in_specs=[smem, vmem, vmem, vmem],
        out_specs=[vmem, vmem],
        compiler_params=params,
        name="chi",
    )(place, mine, other, pieces)
    tiles = jax.ShapeDtypeStruct((OWN_DEV, TILE, TILE), f32)
    image = pl.pallas_call(
        image_kernel,
        out_shape=tiles,
        in_specs=[vmem],
        out_specs=vmem,
        compiler_params=params,
        name="image",
    )(pieces)

    pairings = ([(0, 1), (1, 0), (2, 3), (3, 2)], [(0, 3), (3, 0), (1, 2), (2, 1)])
    halves = [
        half + lax.ppermute(half, "band", pairings[number]) for number, half in enumerate(halves)
    ]
    terms = []
    for number, half in enumerate(halves):
        terms.extend((half, lax.ppermute(half, "band", pairings[1 - number])))
    detection = pl.pallas_call(
        detection_kernel,
        out_shape=tiles,
        in_specs=[vmem] * 4,
        out_specs=vmem,
        compiler_params=params,
        name="detection",
    )(*terms)
    return image[None], detection


def solution(mesh):
    placed = (
        P("band", "visit", None, None),
        P("band", "visit", None, None),
        P("band", "visit", None, None),
        P(),
        P("band", "visit"),
        P("band", "visit", None),
        P("band", "visit"),
    )
    return jax.shard_map(
        local,
        mesh=mesh,
        in_specs=placed,
        out_specs=(P("band", "visit", None, None), P("visit", None, None)),
        check_vma=False,
    )
```
